32 devices in a mesh: seq: 8 (over z, core), clip: 4 (over y, x).
Axes of the slice: x: 2, y: 2, z: 4, core: 2. Of those that a mesh axis runs over, the one named last changes fastest.
Arguments:
- tokens: bfloat16 [8, 8, 256, 1024], P('clip', 'seq'), may hold values from -6 to 6
- cotangent: bfloat16 [8, 8, 256, 1024], P('clip', 'seq'), may hold values from -6 to 6
- context_count: int32 [8], P('clip'), may hold values from 1 to 7
- noise_level: int32 [8, 8], P('clip', 'seq'), may hold values from 0 to 1023
- frame_time: int32 [8, 8], P('clip', 'seq'), may hold values from 0 to 21, as said below
- level_table: bfloat16 [1024, 1024], replicated, may hold values from -6 to 6
- mod_weight: bfloat16 [1024, 6144], replicated, may hold values from -0.1875 to 0.1875
- mod_bias: bfloat16 [6144], replicated, may hold values from -3 to 3
- qkv_weight: bfloat16 [1024, 3072], replicated, may hold values from -0.1875 to 0.1875
- qkv_bias: bfloat16 [3072], replicated, may hold values from -3 to 3
- proj_weight: bfloat16 [1024, 1024], replicated, may hold values from -3 to 3
- proj_bias: bfloat16 [1024], replicated, may hold values from -3 to 3
- up_weight: bfloat16 [1024, 4096], replicated, may hold values from -0.1875 to 0.1875
- up_bias: bfloat16 [4096], replicated, may hold values from -3 to 3
- down_weight: bfloat16 [4096, 1024], replicated, may hold values from -0.09375 to 0.09375
- down_bias: bfloat16 [1024], replicated, may hold values from -3 to 3
Outputs:
- layer_out: bfloat16 [8, 8, 256, 1024], P('clip', 'seq')
- tokens_grad: float32 [8, 8, 256, 1024], P('clip', 'seq')
- table_grad: float32 [1024, 1024], P('seq')
- mod_wgrad: float32 [1024, 6144], P('seq')
- mod_bgrad: float32 [6144], P('seq')
- qkv_wgrad: float32 [1024, 3072], P('seq')
- qkv_bgrad: float32 [3072], P('seq')
- proj_wgrad: float32 [1024, 1024], P('seq')
- proj_bgrad: float32 [1024], P('seq')
- up_wgrad: float32 [1024, 4096], P('seq')
- up_bgrad: float32 [4096], P('seq')
- down_wgrad: float32 [4096, 1024], P('seq')
- down_bgrad: float32 [1024], P('seq')
The draws below stay inside these ranges and needn't reach their ends.
Inputs may be any that keep to these rules, and one draw needn't show every extreme that they name: `frame_time`: within each clip the time stamps start at 0 and rise by 1 to 3 from one frame to the next; in every draw one clip rises by 3 at every frame.
All inputs are finite; a program needn't handle non-finite values.
Results may differ from the reference program's by a relative error of at most 0.017.
Values may be sent and summed in bfloat16 or wider, within the bound.
No kernel may reach another device: no remote copies, remote signals or barrier semaphores. Data moves between devices by JAX's collectives and lax.ppermute only.
A program may use at most 320 MiB of HBM per device.

```python
import jax
import jax.numpy as jnp
from jax import lax

D = 1024
HEADS = 16
FF = 4096
LEVELS = 1024
PATCH = 256
CLIPS = 8
FRAMES = 8


def draw_frame_time(key, part):
    key = jax.random.fold_in(key, 7)
    stride_key, pick_key = jax.random.split(key)
    strides = jax.random.randint(stride_key, (CLIPS, FRAMES), 1, 4).astype(jnp.int32)
    chosen = jax.random.randint(pick_key, (), 0, CLIPS).astype(jnp.int32)
    coarse = (jnp.arange(CLIPS).astype(jnp.int32) == chosen)[:, None]
    strides = jnp.where(coarse, 3, strides).astype(jnp.int32)
    return (jnp.cumsum(strides, axis=1) - strides[:, :1]).astype(jnp.int32)


def set_ends(array, key, low, high):
    place = [jax.random.randint(jax.random.fold_in(key, axis), (), 0, length) for axis, length in enumerate(array.shape)]
    widest = array.shape.index(max(array.shape))
    neighbour = place[:widest] + [(place[widest] + 1) % array.shape[widest]] + place[widest + 1:]
    return array.at[tuple(place)].set(low).at[tuple(neighbour)].set(high)


def steps_of(stream_key, dims, pieces, low, top_value):
    def one(axis_at, parts):
        heights = jax.random.uniform(jax.random.fold_in(jax.random.fold_in(stream_key, 6), axis_at), (parts,), jnp.float32, low / len(pieces), top_value / len(pieces))
        return jnp.repeat(jnp.exp(heights), dims[axis_at] // parts).reshape((-1,) + (1,) * (len(dims) - axis_at - 1))

    factor_of = one(*pieces[0])
    for cut in pieces[1:]:
        factor_of = factor_of * one(*cut)
    return factor_of


def centred(stream_key, shape, width, bound, cuts=(), held_as=jnp.bfloat16):
    array = width * jax.random.normal(stream_key, shape, jnp.float32)
    if cuts:
        array = array * steps_of(stream_key, shape, cuts, -0.22, 0.18)
    return jnp.clip(array, -bound, bound).astype(held_as)


def setup_inputs(seed: int = 0) -> dict:
    seeds = jax.random.split(jax.random.key(seed), 17)
    return {
        "tokens": centred(seeds[0], (CLIPS, FRAMES, PATCH, D), 1.0, 6.0, ((0, 4), (1, 8))),
        "cotangent": centred(seeds[1], (CLIPS, FRAMES, PATCH, D), 1.0, 6.0, ((0, 4), (1, 8))),
        "context_count": set_ends(jax.random.randint(seeds[2], (CLIPS,), 1, FRAMES), jax.random.fold_in(seeds[2], 1), 1, FRAMES - 1).astype(jnp.int32),
        "noise_level": set_ends(jax.random.randint(seeds[3], (CLIPS, FRAMES), 0, LEVELS), jax.random.fold_in(seeds[3], 1), 0, LEVELS - 1).astype(jnp.int32),
        "frame_time": draw_frame_time(jax.random.fold_in(seeds[16], 71), 0),
        "level_table": centred(seeds[5], (LEVELS, D), 1.0, 6.0),
        "mod_weight": centred(seeds[6], (D, 6 * D), D ** -0.5, 0.1875),
        "mod_bias": centred(seeds[7], (6 * D,), 0.3, 3.0),
        "qkv_weight": centred(seeds[8], (D, 3 * D), D ** -0.5, 0.1875),
        "qkv_bias": centred(seeds[9], (3 * D,), 0.3, 3.0),
        "proj_weight": centred(seeds[10], (D, D), (max(D // 256, 1)) ** -0.5, 3.0),
        "proj_bias": centred(seeds[11], (D,), 0.3, 3.0),
        "up_weight": centred(seeds[12], (D, FF), D ** -0.5, 0.1875),
        "up_bias": centred(seeds[13], (FF,), 0.3, 3.0),
        "down_weight": centred(seeds[14], (FF, D), FF ** -0.5, 0.09375),
        "down_bias": centred(seeds[15], (D,), 0.3, 3.0),
    }


@jax.custom_vjp
def low(v):
    return lax.optimization_barrier(v.astype(jnp.bfloat16)).astype(jnp.float32)

@jax.custom_vjp
def low_back(v):
    return v

def low_keep(v):
    return (low(v), None)

def low_pass(kept, grad):
    return (grad,)

def back_keep(v):
    return (v, None)

def back_low(kept, grad):
    return (low(grad),)
low.defvjp(low_keep, low_pass)
low_back.defvjp(back_keep, back_low)
EPS = 1e-06
HIGHEST_PRECISION = lax.Precision.HIGHEST
MASKED = -1e+30

def silu_act(values_in):
    return values_in * jax.nn.sigmoid(values_in)

def gelu_act(values_in):
    return 0.5 * values_in * (1.0 + jnp.tanh(0.7978845608028654 * (values_in + 0.044715 * values_in * values_in * values_in)))

def modulate(values_in, shift_part, scale_part):
    center = lax.optimization_barrier(jnp.mean(values_in, axis=-1, keepdims=True))
    offset = values_in - center
    spread = lax.optimization_barrier(jnp.mean(offset * offset, axis=-1, keepdims=True))
    return offset * lax.rsqrt(spread + EPS) * (1.0 + scale_part) + shift_part

def rotary_tables(stamps, patch_count, head_size):
    quarter = head_size // 4
    freqs = 10000.0 ** (-jnp.arange(quarter).astype(jnp.float32) / quarter)
    temporal = stamps.astype(jnp.float32)[:, None, None] * freqs[None, None, :]
    spatial = jnp.arange(patch_count).astype(jnp.float32)[None, :, None] * freqs[None, None, :]
    shape_full = (stamps.shape[0], patch_count, quarter)
    angles = jnp.concatenate([jnp.broadcast_to(temporal, shape_full), jnp.broadcast_to(spatial, shape_full)], axis=-1)
    cosine = jnp.cos(angles)
    sine = jnp.sin(angles)
    return (jnp.concatenate([cosine, cosine], axis=-1), jnp.concatenate([sine, sine], axis=-1))

def rotate(tensor, cosine, sine):
    half_size = tensor.shape[-1] // 2
    turned = jnp.concatenate([-tensor[..., half_size:], tensor[..., :half_size]], axis=-1)
    return tensor * cosine[..., None, :] + turned * sine[..., None, :]

def clip_forward(inputs, params, context, levels_in, frame_times):
    level_table, mod_weight, mod_bias, qkv_weight, qkv_bias, proj_weight, proj_bias, up_weight, up_bias, down_weight, down_bias = params
    frame_total, patch_count, model_width = inputs.shape
    head_size = model_width // HEADS
    score_scale = head_size ** (-0.5)
    frame_ids = jnp.arange(frame_total).astype(jnp.int32)
    levels_used = jnp.where(frame_ids < context, 0, levels_in).astype(jnp.int32)
    condition = jnp.take(level_table, levels_used, axis=0)
    modulation = low_back(jnp.dot(low(silu_act(condition)), mod_weight, precision=HIGHEST_PRECISION) + mod_bias)
    shift_one, scale_one, gate_one, shift_two, scale_two, gate_two = jnp.split(modulation[:, None, :], 6, axis=-1)
    normed = low(modulate(inputs, shift_one, scale_one)).reshape(-1, model_width)
    projected = low_back(jnp.dot(normed, qkv_weight, precision=HIGHEST_PRECISION) + qkv_bias)
    projected = projected.reshape(frame_total, patch_count, 3, HEADS, head_size)
    cosine, sine = rotary_tables(frame_times, patch_count, head_size)
    queries = low(rotate(projected[:, :, 0], cosine, sine))
    key_rows = low(rotate(projected[:, :, 1], cosine, sine)).reshape(frame_total * patch_count, HEADS, head_size)
    value_rows = low(projected[:, :, 2]).reshape(frame_total * patch_count, HEADS, head_size)
    key_frame = jnp.repeat(frame_ids, patch_count)
    key_limit = jnp.maximum(frame_ids, context - 1)

    def attend(block):
        query_block, block_limit = block
        scores = low_back(jnp.einsum('qhd,khd->hqk', query_block, key_rows, precision=HIGHEST_PRECISION) * score_scale)
        scores = jnp.where((key_frame <= block_limit)[None, None, :], scores, MASKED)
        shifted = jnp.exp(scores - lax.optimization_barrier(jnp.max(scores, axis=-1, keepdims=True)))
        weights = shifted / lax.optimization_barrier(jnp.sum(shifted, axis=-1, keepdims=True))
        return jnp.einsum('hqk,khd->qhd', low(weights), value_rows, precision=HIGHEST_PRECISION)
    attended = lax.map(jax.checkpoint(attend), (queries, key_limit))
    attended = low(low_back(attended)).reshape(-1, model_width)
    branch_one = low_back(jnp.dot(attended, proj_weight, precision=HIGHEST_PRECISION) + proj_bias)
    middle = inputs + gate_one * branch_one.reshape(frame_total, patch_count, model_width)
    normed_two = low(modulate(middle, shift_two, scale_two)).reshape(-1, model_width)
    hidden = low_back(jnp.dot(normed_two, up_weight, precision=HIGHEST_PRECISION) + up_bias)
    active = low(gelu_act(hidden))
    branch_two = low_back(jnp.dot(active, down_weight, precision=HIGHEST_PRECISION) + down_bias)
    return middle + gate_two * branch_two.reshape(frame_total, patch_count, model_width)

def reference(tokens, cotangent, context_count, noise_level, frame_time, level_table, mod_weight, mod_bias, qkv_weight, qkv_bias, proj_weight, proj_bias, up_weight, up_bias, down_weight, down_bias):
    params = tuple((item.astype(jnp.float32) for item in (level_table, mod_weight, mod_bias, qkv_weight, qkv_bias, proj_weight, proj_bias, up_weight, up_bias, down_weight, down_bias)))
    zeros = tuple((jnp.zeros_like(item) for item in params))

    def one_clip(running, item):
        clip_tokens, clip_cotangent, context, levels_in, frame_times = item

        def forward(values_in, weights_in):
            return clip_forward(values_in, weights_in, context, levels_in, frame_times)
        output, pull = jax.vjp(forward, clip_tokens.astype(jnp.float32), params)
        grad_tokens, grad_params = pull(clip_cotangent.astype(jnp.float32))
        summed = tuple((total_part + new_part for total_part, new_part in zip(running, grad_params)))
        return (summed, (output.astype(jnp.bfloat16), grad_tokens))
    sums, (layer_out, tokens_grad) = lax.scan(one_clip, zeros, (tokens, cotangent, context_count, noise_level, frame_time))
    return (layer_out, tokens_grad, sums[0], sums[1], sums[2], sums[3], sums[4], sums[5], sums[6], sums[7], sums[8], sums[9], sums[10])
```

```python
import functools

import jax
import jax.numpy as jnp
from jax import lax
from jax.experimental import pallas as pl
from jax.experimental.pallas import tpu as pltpu
from jax.sharding import PartitionSpec as P

HEADS = 16
EPS = 1e-06
HIGHEST_PRECISION = lax.Precision.HIGHEST
F32 = jnp.float32
BF16 = jnp.bfloat16
ANY = pl.BlockSpec(memory_space=pl.ANY)
VMEM = pl.BlockSpec(memory_space=pltpu.VMEM)
SMEM = pl.BlockSpec(memory_space=pltpu.SMEM)
LANES = 128
BLOCK = 256
FF_BLOCK = 512
GELU_A = 0.7978845608028654
GELU_B = 0.044715


def shaped(shape, dtype):
    return jax.ShapeDtypeStruct(shape, dtype)


def params(mib):
    return pltpu.CompilerParams(vmem_limit_bytes=mib << 20)


def cost(flops, moved, transcendentals=0):
    return pl.CostEstimate(
        flops=int(flops), bytes_accessed=int(moved), transcendentals=int(transcendentals)
    )


def dot_nn(left, right):
    return lax.dot_general(left, right, (((1,), (0,)), ((), ())), preferred_element_type=F32)


def dot_nt(left, right):
    return lax.dot_general(left, right, (((1,), (1,)), ((), ())), preferred_element_type=F32)


def dot_tn(left, right):
    return lax.dot_general(left, right, (((0,), (0,)), ((), ())), preferred_element_type=F32)


def split_heads(values, pairs, head):
    if pairs == 1:
        return [values]
    lane = lax.broadcasted_iota(jnp.int32, values.shape, 1)
    return [jnp.where(lane // head == h, values, jnp.zeros_like(values)) for h in range(pairs)]


def swap_halves(values, head):
    half = head // 2
    lane = lax.broadcasted_iota(jnp.int32, values.shape, 1)
    ahead = pltpu.roll(values, values.shape[1] - half, 1)
    behind = pltpu.roll(values, half, 1)
    return jnp.where(lax.rem(lane, head) < half, ahead, behind)


def turn(values, cosine, signed_sine, head, back):
    parts = []
    for at in range(0, values.shape[1], LANES):
        piece = values[:, at : at + LANES]
        other = swap_halves(piece, head) * signed_sine
        parts.append(piece * cosine - other if back else piece * cosine + other)
    return jnp.concatenate(parts, axis=1)


def norm_parts(values):
    center = jnp.mean(values, axis=-1, keepdims=True)
    offset = values - center
    spread = jnp.mean(offset * offset, axis=-1, keepdims=True)
    inverse = lax.rsqrt(spread + EPS)
    return offset * inverse, inverse


def norm_pull(grad, hat, inverse, scale_row):
    grad_shift = jnp.sum(grad, axis=0, keepdims=True)
    grad_scale = jnp.sum(grad * hat, axis=0, keepdims=True)
    inner = grad * (1.0 + scale_row)
    mean_one = jnp.mean(inner, axis=-1, keepdims=True)
    mean_two = jnp.mean(inner * hat, axis=-1, keepdims=True)
    return inverse * (inner - mean_one - hat * mean_two), grad_shift, grad_scale


def store_by_parity(own_ref, other_ref, where, parity, block_index, value):
    own = parity == block_index % 2

    @pl.when(own)
    def _():
        own_ref[:, where] = value

    @pl.when(jnp.logical_not(own))
    def _():
        other_ref[:, where] = value


def qkv_kernel(slots, head, meta, tokens, mod, cosine, sine, *refs):
    weights, biases = refs[:3], refs[3:6]
    outs, own, other, normed, held = refs[6 : 6 + slots], refs[-4], refs[-3], refs[-2], refs[-1]
    step = pl.program_id(0)
    me = meta[0]
    rows, width = tokens.shape
    lanes = width // slots

    @pl.when(step == 0)
    def _():
        hat, _ = norm_parts(tokens[...].astype(F32))
        low = (hat * (1.0 + mod[1:2]) + mod[0:1]).astype(BF16)
        normed[...] = low
        chunk = width // slots
        for block in range(slots):
            store_by_parity(
                own, other, slice(block // 2 * chunk, (block // 2 + 1) * chunk), me % 2, block,
                low[:, block * chunk : (block + 1) * chunk],
            )

    for kind in range(3):
        value = dot_nn(normed[...], weights[kind][...]) + biases[kind][...].astype(F32)
        if kind < 2:
            value = turn(value, cosine[...], sine[...], head, False)
        value = value.astype(BF16)
        if kind == 0:
            value = value * jnp.asarray(head**-0.5, BF16)
        for part in range(BLOCK // lanes):
            target = (step * (BLOCK // lanes) + part) ^ me
            held[target, kind] = value[:, part * lanes : (part + 1) * lanes]

    @pl.when(step == pl.num_programs(0) - 1)
    def _():
        for slot in range(slots):
            outs[slot][...] = held[slot]


def qkv_call(meta, tokens, mod, cosine, sine, weight, bias, slots, head):
    rows, width = tokens.shape
    lanes = width // slots
    steps = width // BLOCK
    whole = lambda shape: pl.BlockSpec(shape, lambda t: (0,) * len(shape))
    weight_specs = [
        pl.BlockSpec((width, BLOCK), lambda t, k=k: (0, k * steps + t)) for k in range(3)
    ]
    bias_specs = [pl.BlockSpec((1, BLOCK), lambda t, k=k: (0, k * steps + t)) for k in range(3)]
    half = width // 2
    return pl.pallas_call(
        functools.partial(qkv_kernel, slots, head),
        grid=(steps,),
        out_shape=[shaped((3, rows, lanes), BF16)] * slots + [shaped((rows, half), BF16)] * 2,
        in_specs=[SMEM, whole(tokens.shape), whole(mod.shape), whole(cosine.shape), whole(sine.shape)]
        + weight_specs
        + bias_specs,
        out_specs=[whole((3, rows, lanes))] * slots + [whole((rows, half))] * 2,
        scratch_shapes=[pltpu.VMEM((rows, width), BF16), pltpu.VMEM((slots, 3, rows, lanes), BF16)],
        compiler_params=params(32),
        cost_estimate=cost(6 * rows * width * width, 6 * width * width + 14 * rows * width),
        name="norm_qkv",
    )(meta, tokens, mod, cosine, sine, weight, weight, weight, bias, bias, bias)


def attend_kernel(slots, head, meta, *refs):
    parts, outs = refs[:slots], refs[slots : 2 * slots]
    exact, logs, held, scores, values, sems = refs[2 * slots :]
    copies = [pltpu.make_async_copy(parts[k], held.at[k], sems.at[k]) for k in range(slots)]
    for copy in copies:
        copy.start()
    for copy in copies:
        copy.wait()
    me, context = meta[0], meta[1]
    rows, width = held.shape[2], held.shape[3]
    pairs = width // head

    def prepare(frame, _):
        split = split_heads(held[frame ^ me, 2], pairs, head)
        ones = split_heads(jnp.ones((rows, width), BF16), pairs, head)
        for h in range(pairs):
            values[frame, h] = jnp.concatenate([split[h], ones[h]], axis=1)
        return 0

    lax.fori_loop(0, slots, prepare, 0)

    def attend(slot, count):
        queries = split_heads(held[slot, 0], pairs, head)
        total, tops = None, []
        for h in range(pairs):
            peak = None
            for frame in range(count):
                score = dot_nt(queries[h], held[frame ^ me, 1])
                scores[frame, h * rows : (h + 1) * rows] = score
                for at in range(0, rows, LANES):
                    piece = score[:, at : at + LANES]
                    peak = piece if peak is None else jnp.maximum(peak, piece)
            top = jnp.max(peak, axis=1, keepdims=True)
            tops.append(top)
            for frame in range(count):
                power = jnp.exp(scores[frame, h * rows : (h + 1) * rows] - top).astype(BF16)
                term = dot_nn(power, values[frame, h])
                total = term if total is None else total + term
        weight_sum = total[:, width:]
        result = total[:, :width] / weight_sum
        exact[slot] = result
        top = jnp.broadcast_to(tops[0], (rows, width))
        if pairs > 1:
            lane = lax.broadcasted_iota(jnp.int32, (rows, width), 1)
            for h in range(1, pairs):
                top = jnp.where(lane // head >= h, tops[h], top)
        turned = (top + jnp.log(weight_sum)).T
        logs[slot] = jnp.concatenate(
            [turned[h * head : h * head + 1] for h in range(pairs)], axis=1
        )

    def one_frame(frame, _):
        count = jnp.maximum(frame, context - 1) + 1
        for known in range(1, slots + 1):

            @pl.when(count == known)
            def _():
                attend(frame ^ me, known)

        return 0

    lax.fori_loop(0, slots, one_frame, 0)
    for slot in range(slots):
        outs[slot][...] = exact[slot].astype(BF16)


def attend_call(meta, parts, head):
    slots = len(parts)
    _, rows, width = parts[0].shape
    pairs = width // head
    work = slots * slots * rows * rows
    return pl.pallas_call(
        functools.partial(attend_kernel, slots, head),
        out_shape=[shaped((rows, width), BF16)] * slots
        + [shaped((slots, rows, width), F32), shaped((slots, 1, pairs * rows), F32)],
        in_specs=[SMEM] + [ANY] * slots,
        out_specs=[VMEM] * (slots + 2),
        scratch_shapes=[
            pltpu.VMEM((slots, 3, rows, width), BF16),
            pltpu.VMEM((slots, pairs * rows, rows), F32),
            pltpu.VMEM((slots, pairs, rows, 2 * width), BF16),
            pltpu.SemaphoreType.DMA((slots,)),
        ],
        compiler_params=params(40),
        cost_estimate=cost(work * 16 * width, slots * rows * width * 12, work * pairs),
        name="attend",
    )(meta, *parts)


def attend_grad_kernel(slots, head, meta, *refs):
    parts, grads = refs[:slots], refs[slots : 2 * slots]
    exact, logs = refs[2 * slots], refs[2 * slots + 1]
    outs = refs[2 * slots + 2 : 3 * slots + 2]
    held, grad, query_rows, grad_rows, delta, grad_q, grad_k, grad_v, sems, more = refs[
        3 * slots + 2 :
    ]
    copies = [pltpu.make_async_copy(parts[k], held.at[k], sems.at[k]) for k in range(slots)]
    copies += [pltpu.make_async_copy(grads[k], grad.at[k], more.at[k]) for k in range(slots)]
    for copy in copies:
        copy.start()
    for copy in copies:
        copy.wait()
    me, context = meta[0], meta[1]
    rows, width = held.shape[2], held.shape[3]
    pairs = width // head

    def prepare(slot, _):
        query_rows[slot] = jnp.concatenate(split_heads(held[slot, 0], pairs, head), axis=0)
        grad_rows[slot] = jnp.concatenate(split_heads(grad[slot], pairs, head), axis=0)
        product = (grad[slot].astype(F32) * exact[slot]).T
        delta[slot] = jnp.concatenate(
            [
                jnp.sum(product[h * head : (h + 1) * head], axis=0, keepdims=True)
                for h in range(pairs)
            ],
            axis=1,
        )
        grad_q[slot] = jnp.zeros((rows, width), F32)
        return 0

    lax.fori_loop(0, slots, prepare, 0)

    def key_frame(frame, _):
        place = frame ^ me
        keys, values = held[place, 1], held[place, 2]
        head_keys = split_heads(keys, pairs, head)
        grad_k[...] = jnp.zeros_like(grad_k)
        grad_v[...] = jnp.zeros_like(grad_v)

        def query_frame(query, _):
            slot = query ^ me
            score = dot_nt(keys, query_rows[slot])
            grad_weight = dot_nt(values, grad_rows[slot])
            weight = jnp.exp(score - logs[slot])
            grad_score = (weight * (grad_weight - delta[slot])).astype(BF16)
            grad_v[...] += dot_nn(weight.astype(BF16), grad_rows[slot])
            grad_k[...] += dot_nn(grad_score, query_rows[slot])
            total = grad_q[slot]
            for h in range(pairs):
                total = total + dot_tn(grad_score[:, h * rows : (h + 1) * rows], head_keys[h])
            grad_q[slot] = total
            return 0

        lax.fori_loop(jnp.where(frame < context, 0, frame), slots, query_frame, 0)
        held[place, 1] = grad_k[...].astype(BF16)
        held[place, 2] = grad_v[...].astype(BF16)
        return 0

    lax.fori_loop(0, slots, key_frame, 0)
    for slot in range(slots):
        outs[slot][0] = (grad_q[slot] * head**-0.5).astype(BF16)
        outs[slot][1] = held[slot, 1]
        outs[slot][2] = held[slot, 2]


def attend_grad_call(meta, parts, grads, exact, logs, head):
    slots = len(parts)
    _, rows, width = parts[0].shape
    pairs = width // head
    work = slots * slots * rows * rows
    return pl.pallas_call(
        functools.partial(attend_grad_kernel, slots, head),
        out_shape=[shaped((3, rows, width), BF16)] * slots,
        in_specs=[SMEM] + [ANY] * (2 * slots) + [VMEM, VMEM],
        out_specs=[VMEM] * slots,
        scratch_shapes=[
            pltpu.VMEM((slots, 3, rows, width), BF16),
            pltpu.VMEM((slots, rows, width), BF16),
            pltpu.VMEM((slots, pairs * rows, width), BF16),
            pltpu.VMEM((slots, pairs * rows, width), BF16),
            pltpu.VMEM((slots, 1, pairs * rows), F32),
            pltpu.VMEM((slots, rows, width), F32),
            pltpu.VMEM((rows, width), F32),
            pltpu.VMEM((rows, width), F32),
            pltpu.SemaphoreType.DMA((slots,)),
            pltpu.SemaphoreType.DMA((slots,)),
        ],
        compiler_params=params(40),
        cost_estimate=cost(work * 40 * width, slots * rows * width * 20, work * pairs),
        name="attend_grad",
    )(meta, *parts, *grads, exact, logs)


def forward_back_kernel(slots, meta, tokens, cotangent, mod, proj_b, up_b, down_b, *refs):
    parts, (proj_hbm, up_hbm, down_hbm) = refs[:slots], refs[slots : slots + 3]
    (
        layer_out, grad_middle_out, row_grads, up_bgrad,
        att_own, att_other, gone_low,
        n2_own, n2_other, hid_low,
        act_own, act_other, gtwo_low,
    ) = refs[slots + 3 : slots + 16]
    grads_out = refs[slots + 16 : 2 * slots + 16]
    held, proj, up, down, slope, active, sems = refs[2 * slots + 16 :]
    copies = [pltpu.make_async_copy(parts[k], held.at[k], sems.at[k]) for k in range(slots)]
    proj_copy = pltpu.make_async_copy(proj_hbm, proj, sems.at[slots])
    up_copy = pltpu.make_async_copy(up_hbm, up, sems.at[slots + 1])
    down_copy = pltpu.make_async_copy(down_hbm, down, sems.at[slots + 2])
    for copy in copies:
        copy.start()
    proj_copy.start()
    up_copy.start()
    down_copy.start()
    me = meta[0]
    parity = me % 2
    rows, width = tokens.shape
    lanes = width // slots
    hidden_width = up.shape[1]
    gate_one, shift_two, scale_two, gate_two = (mod[k : k + 1] for k in (2, 3, 4, 5))
    for copy in copies:
        copy.wait()
    attended = jnp.concatenate([held[k ^ me] for k in range(slots)], axis=1)
    for block in range(slots):
        store_by_parity(
            att_own, att_other, slice(block // 2 * lanes, (block // 2 + 1) * lanes), parity, block,
            held[block ^ me],
        )
    proj_copy.wait()
    branch_one = dot_nn(attended, proj[...]) + proj_b[...].astype(F32)
    middle = tokens[...].astype(F32) + gate_one * branch_one
    hat_two, inverse_two = norm_parts(middle)
    low_two = (hat_two * (1.0 + scale_two) + shift_two).astype(BF16)
    for block in range(slots):
        store_by_parity(
            n2_own, n2_other, slice(block // 2 * lanes, (block // 2 + 1) * lanes), parity, block,
            low_two[:, block * lanes : (block + 1) * lanes],
        )
    up_copy.wait()
    chunk = hidden_width // slots
    for block in range(hidden_width // FF_BLOCK):
        at = slice(block * FF_BLOCK, (block + 1) * FF_BLOCK)
        hidden = dot_nn(low_two, up[:, at]) + up_b[:, at].astype(F32)
        square = hidden * hidden
        bent = jnp.tanh(GELU_A * (hidden + GELU_B * square * hidden))
        half = 0.5 * (1.0 + bent)
        low = (hidden * half).astype(BF16)
        slope[:, at] = half + (0.5 * GELU_A) * hidden * (1.0 - bent * bent) * (
            1.0 + (3.0 * GELU_B) * square
        )
        active[:, at] = low
        for piece in range(FF_BLOCK // chunk):
            index = block * (FF_BLOCK // chunk) + piece
            store_by_parity(
                act_own, act_other, slice(index // 2 * chunk, (index // 2 + 1) * chunk), parity,
                index, low[:, piece * chunk : (piece + 1) * chunk],
            )
    down_copy.wait()
    branch_two = dot_nn(active[...], down[...]) + down_b[...].astype(F32)
    layer_out[...] = (middle + gate_two * branch_two).astype(BF16)
    grad_out = cotangent[...].astype(F32)
    low_grad_two = (grad_out * gate_two).astype(BF16)
    gtwo_low[...] = low_grad_two
    row_grads[3:4] = jnp.sum(grad_out * branch_two, axis=0, keepdims=True)
    row_grads[4:5] = jnp.sum(low_grad_two.astype(F32), axis=0, keepdims=True)
    grad_normed = None
    for block in range(hidden_width // FF_BLOCK):
        at = slice(block * FF_BLOCK, (block + 1) * FF_BLOCK)
        low = (dot_nt(low_grad_two, down[at, :]) * slope[:, at]).astype(BF16)
        hid_low[:, at] = low
        up_bgrad[:, at] = jnp.sum(low.astype(F32), axis=0, keepdims=True)
        term = dot_nt(low, up[:, at])
        grad_normed = term if grad_normed is None else grad_normed + term
    grad_middle, grad_shift, grad_scale = norm_pull(grad_normed, hat_two, inverse_two, scale_two)
    grad_middle = grad_middle + grad_out
    grad_middle_out[...] = grad_middle
    low_grad_one = (grad_middle * gate_one).astype(BF16)
    gone_low[...] = low_grad_one
    row_grads[0:1] = jnp.sum(grad_middle * branch_one, axis=0, keepdims=True)
    row_grads[1:2] = grad_shift
    row_grads[2:3] = grad_scale
    row_grads[5:6] = jnp.sum(low_grad_one.astype(F32), axis=0, keepdims=True)
    row_grads[6:8] = jnp.zeros((2, width), F32)
    grad_attended = dot_nt(low_grad_one, proj[...]).astype(BF16)
    for block in range(slots):
        held[block ^ me] = grad_attended[:, block * lanes : (block + 1) * lanes]
    for slot in range(slots):
        grads_out[slot][...] = held[slot]


def forward_back_call(
    meta, tokens, cotangent, mod, proj_b, up_b, down_b, parts, proj, up, down
):
    slots = len(parts)
    rows, width = tokens.shape
    lanes = width // slots
    hidden = up.shape[1]
    half, half_hidden = width // 2, hidden // 2
    out_shape = [
        shaped((rows, width), BF16),
        shaped((rows, width), F32),
        shaped((8, width), F32),
        shaped((1, hidden), F32),
        shaped((rows, half), BF16),
        shaped((rows, half), BF16),
        shaped((rows, width), BF16),
        shaped((rows, half), BF16),
        shaped((rows, half), BF16),
        shaped((rows, hidden), BF16),
        shaped((rows, half_hidden), BF16),
        shaped((rows, half_hidden), BF16),
        shaped((rows, width), BF16),
    ] + [shaped((rows, lanes), BF16)] * slots
    return pl.pallas_call(
        functools.partial(forward_back_kernel, slots),
        out_shape=out_shape,
        in_specs=[SMEM] + [VMEM] * 6 + [ANY] * (slots + 3),
        out_specs=[VMEM] * len(out_shape),
        scratch_shapes=[
            pltpu.VMEM((slots, rows, lanes), BF16),
            pltpu.VMEM(proj.shape, BF16),
            pltpu.VMEM(up.shape, BF16),
            pltpu.VMEM(down.shape, BF16),
            pltpu.VMEM((rows, hidden), F32),
            pltpu.VMEM((rows, hidden), BF16),
            pltpu.SemaphoreType.DMA((slots + 3,)),
        ],
        compiler_params=params(56),
        cost_estimate=cost(
            4 * rows * width * (width + 2 * hidden),
            4 * width * (width + 2 * hidden),
            rows * hidden,
        ),
        name="feed_forward",
    )(meta, tokens, cotangent, mod, proj_b, up_b, down_b, *parts, proj, up, down)


def qkv_grad_kernel(slots, head, meta, tokens, mod, cosine, sine, grad_middle, *refs):
    parts, weights = refs[:slots], refs[slots : slots + 3]
    tokens_grad, row_grads, outs = refs[slots + 3], refs[slots + 4], refs[slots + 5 : slots + 8]
    bias_grads = refs[slots + 8 : slots + 11]
    held, total, sems = refs[slots + 11 :]
    step = pl.program_id(0)
    me = meta[0]
    rows, width = tokens.shape
    lanes = width // slots

    @pl.when(step == 0)
    def _():
        copies = [pltpu.make_async_copy(parts[k], held.at[k], sems.at[k]) for k in range(slots)]
        for copy in copies:
            copy.start()
        for copy in copies:
            copy.wait()
        total[...] = jnp.zeros_like(total)

    term = None
    for kind in range(3):
        pieces = [
            held[(step * (BLOCK // lanes) + part) ^ me, kind] for part in range(BLOCK // lanes)
        ]
        low = jnp.concatenate(pieces, axis=1)
        if kind < 2:
            low = turn(low.astype(F32), cosine[...], sine[...], head, True).astype(BF16)
        outs[kind][...] = low
        bias_grads[kind][...] = jnp.sum(low.astype(F32), axis=0, keepdims=True)
        product = dot_nt(low, weights[kind][...])
        term = product if term is None else term + product
    total[...] += term

    @pl.when(step == pl.num_programs(0) - 1)
    def _():
        hat, inverse = norm_parts(tokens[...].astype(F32))
        grad, grad_shift, grad_scale = norm_pull(total[...], hat, inverse, mod[1:2])
        tokens_grad[...] = grad + grad_middle[...]
        row_grads[0:1] = grad_shift
        row_grads[1:2] = grad_scale
        row_grads[2:8] = jnp.zeros((6, width), F32)


def qkv_grad_call(meta, tokens, mod, cosine, sine, grad_middle, parts, weight, head):
    slots = len(parts)
    rows, width = tokens.shape
    lanes = width // slots
    steps = width // BLOCK
    whole = lambda shape: pl.BlockSpec(shape, lambda t: (0,) * len(shape))
    weight_specs = [
        pl.BlockSpec((width, BLOCK), lambda t, k=k: (0, k * steps + t)) for k in range(3)
    ]
    column = lambda height: pl.BlockSpec((height, BLOCK), lambda t: (0, t))
    return pl.pallas_call(
        functools.partial(qkv_grad_kernel, slots, head),
        grid=(steps,),
        out_shape=[shaped((rows, width), F32), shaped((8, width), F32)]
        + [shaped((rows, width), BF16)] * 3
        + [shaped((1, width), F32)] * 3,
        in_specs=[SMEM]
        + [whole(a.shape) for a in (tokens, mod, cosine, sine, grad_middle)]
        + [ANY] * slots
        + weight_specs,
        out_specs=[whole((rows, width)), whole((8, width))] + [column(rows)] * 3 + [column(1)] * 3,
        scratch_shapes=[
            pltpu.VMEM((slots, 3, rows, lanes), BF16),
            pltpu.VMEM((rows, width), F32),
            pltpu.SemaphoreType.DMA((slots,)),
        ],
        compiler_params=params(32),
        cost_estimate=cost(6 * rows * width * width, 6 * width * width + 20 * rows * width),
        name="qkv_grad",
    )(meta, tokens, mod, cosine, sine, grad_middle, *parts, weight, weight, weight)


def weight_grad_kernel(jobs, pieces, zs, meta, *refs):
    count = sum(job[0] + job[1] for job in jobs)
    outs = refs[count : count + pieces]
    held, sems = refs[-2:]
    step = pl.program_id(0) * pl.num_programs(1) + pl.program_id(1)
    last = pl.num_programs(0) * pl.num_programs(1) - 1
    slot = step % 2
    tile_rows, cols = held.shape[1] * held.shape[2], held.shape[3]

    def drain(which):
        pltpu.make_async_copy(held.at[which], held.at[which], sems.at[which]).wait()

    @pl.when(step >= 2)
    def _():
        drain(slot)

    at = 0
    index = 0
    for rows_n, cols_n, tall, repeats, first in jobs:
        lefts = refs[at : at + rows_n]
        rights = refs[at + rows_n : at + rows_n + cols_n]
        at += rows_n + cols_n
        for repeat in range(repeats):

            @pl.when(pl.program_id(1) == index)
            def _():
                total = None
                for left, right in zip(lefts, rights):
                    picked = left[:, repeat * tile_rows : (repeat + 1) * tile_rows] if tall else left[...]
                    term = dot_tn(picked, right[...])
                    total = term if total is None else total + term
                value = total.astype(BF16)
                height = tile_rows // zs
                held[slot] = value.reshape(held.shape[1:])
                for k in range(pieces):

                    @pl.when(pl.program_id(0) == k)
                    def _():
                        if tall:
                            for z in range(zs):
                                place = repeat * zs + z
                                inner = first + place % repeats * height
                                pltpu.make_async_copy(
                                    held.at[slot, z],
                                    outs[k].at[place // repeats, pl.ds(inner, height)],
                                    sems.at[slot],
                                ).start()
                        else:
                            pltpu.make_async_copy(
                                held.at[slot],
                                outs[k].at[:, pl.ds(first + repeat * height, height)],
                                sems.at[slot],
                            ).start()

            index += 1

    @pl.when(step == last)
    def _():
        drain(1 - slot)
        drain(slot)


def weight_grad_call(meta, products, pieces, zs, name):
    jobs, specs, arrays = [], [], []
    first = 0
    width = products[0][0][0].shape[1]
    cols = 2 * width // pieces
    height = width // zs
    flops = 0
    steps = sum(
        (p[0][0].shape[1] // width) if p[2] else (p[1][0].shape[1] // (2 * width)) for p in products
    )
    index = 0
    for lefts, rights, tall in products:
        repeats = lefts[0].shape[1] // width if tall else rights[0].shape[1] // (2 * width)
        jobs.append((len(lefts), len(rights), tall, repeats, first))
        first += height * repeats
        for left in lefts:
            arrays.append(left)
            specs.append(pl.BlockSpec(left.shape, lambda e, t, m: (0, 0)))
            flops += 2 * left.shape[0] * left.shape[1] * rights[0].shape[1]
        for right in rights:
            arrays.append(right)
            start = index

            def place(e, t, m, start=start, repeats=repeats, tall=tall):
                block = 0 if tall else jnp.clip(t - start, 0, repeats - 1)
                return (0, block * pieces + (e ^ m[2]))

            specs.append(pl.BlockSpec((right.shape[0], cols), place))
        index += repeats
    out = shaped((zs, first, cols), BF16)
    return pl.pallas_call(
        functools.partial(weight_grad_kernel, tuple(jobs), pieces, zs),
        out_shape=[out] * pieces,
        grid_spec=pltpu.PrefetchScalarGridSpec(
            num_scalar_prefetch=1,
            grid=(pieces, steps),
            in_specs=specs,
            out_specs=[ANY] * pieces,
            scratch_shapes=[
                pltpu.VMEM((2, zs, height, cols), BF16),
                pltpu.SemaphoreType.DMA((2,)),
            ],
        ),
        compiler_params=params(48),
        cost_estimate=cost(flops, sum(a.size * 2 for a in arrays) + pieces * zs * first * cols * 2),
        name=name,
    )(meta, *arrays)


def unpack_kernel(jobs, pieces, meta, *refs):
    parts, outs = refs[:pieces], refs[pieces:]
    clip = meta[2]
    cols = parts[0].shape[1]
    for e in range(pieces):
        first = 0
        for out, (height, repeats, tall) in zip(outs, jobs):
            for repeat in range(repeats):
                base = 0 if tall else repeat * cols * pieces
                target = pl.ds(pl.multiple_of(base + (clip ^ e) * cols, cols), cols)
                value = parts[e][first : first + height].astype(F32)
                if tall:
                    out[repeat * height : (repeat + 1) * height, target] = value
                else:
                    out[:, target] = value
                first += height


def unpack_call(meta, parts, jobs, outs, name):
    return pl.pallas_call(
        functools.partial(unpack_kernel, jobs, len(parts)),
        out_shape=outs,
        in_specs=[SMEM] + [VMEM] * len(parts),
        out_specs=[VMEM] * len(outs),
        compiler_params=params(32),
        cost_estimate=cost(0, sum(o.size * 4 for o in outs)),
        name=name,
    )(meta, *parts)


def exchange(array, axis, size, distance):
    return lax.ppermute(array, axis, [(k, k ^ distance) for k in range(size)])


def spread(slots_out, axis, size):
    return [slots_out[0]] + [exchange(slots_out[d], axis, size, d) for d in range(1, size)]


def sum_shares(shares, clip_size, seq_size, me):
    zs = seq_size // 2
    arrived = spread(shares, "clip", clip_size)
    kept = []
    for k in range(zs):
        total = None
        for share in arrived:
            part = lax.dynamic_index_in_dim(share, (me // 2) ^ k, 0, keepdims=False).astype(F32)
            total = part if total is None else total + part
        kept.append(total.astype(BF16))
    landed = [kept[0]] + [exchange(kept[k], "seq", seq_size, 2 * k) for k in range(1, zs)]
    total = landed[0].astype(F32)
    for part in landed[1:]:
        total = total + part.astype(F32)
    return total.astype(BF16)


def gather_pieces(piece, clip_size):
    return [piece] + [exchange(piece, "clip", clip_size, d) for d in range(1, clip_size)]


def gather_all(rows, clip_size, seq_size):
    by_seq = jnp.stack([rows] + [exchange(rows, "seq", seq_size, d) for d in range(1, seq_size)])
    return jnp.concatenate(
        [by_seq] + [exchange(by_seq, "clip", clip_size, d) for d in range(1, clip_size)]
    )


def silu_act(values_in):
    return values_in * jax.nn.sigmoid(values_in)


def rotary_tables(stamps, patch_count, head):
    lane = jnp.arange(LANES, dtype=jnp.int32)
    quarter = head // 4
    pair = lane % (head // 2)
    freqs = 10000.0 ** (-(pair % quarter).astype(F32) / quarter)
    temporal = stamps.astype(F32)[:, None, None] * freqs[None, None, :]
    spatial = jnp.arange(patch_count).astype(F32)[None, :, None] * freqs[None, None, :]
    angles = jnp.where((pair < quarter)[None, None, :], temporal, spatial)
    sign = jnp.where(lane % head < head // 2, -1.0, 1.0).astype(F32)
    return jnp.cos(angles), jnp.sin(angles) * sign[None, None, :]


def on_device(
    tokens,
    cotangent,
    context_count,
    noise_level,
    frame_time,
    level_table,
    mod_weight,
    mod_bias,
    qkv_weight,
    qkv_bias,
    proj_weight,
    proj_bias,
    up_weight,
    up_bias,
    down_weight,
    down_bias,
):
    seq_size, clip_size = lax.axis_size("seq"), lax.axis_size("clip")
    me, mine = lax.axis_index("seq"), lax.axis_index("clip")
    clips, _, rows, width = tokens.shape
    head = width // HEADS
    hidden = up_weight.shape[1]
    zs = seq_size // 2
    me = me.astype(jnp.int32)
    mine = mine.astype(jnp.int32)
    metas = [jnp.stack([me, context_count[c], mine]) for c in range(clips)]
    levels_used = jnp.where(me < context_count, 0, noise_level[:, 0])
    condition = jnp.concatenate(
        [
            lax.dynamic_slice(level_table, (levels_used[c], jnp.int32(0)), (1, width))
            for c in range(clips)
        ]
    )
    condition_low = silu_act(condition.astype(F32)).astype(BF16)
    modulation = jnp.dot(
        condition_low, mod_weight, preferred_element_type=F32
    ) + mod_bias.astype(F32)
    mods = modulation.reshape(clips, 6, width)
    cosine, sine = rotary_tables(frame_time[:, 0], rows, head)

    level_rows = jnp.stack([levels_used // 32, levels_used % 32]).astype(BF16)
    level_rows = jnp.concatenate([level_rows, jnp.zeros((2, width - clips), BF16)], axis=1)
    early = jnp.concatenate(
        [condition, level_rows, jnp.zeros((16 - clips - 2, width), BF16)], axis=0
    )
    early = gather_all(early, clip_size, seq_size)

    qkv_bias_row = qkv_bias[None]
    sent, normed_own, normed_other = [], [], []
    for c in range(clips):
        out = qkv_call(
            metas[c], tokens[c, 0], mods[c], cosine[c], sine[c], qkv_weight, qkv_bias_row,
            seq_size, head,
        )
        sent.append(out[:seq_size])
        normed_own.append(out[seq_size])
        normed_other.append(out[seq_size + 1])
    parts = [spread(s, "seq", seq_size) for s in sent]
    attended, exact, logs = [], [], []
    for c in range(clips):
        out = attend_call(metas[c], parts[c], head)
        attended.append(spread(out[:seq_size], "seq", seq_size))
        exact.append(out[seq_size])
        logs.append(out[seq_size + 1])
    layer, middles, row_grads, up_bgrads, saved, grads = [], [], [], [], [], []
    for c in range(clips):
        out = forward_back_call(
            metas[c], tokens[c, 0], cotangent[c, 0], mods[c], proj_bias[None], up_bias[None],
            down_bias[None], attended[c], proj_weight, up_weight, down_weight,
        )
        layer.append(out[0])
        middles.append(out[1])
        row_grads.append(out[2])
        up_bgrads.append(out[3])
        saved.append(out[4:13])
        grads.append(spread(out[13:], "seq", seq_size))
    swap = lambda array: exchange(array, "seq", seq_size, 1)
    products = []
    for own, other, right, tall in ((3, 4, 5, False), (6, 7, 8, True), (0, 1, 2, False)):
        lefts, rights = [], []
        for c in range(clips):
            lefts += [saved[c][own], swap(saved[c][other])]
            rights += [saved[c][right], swap(saved[c][right])]
        products.append((lefts, rights, tall))
    shares = weight_grad_call(metas[0], products, clip_size, zs, "weight_grads")
    piece = sum_shares(shares, clip_size, seq_size, me)
    row = width // seq_size
    up_wgrad, down_wgrad, proj_wgrad = unpack_call(
        metas[0],
        gather_pieces(piece, clip_size),
        (
            (row, hidden // width, False),
            (row, hidden // width, True),
            (row, 1, False),
        ),
        [shaped((row, hidden), F32), shaped((hidden // seq_size, width), F32), shaped((row, width), F32)],
        "place_weight_grads",
    )

    returned = []
    for c in range(clips):
        out = attend_grad_call(metas[c], parts[c], grads[c], exact[c], logs[c], head)
        returned.append(spread(out, "seq", seq_size))
    tokens_grads, late_rows, grad_projected, qkv_bgrads = [], [], [], []
    for c in range(clips):
        out = qkv_grad_call(
            metas[c], tokens[c, 0], mods[c], cosine[c], sine[c], middles[c], returned[c],
            qkv_weight, head,
        )
        tokens_grads.append(out[0])
        late_rows.append(out[1])
        grad_projected.append(out[2:5])
        qkv_bgrads.append(jnp.concatenate(out[5:8], axis=0))
    lefts = []
    for c in range(clips):
        lefts += [normed_own[c], swap(normed_other[c])]
    products = []
    for kind in range(3):
        rights = []
        for c in range(clips):
            rights += [grad_projected[c][kind], swap(grad_projected[c][kind])]
        products.append((lefts, rights, False))
    shares = weight_grad_call(metas[0], products, clip_size, zs, "qkv_weight_grad")
    piece = sum_shares(shares, clip_size, seq_size, me)
    (qkv_wgrad,) = unpack_call(
        metas[0],
        gather_pieces(piece, clip_size),
        ((row, 3, False),),
        [shaped((row, 3 * width), F32)],
        "place_qkv_grad",
    )

    mod_rows = [
        jnp.concatenate([late_rows[c][0:2], row_grads[c][0:4]], axis=0) for c in range(clips)
    ]
    bias_rows = [
        sum(qkv_bgrads),
        sum(up_bgrads).reshape(hidden // width, width),
        sum(r[4:5] for r in row_grads),
        sum(r[5:6] for r in row_grads),
    ]
    late = jnp.concatenate(mod_rows + bias_rows, axis=0).astype(BF16)
    used = late.shape[0]
    late = jnp.concatenate([late, jnp.zeros((-used % 16, width), BF16)], axis=0)
    late = gather_all(late, clip_size, seq_size)
    devices = late.shape[0]
    grad_modulation = late[:, : 6 * clips].reshape(devices * clips, 6 * width)
    bias_sums = jnp.sum(late[:, 6 * clips : used].astype(F32), axis=0)
    all_condition = early[:, :clips].reshape(devices * clips, width).astype(F32)
    codes = early[:, clips : clips + 2, :clips].astype(jnp.int32)
    all_levels = (codes[:, 0] * 32 + codes[:, 1]).reshape(devices * clips)
    all_active, silu_pull = jax.vjp(silu_act, all_condition)
    my_active = lax.dynamic_slice_in_dim(all_active, me * row, row, axis=1).astype(BF16)
    mod_wgrad = lax.dot_general(
        my_active, grad_modulation, (((0,), (0,)), ((), ())), preferred_element_type=F32
    )
    (grad_condition,) = silu_pull(
        lax.dot_general(
            grad_modulation, mod_weight, (((1,), (1,)), ((), ())), preferred_element_type=F32
        )
    )
    table_row = level_table.shape[0] // seq_size
    onehot = (
        all_levels[:, None] == (me * table_row + jnp.arange(table_row, dtype=jnp.int32))[None, :]
    ).astype(F32)
    table_grad = lax.dot_general(
        onehot,
        grad_condition,
        (((0,), (0,)), ((), ())),
        precision=HIGHEST_PRECISION,
        preferred_element_type=F32,
    )
    mod_sums = jnp.sum(grad_modulation.astype(F32), axis=0)

    def own_part(vector):
        size = vector.shape[0] // seq_size
        return lax.dynamic_slice_in_dim(vector, me * size, size, axis=0)

    mod_bgrad = own_part(mod_sums)
    qkv_bgrad = own_part(bias_sums[:3].reshape(3 * width))
    up_bgrad = own_part(bias_sums[3 : 3 + hidden // width].reshape(hidden))
    down_bgrad = own_part(bias_sums[3 + hidden // width])
    proj_bgrad = own_part(bias_sums[4 + hidden // width])
    layer_out = jnp.stack(layer)[:, None]
    tokens_grad = jnp.stack(tokens_grads)[:, None]
    return (
        layer_out,
        tokens_grad,
        table_grad,
        mod_wgrad,
        mod_bgrad,
        qkv_wgrad,
        qkv_bgrad,
        proj_wgrad,
        proj_bgrad,
        up_wgrad,
        up_bgrad,
        down_wgrad,
        down_bgrad,
    )


def solution(mesh):
    placed = (
        P("clip", "seq", None, None),
        P("clip", "seq", None, None),
        P("clip"),
        P("clip", "seq"),
        P("clip", "seq"),
    ) + (P(),) * 11
    return jax.shard_map(
        on_device,
        mesh=mesh,
        in_specs=placed,
        out_specs=(
            P("clip", "seq", None, None),
            P("clip", "seq", None, None),
            P("seq", None),
            P("seq", None),
            P("seq"),
            P("seq", None),
            P("seq"),
            P("seq", None),
            P("seq"),
            P("seq", None),
            P("seq"),
            P("seq", None),
            P("seq"),
        ),
        check_vma=False,
    )
```

```python
import functools

import jax
import jax.numpy as jnp
from jax import lax
from jax.experimental import pallas as pl
from jax.experimental.pallas import tpu as pltpu
from jax.sharding import PartitionSpec as P

HEADS = 16
EPS = 1e-06
HIGHEST_PRECISION = lax.Precision.HIGHEST
F32 = jnp.float32
BF16 = jnp.bfloat16
ANY = pl.BlockSpec(memory_space=pl.ANY)
VMEM = pl.BlockSpec(memory_space=pltpu.VMEM)
SMEM = pl.BlockSpec(memory_space=pltpu.SMEM)
LANES = 128
BLOCK = 256
FF_BLOCK = 512
GELU_A = 0.7978845608028654
GELU_B = 0.044715


def shaped(shape, dtype):
    return jax.ShapeDtypeStruct(shape, dtype)


def params(mib):
    return pltpu.CompilerParams(vmem_limit_bytes=mib << 20)


def cost(flops, moved, transcendentals=0):
    return pl.CostEstimate(
        flops=int(flops), bytes_accessed=int(moved), transcendentals=int(transcendentals)
    )


def dot_nn(left, right):
    return lax.dot_general(left, right, (((1,), (0,)), ((), ())), preferred_element_type=F32)


def dot_nt(left, right):
    return lax.dot_general(left, right, (((1,), (1,)), ((), ())), preferred_element_type=F32)


def dot_tn(left, right):
    return lax.dot_general(left, right, (((0,), (0,)), ((), ())), preferred_element_type=F32)


def split_heads(values, pairs, head):
    if pairs == 1:
        return [values]
    lane = lax.broadcasted_iota(jnp.int32, values.shape, 1)
    return [jnp.where(lane // head == h, values, jnp.zeros_like(values)) for h in range(pairs)]


def swap_halves(values, head):
    half = head // 2
    lane = lax.broadcasted_iota(jnp.int32, values.shape, 1)
    ahead = pltpu.roll(values, values.shape[1] - half, 1)
    behind = pltpu.roll(values, half, 1)
    return jnp.where(lax.rem(lane, head) < half, ahead, behind)


def turn(values, cosine, signed_sine, head, back):
    parts = []
    for at in range(0, values.shape[1], LANES):
        piece = values[:, at : at + LANES]
        other = swap_halves(piece, head) * signed_sine
        parts.append(piece * cosine - other if back else piece * cosine + other)
    return jnp.concatenate(parts, axis=1)


def norm_parts(values):
    center = jnp.mean(values, axis=-1, keepdims=True)
    offset = values - center
    spread = jnp.mean(offset * offset, axis=-1, keepdims=True)
    inverse = lax.rsqrt(spread + EPS)
    return offset * inverse, inverse


def norm_pull(grad, hat, inverse, scale_row):
    grad_shift = jnp.sum(grad, axis=0, keepdims=True)
    grad_scale = jnp.sum(grad * hat, axis=0, keepdims=True)
    inner = grad * (1.0 + scale_row)
    mean_one = jnp.mean(inner, axis=-1, keepdims=True)
    mean_two = jnp.mean(inner * hat, axis=-1, keepdims=True)
    return inverse * (inner - mean_one - hat * mean_two), grad_shift, grad_scale


def store_by_parity(own_ref, other_ref, where, parity, block_index, value):
    own = parity == block_index % 2

    @pl.when(own)
    def _():
        own_ref[:, where] = value

    @pl.when(jnp.logical_not(own))
    def _():
        other_ref[:, where] = value


def half_columns(weight, groups, parity):
    rows, total = weight.shape
    view = weight.reshape(rows, 3, groups // 2, 2, total // (3 * groups))
    return lax.dynamic_index_in_dim(view, parity, 3, keepdims=False).reshape(rows, total // 2)


def half_specs(height, width, groups, aligned):
    specs = []
    for kind in range(3):
        for block in range(width // (2 * LANES)):
            if aligned:
                specs.append(
                    pl.BlockSpec(
                        (height, LANES), lambda t, m, k=kind, b=block: (0, k * groups + 2 * b + m[0] % 2)
                    )
                )
            else:
                specs.append(
                    pl.BlockSpec(
                        (height, LANES),
                        lambda t, m, k=kind, b=block: (0, k * (width // (2 * LANES)) + b),
                    )
                )
    return specs


def qkv_kernel(zs, head, clip, meta, tokens, other_tokens, mod, cosine, sine, *refs):
    blocks = tokens.shape[-1] // (2 * LANES)
    weights, biases = refs[: 3 * blocks], refs[3 * blocks : 6 * blocks]
    outs, normed_outs, (normed, held) = refs[6 * blocks : 6 * blocks + zs], refs[-4:-2], refs[-2:]
    rows, width = tokens.shape[-2:]
    lanes = width // (2 * zs)
    clips = mod.shape[0] // 2
    z = meta[0] // 2
    for role, source in enumerate((tokens, other_tokens)):
        row = role * clips + clip
        hat, _ = norm_parts(source[...].reshape(rows, width).astype(F32))
        low = (hat * (1.0 + mod[row, 1:2]) + mod[row, 0:1]).astype(BF16)
        normed[role * rows : (role + 1) * rows] = low
        normed_outs[role][...] = low
    for kind in range(3):
        pick = slice(kind * blocks, (kind + 1) * blocks)
        weight = jnp.concatenate([w[...] for w in weights[pick]], axis=1)
        bias = jnp.concatenate([b[...] for b in biases[pick]], axis=1).astype(F32)
        for role in range(2):
            row = role * clips + clip
            value = dot_nn(normed[role * rows : (role + 1) * rows], weight) + bias
            if kind < 2:
                value = turn(value, cosine[row], sine[row], head, False)
            value = value.astype(BF16)
            if kind == 0:
                value = value * jnp.asarray(head**-0.5, BF16)
            for group in range(zs):
                held[group ^ z, role, kind] = value[:, group * lanes : (group + 1) * lanes]
    for slot in range(zs):
        outs[slot][...] = held[slot]


def qkv_call(meta, clip, tokens, other_tokens, mod, cosine, sine, weight, bias, zs, head, aligned):
    rows, width = tokens.shape[-2:]
    lanes = width // (2 * zs)
    whole = lambda a: pl.BlockSpec(a.shape, lambda t, m: (0,) * a.ndim)
    blocks = width // (2 * LANES)
    flat = pl.BlockSpec((rows, width), lambda t, m: (0, 0))
    return pl.pallas_call(
        functools.partial(qkv_kernel, zs, head, clip),
        out_shape=[shaped((2, 3, rows, lanes), BF16)] * zs + [shaped((rows, width), BF16)] * 2,
        grid_spec=pltpu.PrefetchScalarGridSpec(
            num_scalar_prefetch=1,
            grid=(1,),
            in_specs=[
                pl.BlockSpec((1, 1, rows, width), lambda t, m: (clip, 0, 0, 0)),
                pl.BlockSpec((1, 1, rows, width), lambda t, m: (clip, 0, 0, 0)),
                whole(mod),
                whole(cosine),
                whole(sine),
            ]
            + half_specs(width, width, 2 * zs, aligned)
            + half_specs(1, width, 2 * zs, aligned),
            out_specs=[pl.BlockSpec((2, 3, rows, lanes), lambda t, m: (0, 0, 0, 0))] * zs
            + [flat, flat],
            scratch_shapes=[
                pltpu.VMEM((2 * rows, width), BF16),
                pltpu.VMEM((zs, 2, 3, rows, lanes), BF16),
            ],
        ),
        compiler_params=params(48),
        cost_estimate=cost(6 * rows * width * width, 3 * width * width + 16 * rows * width),
        name="norm_qkv",
    )(meta, tokens, other_tokens, mod, cosine, sine, *[weight] * (3 * blocks), *[bias] * (3 * blocks))


def attend_kernel(slots, head, meta, *refs):
    zs = slots // 2
    parts, outs = refs[:zs], refs[zs:slots]
    exact, logs, held, scores, values, sems = refs[slots:]
    copies = [
        pltpu.make_async_copy(parts[k], held.at[pl.ds(2 * k, 2)], sems.at[k]) for k in range(zs)
    ]
    for copy in copies:
        copy.start()
    for copy in copies:
        copy.wait()
    me, context = meta[0], meta[1]
    rows, width = held.shape[2], held.shape[3]
    pairs = width // head

    def prepare(frame, _):
        split = split_heads(held[frame ^ me, 2], pairs, head)
        ones = split_heads(jnp.ones((rows, width), BF16), pairs, head)
        for h in range(pairs):
            values[frame, h] = jnp.concatenate([split[h], ones[h]], axis=1)
        return 0

    lax.fori_loop(0, slots, prepare, 0)

    def attend(slot, count):
        queries = split_heads(held[slot, 0], pairs, head)
        total, tops = None, []
        for h in range(pairs):
            peak = None
            for frame in range(count):
                score = dot_nt(queries[h], held[frame ^ me, 1])
                scores[frame, h * rows : (h + 1) * rows] = score
                for at in range(0, rows, LANES):
                    piece = score[:, at : at + LANES]
                    peak = piece if peak is None else jnp.maximum(peak, piece)
            top = jnp.max(peak, axis=1, keepdims=True)
            tops.append(top)
            for frame in range(count):
                power = jnp.exp(scores[frame, h * rows : (h + 1) * rows] - top).astype(BF16)
                term = dot_nn(power, values[frame, h])
                total = term if total is None else total + term
        weight_sum = total[:, width:]
        result = total[:, :width] / weight_sum
        exact[slot] = result
        top = jnp.broadcast_to(tops[0], (rows, width))
        if pairs > 1:
            lane = lax.broadcasted_iota(jnp.int32, (rows, width), 1)
            for h in range(1, pairs):
                top = jnp.where(lane // head >= h, tops[h], top)
        turned = (top + jnp.log(weight_sum)).T
        logs[slot] = jnp.concatenate(
            [turned[h * head : h * head + 1] for h in range(pairs)], axis=1
        )

    def one_frame(frame, _):
        count = jnp.maximum(frame, context - 1) + 1
        for known in range(1, slots + 1):

            @pl.when(count == known)
            def _():
                attend(frame ^ me, known)

        return 0

    lax.fori_loop(0, slots, one_frame, 0)
    for slot in range(slots):
        outs[slot // 2][slot % 2] = exact[slot].astype(BF16)


def attend_call(meta, parts, head):
    zs = len(parts)
    slots = 2 * zs
    rows, width = parts[0].shape[-2:]
    pairs = width // head
    work = slots * slots * rows * rows
    return pl.pallas_call(
        functools.partial(attend_kernel, slots, head),
        out_shape=[shaped((2, rows, width), BF16)] * zs
        + [shaped((slots, rows, width), F32), shaped((slots, 1, pairs * rows), F32)],
        in_specs=[SMEM] + [ANY] * zs,
        out_specs=[VMEM] * (zs + 2),
        scratch_shapes=[
            pltpu.VMEM((slots, 3, rows, width), BF16),
            pltpu.VMEM((slots, pairs * rows, rows), F32),
            pltpu.VMEM((slots, pairs, rows, 2 * width), BF16),
            pltpu.SemaphoreType.DMA((zs,)),
        ],
        compiler_params=params(40),
        cost_estimate=cost(work * 16 * width, slots * rows * width * 12, work * pairs),
        name="attend",
    )(meta, *parts)


def attend_grad_kernel(slots, head, meta, *refs):
    zs = slots // 2
    parts, grads = refs[:zs], refs[zs:slots]
    exact, logs = refs[slots], refs[slots + 1]
    outs = refs[slots + 2 : slots + 2 + zs]
    held, grad, query_rows, grad_rows, delta, grad_q, grad_k, grad_v, sems, more = refs[
        slots + 2 + zs :
    ]
    copies = []
    for k in range(zs):
        pair = pl.ds(2 * k, 2)
        copies.append(pltpu.make_async_copy(parts[k], held.at[pair], sems.at[k]))
        copies.append(pltpu.make_async_copy(grads[k], grad.at[pair], more.at[k]))
    for copy in copies:
        copy.start()
    for copy in copies:
        copy.wait()
    me, context = meta[0], meta[1]
    rows, width = held.shape[2], held.shape[3]
    pairs = width // head

    def prepare(slot, _):
        query_rows[slot] = jnp.concatenate(split_heads(held[slot, 0], pairs, head), axis=0)
        grad_rows[slot] = jnp.concatenate(split_heads(grad[slot], pairs, head), axis=0)
        product = (grad[slot].astype(F32) * exact[slot]).T
        delta[slot] = jnp.concatenate(
            [
                jnp.sum(product[h * head : (h + 1) * head], axis=0, keepdims=True)
                for h in range(pairs)
            ],
            axis=1,
        )
        grad_q[slot] = jnp.zeros((rows, width), F32)
        return 0

    lax.fori_loop(0, slots, prepare, 0)

    def key_frame(frame, _):
        place = frame ^ me
        keys, values = held[place, 1], held[place, 2]
        head_keys = split_heads(keys, pairs, head)
        grad_k[...] = jnp.zeros_like(grad_k)
        grad_v[...] = jnp.zeros_like(grad_v)

        def query_frame(query, _):
            slot = query ^ me
            score = dot_nt(keys, query_rows[slot])
            grad_weight = dot_nt(values, grad_rows[slot])
            weight = jnp.exp(score - logs[slot])
            grad_score = (weight * (grad_weight - delta[slot])).astype(BF16)
            grad_v[...] += dot_nn(weight.astype(BF16), grad_rows[slot])
            grad_k[...] += dot_nn(grad_score, query_rows[slot])
            total = grad_q[slot]
            for h in range(pairs):
                total = total + dot_tn(grad_score[:, h * rows : (h + 1) * rows], head_keys[h])
            grad_q[slot] = total
            return 0

        lax.fori_loop(jnp.where(frame < context, 0, frame), slots, query_frame, 0)
        held[place, 1] = grad_k[...].astype(BF16)
        held[place, 2] = grad_v[...].astype(BF16)
        return 0

    lax.fori_loop(0, slots, key_frame, 0)
    for slot in range(slots):
        out, role = outs[slot // 2], slot % 2
        out[role, 0] = (grad_q[slot] * head**-0.5).astype(BF16)
        out[role, 1] = held[slot, 1]
        out[role, 2] = held[slot, 2]


def attend_grad_call(meta, parts, grads, exact, logs, head):
    zs = len(parts)
    slots = 2 * zs
    rows, width = parts[0].shape[-2:]
    pairs = width // head
    work = slots * slots * rows * rows
    return pl.pallas_call(
        functools.partial(attend_grad_kernel, slots, head),
        out_shape=[shaped((2, 3, rows, width), BF16)] * zs,
        in_specs=[SMEM] + [ANY] * slots + [VMEM, VMEM],
        out_specs=[VMEM] * zs,
        scratch_shapes=[
            pltpu.VMEM((slots, 3, rows, width), BF16),
            pltpu.VMEM((slots, rows, width), BF16),
            pltpu.VMEM((slots, pairs * rows, width), BF16),
            pltpu.VMEM((slots, pairs * rows, width), BF16),
            pltpu.VMEM((slots, 1, pairs * rows), F32),
            pltpu.VMEM((slots, rows, width), F32),
            pltpu.VMEM((rows, width), F32),
            pltpu.VMEM((rows, width), F32),
            pltpu.SemaphoreType.DMA((zs,)),
            pltpu.SemaphoreType.DMA((zs,)),
        ],
        compiler_params=params(40),
        cost_estimate=cost(work * 40 * width, slots * rows * width * 20, work * pairs),
        name="attend_grad",
    )(meta, *parts, *grads, exact, logs)


def forward_back_kernel(slots, clip, meta, tokens, cotangent, mod, proj_b, up_b, down_b, *refs):
    zs = slots // 2
    parts, swapped, (proj_hbm, up_hbm, down_hbm) = refs[:zs], refs[zs], refs[zs + 1 : zs + 4]
    (
        layer_out, grad_middle_out, row_grads, up_bgrad,
        att_own, att_far, gone_low,
        n2_own, n2_other, hid_low,
        act_own, act_other, gtwo_low,
        held, far, proj, up, down, slope, active, sems,
    ) = refs[zs + 4 :]
    proj_copy = pltpu.make_async_copy(proj_hbm, proj, sems.at[0])
    up_copy = pltpu.make_async_copy(up_hbm, up, sems.at[1])
    down_copy = pltpu.make_async_copy(down_hbm, down, sems.at[2])
    proj_copy.start()
    up_copy.start()
    down_copy.start()
    me = meta[0]
    parity = me % 2
    rows, width = tokens.shape[-2:]
    lanes = width // slots
    hidden_width = up.shape[1]
    gate_one, shift_two, scale_two, gate_two = (mod[clip, k : k + 1] for k in (2, 3, 4, 5))
    for k in range(zs):
        held[(2 * k) ^ me] = parts[k][0]
        held[(2 * k + 1) ^ me] = swapped[k]
        far[k ^ (me // 2)] = parts[k][1]
    attended = jnp.concatenate([held[k] for k in range(slots)], axis=1)
    att_own[...] = jnp.concatenate([held[2 * k + parity] for k in range(zs)], axis=1)
    att_far[...] = jnp.concatenate([far[k] for k in range(zs)], axis=1)
    proj_copy.wait()
    branch_one = dot_nn(attended, proj[...]) + proj_b[...].astype(F32)
    middle = tokens[...].reshape(rows, width).astype(F32) + gate_one * branch_one
    hat_two, inverse_two = norm_parts(middle)
    low_two = (hat_two * (1.0 + scale_two) + shift_two).astype(BF16)
    for block in range(slots):
        store_by_parity(
            n2_own, n2_other, slice(block // 2 * lanes, (block // 2 + 1) * lanes), parity, block,
            low_two[:, block * lanes : (block + 1) * lanes],
        )
    up_copy.wait()
    chunk = hidden_width // slots
    for block in range(hidden_width // FF_BLOCK):
        at = slice(block * FF_BLOCK, (block + 1) * FF_BLOCK)
        hidden = dot_nn(low_two, up[:, at]) + up_b[:, at].astype(F32)
        square = hidden * hidden
        bent = jnp.tanh(GELU_A * (hidden + GELU_B * square * hidden))
        half = 0.5 * (1.0 + bent)
        low = (hidden * half).astype(BF16)
        slope[:, at] = half + (0.5 * GELU_A) * hidden * (1.0 - bent * bent) * (
            1.0 + (3.0 * GELU_B) * square
        )
        active[:, at] = low
        for piece in range(FF_BLOCK // chunk):
            index = block * (FF_BLOCK // chunk) + piece
            store_by_parity(
                act_own, act_other, slice(index // 2 * chunk, (index // 2 + 1) * chunk), parity,
                index, low[:, piece * chunk : (piece + 1) * chunk],
            )
    down_copy.wait()
    branch_two = dot_nn(active[...], down[...]) + down_b[...].astype(F32)
    layer_out[...] = (middle + gate_two * branch_two).astype(BF16)
    grad_out = cotangent[...].reshape(rows, width).astype(F32)
    low_grad_two = (grad_out * gate_two).astype(BF16)
    gtwo_low[...] = low_grad_two
    row_grads[3:4] = jnp.sum(grad_out * branch_two, axis=0, keepdims=True)
    row_grads[4:5] = jnp.sum(low_grad_two.astype(F32), axis=0, keepdims=True)
    grad_normed = None
    for block in range(hidden_width // FF_BLOCK):
        at = slice(block * FF_BLOCK, (block + 1) * FF_BLOCK)
        low = (dot_nt(low_grad_two, down[at, :]) * slope[:, at]).astype(BF16)
        hid_low[:, at] = low
        up_bgrad[:, at] = jnp.sum(low.astype(F32), axis=0, keepdims=True)
        term = dot_nt(low, up[:, at])
        grad_normed = term if grad_normed is None else grad_normed + term
    grad_middle, grad_shift, grad_scale = norm_pull(grad_normed, hat_two, inverse_two, scale_two)
    grad_middle = grad_middle + grad_out
    grad_middle_out[...] = grad_middle
    low_grad_one = (grad_middle * gate_one).astype(BF16)
    gone_low[...] = low_grad_one
    row_grads[0:1] = jnp.sum(grad_middle * branch_one, axis=0, keepdims=True)
    row_grads[1:2] = grad_shift
    row_grads[2:3] = grad_scale
    row_grads[5:6] = jnp.sum(low_grad_one.astype(F32), axis=0, keepdims=True)
    row_grads[6:8] = jnp.zeros((2, width), F32)


def forward_back_call(
    meta, clip, tokens, cotangent, mod, proj_b, up_b, down_b, parts, swapped, proj, up, down
):
    zs = len(parts)
    slots = 2 * zs
    rows, width = tokens.shape[-2:]
    lanes = width // slots
    hidden = up.shape[1]
    half, half_hidden = width // 2, hidden // 2
    out_shape = [
        shaped((rows, width), BF16),
        shaped((rows, width), F32),
        shaped((8, width), F32),
        shaped((1, hidden), F32),
        shaped((rows, half), BF16),
        shaped((rows, half), BF16),
        shaped((rows, width), BF16),
        shaped((rows, half), BF16),
        shaped((rows, half), BF16),
        shaped((rows, hidden), BF16),
        shaped((rows, half_hidden), BF16),
        shaped((rows, half_hidden), BF16),
        shaped((rows, width), BF16),
    ]
    full = lambda shape: pl.BlockSpec(shape, lambda t: (0,) * len(shape))
    pick = pl.BlockSpec((1, 1, rows, width), lambda t: (clip, 0, 0, 0))
    return pl.pallas_call(
        functools.partial(forward_back_kernel, slots, clip),
        grid=(1,),
        out_shape=out_shape,
        in_specs=[SMEM, pick, pick]
        + [full(a.shape) for a in (mod, proj_b, up_b, down_b, *parts, swapped)]
        + [ANY] * 3,
        out_specs=[full(o.shape) for o in out_shape],
        scratch_shapes=[
            pltpu.VMEM((slots, rows, lanes), BF16),
            pltpu.VMEM((zs, rows, lanes), BF16),
            pltpu.VMEM(proj.shape, BF16),
            pltpu.VMEM(up.shape, BF16),
            pltpu.VMEM(down.shape, BF16),
            pltpu.VMEM((rows, hidden), F32),
            pltpu.VMEM((rows, hidden), BF16),
            pltpu.SemaphoreType.DMA((3,)),
        ],
        compiler_params=params(60),
        cost_estimate=cost(
            4 * rows * width * (width + 2 * hidden),
            4 * width * (width + 2 * hidden),
            rows * hidden,
        ),
        name="feed_forward",
    )(meta, tokens, cotangent, mod, proj_b, up_b, down_b, *parts, swapped, proj, up, down)


def proj_back_kernel(meta, near, far, proj, *outs):
    me = meta[0]
    rows, lanes = near.shape[0], outs[0].shape[2]
    for k, out in enumerate(outs):
        group = me ^ (2 * k)
        weight = proj[pl.ds(pl.multiple_of(group * lanes, lanes), lanes), :]
        out[0] = dot_nt(near[...], weight).astype(BF16)
        out[1] = dot_nt(far[...], weight).astype(BF16)


def proj_back_call(meta, near, far, proj, zs):
    rows, width = near.shape
    lanes = width // (2 * zs)
    return pl.pallas_call(
        proj_back_kernel,
        out_shape=[shaped((2, rows, lanes), BF16)] * zs,
        in_specs=[SMEM, VMEM, VMEM, VMEM],
        out_specs=[VMEM] * zs,
        compiler_params=params(32),
        cost_estimate=cost(2 * rows * width * width, 2 * width * width + 6 * rows * width),
        name="proj_back",
    )(meta, near, far, proj)


def qkv_grad_kernel(zs, head, clip, meta, cosine, sine, *refs):
    blocks = refs[zs].shape[0] // (2 * LANES)
    parts, weights = refs[:zs], refs[zs : zs + 3 * blocks]
    near_out, far_out, near_sum, far_sum, bias_out, held = refs[zs + 3 * blocks :]
    rows, width = near_sum.shape
    clips = cosine.shape[0] // 2
    z = meta[0] // 2
    for k in range(zs):
        held[k ^ z] = parts[k][...]
    totals = [None, None]
    bias_out[...] = jnp.zeros_like(bias_out)
    half = width // 2
    for kind in range(3):
        weight = jnp.concatenate([w[...] for w in weights[kind * blocks : (kind + 1) * blocks]], axis=1)
        sums = None
        for role, out in enumerate((near_out, far_out)):
            low = jnp.concatenate([held[k, role, kind] for k in range(zs)], axis=1)
            if kind < 2:
                row = role * clips + clip
                low = turn(low.astype(F32), cosine[row], sine[row], head, True).astype(BF16)
            out[:, kind * half : (kind + 1) * half] = low
            column = jnp.sum(low.astype(F32), axis=0, keepdims=True)
            sums = column if sums is None else sums + column
            term = dot_nt(low, weight)
            totals[role] = term if totals[role] is None else totals[role] + term
        bias_out[kind : kind + 1] = sums
    near_sum[...] = totals[0]
    far_sum[...] = totals[1]


def qkv_grad_call(meta, clip, cosine, sine, parts, weight, head, aligned):
    zs = len(parts)
    rows, lanes = parts[0].shape[-2:]
    width = 2 * zs * lanes
    blocks = width // (2 * LANES)
    whole = lambda shape: pl.BlockSpec(shape, lambda t, m: (0,) * len(shape))
    out_shape = [
        shaped((rows, 3 * width // 2), BF16),
        shaped((rows, 3 * width // 2), BF16),
        shaped((rows, width), F32),
        shaped((rows, width), F32),
        shaped((8, width // 2), F32),
    ]
    return pl.pallas_call(
        functools.partial(qkv_grad_kernel, zs, head, clip),
        out_shape=out_shape,
        grid_spec=pltpu.PrefetchScalarGridSpec(
            num_scalar_prefetch=1,
            grid=(1,),
            in_specs=[whole(a.shape) for a in (cosine, sine, *parts)]
            + half_specs(width, width, 2 * zs, aligned),
            out_specs=[whole(o.shape) for o in out_shape],
            scratch_shapes=[pltpu.VMEM((zs, 2, 3, rows, lanes), BF16)],
        ),
        compiler_params=params(48),
        cost_estimate=cost(6 * rows * width * width, 3 * width * width + 20 * rows * width),
        name="qkv_grad",
    )(meta, cosine, sine, *parts, *[weight] * (3 * blocks))


def norm_grad_kernel(tokens, mod, *refs):
    clips = tokens.shape[0]
    nears, fars, middles = refs[:clips], refs[clips : 2 * clips], refs[2 * clips : 3 * clips]
    tokens_grad, row_grads = refs[3 * clips :]
    for c in range(clips):
        hat, inverse = norm_parts(tokens[c, 0].astype(F32))
        grad, shift, scale = norm_pull(nears[c][...] + fars[c][...], hat, inverse, mod[c, 1:2])
        tokens_grad[c, 0] = grad + middles[c][...]
        row_grads[c, 0:1] = shift
        row_grads[c, 1:2] = scale
        row_grads[c, 2:8] = jnp.zeros((6, tokens.shape[-1]), F32)


def norm_grad_call(tokens, mod, nears, fars, middles):
    clips, _, rows, width = tokens.shape
    return pl.pallas_call(
        norm_grad_kernel,
        out_shape=[shaped(tokens.shape, F32), shaped((clips, 8, width), F32)],
        in_specs=[VMEM] * (2 + 3 * clips),
        out_specs=[VMEM, VMEM],
        compiler_params=params(40),
        cost_estimate=cost(clips * rows * width * 30, clips * rows * width * 18),
        name="norm_grad",
    )(tokens, mod, *nears, *fars, *middles)


def weight_grad_kernel(jobs, clip_size, zs, meta, *refs):
    count = sum(job[0] * (1 + job[1]) for job in jobs)
    outs = refs[count : count + 4]
    held, sems = refs[count + 4], refs[count + 5]
    turned_refs = refs[count + 6 :]
    step = pl.program_id(0) * pl.num_programs(1) + pl.program_id(1)
    last = pl.num_programs(0) * pl.num_programs(1) - 1
    slot = step % 2
    _, _, height, cols = held.shape
    tile = zs * height
    z = meta[0] // 2

    def drain(which):
        pltpu.make_async_copy(held.at[which], held.at[which], sems.at[which]).wait()

    def send_out(e, tiles, repeat, first, tall):
        for half, first_bit in enumerate((1, clip_size // 2)):
            keep, send = outs[2 * half], outs[2 * half + 1]
            rest = [k for k in range(clip_size) if not k & first_bit]
            out, place = (send, rest.index(e ^ first_bit)) if e & first_bit else (keep, rest.index(e))
            low, high = half * zs // 2, (half + 1) * zs // 2
            if not tall:
                pltpu.make_async_copy(
                    held.at[slot, pl.ds(low, zs // 2)],
                    out.at[place, :, pl.ds(first, height)],
                    sems.at[slot],
                ).start()
            else:
                for block in range(zs):
                    row = repeat * zs + block
                    k = row // tiles
                    if low <= k < high:
                        pltpu.make_async_copy(
                            held.at[slot, block],
                            out.at[place, k - low, pl.ds(first + row % tiles * height, height)],
                            sems.at[slot],
                        ).start()

    @pl.when(step >= 2)
    def _():
        drain(slot)

    at = index = 0
    for job, (lefts_n, lane_parts, tall, tiles, first) in enumerate(jobs):
        lefts = refs[at : at + lefts_n]
        rights = refs[at + lefts_n : at + lefts_n * (1 + lane_parts)]
        at += lefts_n * (1 + lane_parts)
        turned = turned_refs[job]
        total_rows = lefts[0].shape[1]
        depth = lefts[0].shape[0]
        block = total_rows // zs

        @pl.when(step == index)
        def _():
            for k in range(zs):
                place = pl.ds(pl.multiple_of((k ^ z) * block, block), block)
                for n, left in enumerate(lefts):
                    turned[place, n * depth : (n + 1) * depth] = left[
                        :, k * block : (k + 1) * block
                    ].T

        for repeat in range(tiles):

            @pl.when(pl.program_id(1) == index)
            def _():
                picked = turned[repeat * tile : (repeat + 1) * tile, :] if tall else turned[...]
                right = jnp.concatenate(
                    [
                        jnp.concatenate([rights[n * lane_parts + p][...] for p in range(lane_parts)], axis=1)
                        for n in range(lefts_n)
                    ],
                    axis=0,
                )
                held[slot] = dot_nn(picked, right).astype(BF16).reshape(held.shape[1:])
                offset = first if tall else first + repeat * height
                for e in range(clip_size):

                    @pl.when(pl.program_id(0) == e)
                    def _():
                        send_out(e, tiles, repeat, offset, tall)

            index += 1

    @pl.when(step == last)
    def _():
        drain(1 - slot)
        drain(slot)


def weight_grad_call(meta, products, clip_size, zs, name):
    jobs, specs, arrays, turned = [], [], [], []
    first = index = flops = 0
    tile = min(p[0][0].shape[1] for p in products)
    height = tile // zs
    piece = None
    for lefts, rights, lane_parts, tall in products:
        total = rights[0].shape[1]
        if tall:
            tiles, block = lefts[0].shape[1] // tile, total // clip_size
        elif lane_parts > 1:
            tiles, block = 1, total // (lane_parts * clip_size)
        else:
            tiles, block = total // (2 * tile), 2 * tile // clip_size
        piece = lane_parts * block
        jobs.append((len(lefts), lane_parts, tall, tiles, first))
        first += height * tiles
        for left in lefts:
            arrays.append(left)
            specs.append(pl.BlockSpec(left.shape, lambda e, t, m: (0, 0)))
            flops += 2 * left.shape[0] * left.shape[1] * total
        for right in rights:
            for part in range(lane_parts):
                arrays.append(right)

                def place(e, t, m, start=index, tiles=tiles, tall=tall, part=part):
                    group = part if tall or tiles == 1 else jnp.clip(t - start, 0, tiles - 1)
                    return (0, group * clip_size + (e ^ m[2]))

                specs.append(pl.BlockSpec((right.shape[0], block), place))
        turned.append(
            pltpu.VMEM((lefts[0].shape[1], len(lefts) * lefts[0].shape[0]), BF16)
        )
        index += tiles
    out = shaped((clip_size // 2, zs // 2, first, piece), BF16)
    return pl.pallas_call(
        functools.partial(weight_grad_kernel, tuple(jobs), clip_size, zs),
        out_shape=[out] * 4,
        grid_spec=pltpu.PrefetchScalarGridSpec(
            num_scalar_prefetch=1,
            grid=(clip_size, index),
            in_specs=specs,
            out_specs=[ANY] * 4,
            scratch_shapes=[
                pltpu.VMEM((2, zs, height, piece), BF16),
                pltpu.SemaphoreType.DMA((2,)),
            ]
            + turned,
        ),
        compiler_params=params(56),
        cost_estimate=cost(flops, sum(a.size * 2 for a in arrays) + 8 * out.size),
        name=name,
    )(meta, *arrays)


def place_kernel(jobs, pieces, meta, *refs):
    parts, outs = refs[:pieces], refs[pieces:]
    clip = meta[2]
    cols = parts[0].shape[1]
    for e in range(pieces):
        first = 0
        for out, (height, repeats, tall) in zip(outs, jobs):
            for repeat in range(repeats):
                base = 0 if tall else repeat * cols * pieces
                target = pl.ds(pl.multiple_of(base + (clip ^ e) * cols, cols), cols)
                value = parts[e][first : first + height].astype(F32)
                if tall:
                    out[repeat * height : (repeat + 1) * height, target] = value
                else:
                    out[:, target] = value
                first += height


def place_call(meta, parts, jobs, outs):
    return pl.pallas_call(
        functools.partial(place_kernel, jobs, len(parts)),
        out_shape=outs,
        in_specs=[SMEM] + [VMEM] * len(parts),
        out_specs=[VMEM] * len(outs),
        compiler_params=params(32),
        cost_estimate=cost(0, sum(o.size * 4 for o in outs)),
        name="place_grads",
    )(meta, *parts)


def place_qkv_kernel(meta, *refs):
    parts, out = refs[:-1], refs[-1]
    parity, clip = meta[0] % 2, meta[2]
    thirds = out.shape[1] // 3
    for e, part in enumerate(parts):
        for role in range(2):
            block = 2 * (clip ^ e) + (parity ^ role)
            for kind in range(3):
                at = pl.ds(pl.multiple_of(kind * thirds + block * LANES, LANES), LANES)
                out[:, at] = part[role, :, kind * LANES : (kind + 1) * LANES].astype(F32)


def place_qkv_call(meta, parts, out):
    return pl.pallas_call(
        place_qkv_kernel,
        out_shape=out,
        in_specs=[SMEM] + [VMEM] * len(parts),
        out_specs=VMEM,
        compiler_params=params(32),
        cost_estimate=cost(0, out.size * 6),
        name="place_qkv_grad",
    )(meta, *parts)


def exchange(array, axis, size, distance):
    return lax.ppermute(array, axis, [(k, k ^ distance) for k in range(size)])


def after(value, *others):
    return lax.optimization_barrier((value, *others))


def spread(slots_out, seq_size):
    return [slots_out[0]] + [
        exchange(slots_out[k], "seq", seq_size, 2 * k) for k in range(1, seq_size // 2)
    ]


def add_low(left, right):
    return (left.astype(F32) + right.astype(F32)).astype(BF16)


def halve(pair, bit, size):
    keep, send = pair
    arrived = exchange(send, "clip", size, bit)
    half = keep.shape[0] // 2
    if half == 0:
        return add_low(keep[0], arrived[0]), None
    return add_low(keep[:half], arrived[:half]), add_low(keep[half:], arrived[half:])


def clip_orders(clip_size):
    down = [1 << k for k in reversed(range(clip_size.bit_length() - 1))]
    return [1] + down[:-1], down


def sum_z(near, far, seq_size):
    zs = seq_size // 2
    half = zs // 2
    total = near[0].astype(F32)
    for k in range(1, zs):
        source = near[k] if k < half else far[k - half]
        total = total + exchange(source, "seq", seq_size, 2 * k).astype(F32)
    return total.astype(BF16)


def gather_pieces(piece, clip_size):
    return [piece] + [exchange(piece, "clip", clip_size, d) for d in range(1, clip_size)]


def gather_all(rows, clip_size, seq_size):
    both = jnp.stack([rows, exchange(rows, "seq", seq_size, 1)])
    by_seq = jnp.concatenate(
        [both] + [exchange(both, "seq", seq_size, 2 * k) for k in range(1, seq_size // 2)]
    )
    return jnp.concatenate(
        [by_seq] + [exchange(by_seq, "clip", clip_size, d) for d in range(1, clip_size)]
    )


def silu_act(values_in):
    return values_in * jax.nn.sigmoid(values_in)


def rotary_tables(stamps, patch_count, head):
    lane = jnp.arange(LANES, dtype=jnp.int32)
    quarter = head // 4
    pair = lane % (head // 2)
    freqs = 10000.0 ** (-(pair % quarter).astype(F32) / quarter)
    temporal = stamps.astype(F32)[:, None, None] * freqs[None, None, :]
    spatial = jnp.arange(patch_count).astype(F32)[None, :, None] * freqs[None, None, :]
    angles = jnp.where((pair < quarter)[None, None, :], temporal, spatial)
    sign = jnp.where(lane % head < head // 2, -1.0, 1.0).astype(F32)
    return jnp.cos(angles), jnp.sin(angles) * sign[None, None, :]


def on_device(
    tokens,
    cotangent,
    context_count,
    noise_level,
    frame_time,
    level_table,
    mod_weight,
    mod_bias,
    qkv_weight,
    qkv_bias,
    proj_weight,
    proj_bias,
    up_weight,
    up_bias,
    down_weight,
    down_bias,
):
    seq_size, clip_size = lax.axis_size("seq"), lax.axis_size("clip")
    me, mine = lax.axis_index("seq"), lax.axis_index("clip")
    clips, _, rows, width = tokens.shape
    head = width // HEADS
    hidden = up_weight.shape[1]
    zs = seq_size // 2
    me = me.astype(jnp.int32)
    mine = mine.astype(jnp.int32)
    parity = me % 2
    aligned = (width // seq_size) % LANES == 0
    metas = [jnp.stack([me, context_count[c], mine]) for c in range(clips)]
    stamps = jnp.stack([noise_level[:, 0], frame_time[:, 0]])
    other_stamps = exchange(stamps, "seq", seq_size, 1)
    other_tokens = exchange(tokens, "seq", seq_size, 1)
    both_levels = jnp.concatenate(
        [
            jnp.where(me < context_count, 0, stamps[0]),
            jnp.where((me ^ 1) < context_count, 0, other_stamps[0]),
        ]
    )
    levels_used = both_levels[:clips]
    picked = (
        both_levels[:, None] == jnp.arange(level_table.shape[0], dtype=jnp.int32)[None, :]
    ).astype(BF16)
    condition = jnp.dot(picked, level_table, preferred_element_type=F32)
    condition_low = silu_act(condition).astype(BF16)
    modulation = jnp.dot(
        condition_low, mod_weight, preferred_element_type=F32
    ) + mod_bias.astype(F32)
    mods = modulation.reshape(2 * clips, 6, width)
    cosine, sine = rotary_tables(jnp.concatenate([stamps[1], other_stamps[1]]), rows, head)
    qkv_bias_row = qkv_bias[None]
    if aligned:
        weight_half, bias_half = qkv_weight, qkv_bias_row
    else:
        weight_half = half_columns(qkv_weight, seq_size, parity)
        bias_half = half_columns(qkv_bias_row, seq_size, parity)

    parts, normed = [], []
    for c in range(clips):
        out = qkv_call(
            metas[c], c, tokens, other_tokens, mods, cosine, sine, weight_half, bias_half, zs,
            head, aligned,
        )
        parts.append(spread(out[:zs], seq_size))
        normed.append(out[zs:])
    attended, swapped, exact, logs = [], [], [], []
    for c in range(clips):
        out = attend_call(metas[c], parts[c], head)
        attended.append(spread(out[:zs], seq_size))
        crossing = jnp.stack([a[1] for a in attended[c]])
        swapped.append(exchange(crossing, "seq", seq_size, 1))
        exact.append(out[zs])
        logs.append(out[zs + 1])
    swap = lambda array: exchange(array, "seq", seq_size, 1)
    layer, middles, row_grads, up_bgrads, saved, grads, far_ones = [], [], [], [], [], [], []
    for c in range(clips):
        out = forward_back_call(
            metas[c], c, tokens, cotangent, mods, proj_bias[None], up_bias[None],
            down_bias[None], attended[c], swapped[c], proj_weight, up_weight, down_weight,
        )
        layer.append(out[0])
        middles.append(out[1])
        row_grads.append(out[2])
        up_bgrads.append(out[3])
        saved.append(out[4:13])
        far_ones.append(swap(out[6]))
        grads.append(spread(proj_back_call(metas[c], out[6], far_ones[c], proj_weight, zs), seq_size))
    products = [([], [], 1, False), ([], [], 1, True), ([], [], 1, False)]
    for c in range(clips):
        att_own, att_far, gone, n2_own, n2_other, hid, act_own, act_other, gtwo = saved[c]
        products[0][0].extend([n2_own, swap(n2_other)])
        products[0][1].extend([hid, swap(hid)])
        products[1][0].extend([act_own, swap(act_other)])
        products[1][1].extend([gtwo, swap(gtwo)])
        products[2][0].extend([att_own, att_far])
        products[2][1].extend([gone, far_ones[c]])
    shares = weight_grad_call(metas[0], products, clip_size, zs, "weight_grads")
    row = width // seq_size
    orders = clip_orders(clip_size)
    steps = len(orders[0])
    near, far = shares[:2], shares[2:]

    metas[0], near, far = after(metas[0], near, far)
    metas[1], near, far = after(metas[1], near, far)
    grad_rights, nears, fars, qkv_bgrads = [], [], [], []
    for c in range(clips):
        out = attend_grad_call(metas[c], parts[c], grads[c], exact[c], logs[c], head)
        if c < steps:
            near = halve(near, orders[0][c], clip_size)
            far = halve(far, orders[1][c], clip_size)
        metas[c], near, far = after(metas[c], near, far)
        out = qkv_grad_call(
            metas[c], c, cosine, sine, spread(out, seq_size), weight_half, head, aligned
        )
        grad_rights.extend(out[:2])
        nears.append(out[2])
        fars.append(swap(out[3]))
        qkv_bgrads.append(out[4][:3])
    tokens_grad, late_rows = norm_grad_call(tokens, mods, nears, fars, middles)
    for at in range(clips, steps):
        near = halve(near, orders[0][at], clip_size)
        far = halve(far, orders[1][at], clip_size)
    piece = sum_z(near[0], far[0], seq_size)
    up_wgrad, down_wgrad, proj_wgrad = place_call(
        metas[0],
        gather_pieces(piece, clip_size),
        (
            (row, hidden // width, False),
            (row, hidden // width, True),
            (row, 1, False),
        ),
        [shaped((row, hidden), F32), shaped((hidden // seq_size, width), F32), shaped((row, width), F32)],
    )
    lefts = [array for pair in normed for array in pair]
    if aligned:
        shares = weight_grad_call(
            metas[0], [(lefts, grad_rights, 3, False)], clip_size, zs, "qkv_weight_grad"
        )
        near, far = shares[:2], shares[2:]
        for at in range(steps):
            near = halve(near, orders[0][at], clip_size)
            far = halve(far, orders[1][at], clip_size)
        piece = sum_z(near[0], far[0], seq_size).reshape(2, row, 3 * LANES)
        own_rows = lax.dynamic_index_in_dim(piece, parity, 0, keepdims=False)
        far_rows = swap(lax.dynamic_index_in_dim(piece, 1 - parity, 0, keepdims=False))
        qkv_wgrad = place_qkv_call(
            metas[0],
            gather_pieces(jnp.stack([own_rows, far_rows]), clip_size),
            shaped((row, 3 * width), F32),
        )
    else:
        share = sum(
            lax.dot_general(left, right, (((0,), (0,)), ((), ())), preferred_element_type=F32)
            for left, right in zip(lefts, grad_rights)
        ).astype(BF16)
        share = share.reshape(width, 3, zs, 1, width // seq_size)
        blank = jnp.zeros_like(share)
        share = jnp.where(
            parity == 0,
            jnp.concatenate([share, blank], axis=3),
            jnp.concatenate([blank, share], axis=3),
        ).reshape(width, 3 * width)
        qkv_wgrad = lax.psum(
            lax.psum_scatter(share, "seq", scatter_dimension=0, tiled=True), "clip"
        ).astype(F32)

    level_rows = jnp.stack([levels_used // 32, levels_used % 32]).astype(F32)
    level_rows = jnp.concatenate([level_rows, jnp.zeros((2, width - clips), F32)], axis=1)
    mod_rows = []
    for c in range(clips):
        mod_rows += [late_rows[c, 0:2], row_grads[c][0:4]]
    bias_rows = [
        sum(qkv_bgrads).reshape(3 * width // 2),
        jnp.zeros((width // 2,), F32),
        sum(up_bgrads).reshape(hidden),
        sum(r[4] for r in row_grads),
        sum(r[5] for r in row_grads),
    ]
    bias_rows = jnp.concatenate(bias_rows).reshape(-1, width)
    late = jnp.concatenate([condition[:clips], level_rows] + mod_rows + [bias_rows], axis=0)
    used = late.shape[0]
    late = jnp.concatenate([late.astype(BF16), jnp.zeros((-used % 16, width), BF16)], axis=0)
    late = gather_all(late, clip_size, seq_size)
    devices = late.shape[0]
    start = clips + 2
    grad_modulation = late[:, start : start + 6 * clips].reshape(devices * clips, 6 * width)
    bias_all = late[:, start + 6 * clips : used].astype(F32).reshape(devices, -1)
    own_sums = jnp.sum(bias_all.reshape(devices // 2, 2, -1), axis=0)
    half_bias = own_sums[:, : 3 * width // 2].reshape(2, 3, zs, 1, width // seq_size)
    bias_sums = jnp.sum(own_sums, axis=0)[2 * width :]
    qkv_bias_sums = jnp.where(
        parity == 0,
        jnp.concatenate([half_bias[0], half_bias[1]], axis=2),
        jnp.concatenate([half_bias[1], half_bias[0]], axis=2),
    ).reshape(3 * width)
    all_condition = late[:, :clips].reshape(devices * clips, width).astype(F32)
    codes = late[:, clips:start, :clips].astype(jnp.int32)
    all_levels = (codes[:, 0] * 32 + codes[:, 1]).reshape(devices * clips)
    all_active, silu_pull = jax.vjp(silu_act, all_condition)
    my_active = lax.dynamic_slice_in_dim(all_active, me * row, row, axis=1).astype(BF16)
    mod_wgrad = lax.dot_general(
        my_active, grad_modulation, (((0,), (0,)), ((), ())), preferred_element_type=F32
    )
    (grad_condition,) = silu_pull(
        lax.dot_general(
            grad_modulation, mod_weight, (((1,), (1,)), ((), ())), preferred_element_type=F32
        )
    )
    table_row = level_table.shape[0] // seq_size
    onehot = (
        all_levels[:, None] == (me * table_row + jnp.arange(table_row, dtype=jnp.int32))[None, :]
    ).astype(F32)
    table_grad = lax.dot_general(
        onehot,
        grad_condition,
        (((0,), (0,)), ((), ())),
        precision=HIGHEST_PRECISION,
        preferred_element_type=F32,
    )
    mod_sums = jnp.sum(grad_modulation.astype(F32), axis=0)

    def own_part(vector):
        size = vector.shape[0] // seq_size
        return lax.dynamic_slice_in_dim(vector, me * size, size, axis=0)

    mod_bgrad = own_part(mod_sums)
    qkv_bgrad = own_part(qkv_bias_sums)
    up_bgrad = own_part(bias_sums[:hidden])
    down_bgrad = own_part(bias_sums[hidden : hidden + width])
    proj_bgrad = own_part(bias_sums[hidden + width : hidden + 2 * width])
    layer_out = jnp.stack(layer)[:, None]
    return (
        layer_out,
        tokens_grad,
        table_grad,
        mod_wgrad,
        mod_bgrad,
        qkv_wgrad,
        qkv_bgrad,
        proj_wgrad,
        proj_bgrad,
        up_wgrad,
        up_bgrad,
        down_wgrad,
        down_bgrad,
    )


def solution(mesh):
    placed = (
        P("clip", "seq", None, None),
        P("clip", "seq", None, None),
        P("clip"),
        P("clip", "seq"),
        P("clip", "seq"),
    ) + (P(),) * 11
    return jax.shard_map(
        on_device,
        mesh=mesh,
        in_specs=placed,
        out_specs=(
            P("clip", "seq", None, None),
            P("clip", "seq", None, None),
            P("seq", None),
            P("seq", None),
            P("seq"),
            P("seq", None),
            P("seq"),
            P("seq", None),
            P("seq"),
            P("seq", None),
            P("seq"),
            P("seq", None),
            P("seq"),
        ),
        check_vma=False,
    )
```

```python
import functools

import jax
import jax.numpy as jnp
from jax import lax
from jax.experimental import pallas as pl
from jax.experimental.pallas import tpu as pltpu
from jax.sharding import PartitionSpec as P

HEADS = 16
EPS = 1e-06
HIGHEST_PRECISION = lax.Precision.HIGHEST
F32 = jnp.float32
BF16 = jnp.bfloat16
ANY = pl.BlockSpec(memory_space=pl.ANY)
VMEM = pl.BlockSpec(memory_space=pltpu.VMEM)
SMEM = pl.BlockSpec(memory_space=pltpu.SMEM)
LANES = 128
BLOCK = 256
FF_BLOCK = 1024
IN_FLIGHT = 3
GELU_A = 0.7978845608028654
GELU_B = 0.044715
WEIGHT = 1.0


def shaped(shape, dtype):
    return jax.ShapeDtypeStruct(shape, dtype)


def params(mib):
    return pltpu.CompilerParams(vmem_limit_bytes=mib << 20)


def cost(flops, moved, transcendentals=0):
    return pl.CostEstimate(
        flops=int(flops * WEIGHT),
        bytes_accessed=int(moved * WEIGHT),
        transcendentals=int(transcendentals * WEIGHT),
    )


def dot_nn(left, right):
    return lax.dot_general(left, right, (((1,), (0,)), ((), ())), preferred_element_type=F32)


def dot_nt(left, right):
    return lax.dot_general(left, right, (((1,), (1,)), ((), ())), preferred_element_type=F32)


def dot_tn(left, right):
    return lax.dot_general(left, right, (((0,), (0,)), ((), ())), preferred_element_type=F32)


def split_heads(values, pairs, head):
    if pairs == 1:
        return [values]
    lane = lax.broadcasted_iota(jnp.int32, values.shape, 1)
    return [jnp.where(lane // head == h, values, jnp.zeros_like(values)) for h in range(pairs)]


def swap_halves(values, head):
    half = head // 2
    lane = lax.broadcasted_iota(jnp.int32, values.shape, 1)
    ahead = pltpu.roll(values, values.shape[1] - half, 1)
    behind = pltpu.roll(values, half, 1)
    return jnp.where(lax.rem(lane, head) < half, ahead, behind)


def turn(values, cosine, signed_sine, head, back):
    parts = []
    for at in range(0, values.shape[1], LANES):
        piece = values[:, at : at + LANES]
        other = swap_halves(piece, head) * signed_sine
        parts.append(piece * cosine - other if back else piece * cosine + other)
    return jnp.concatenate(parts, axis=1)


def norm_parts(values):
    center = jnp.mean(values, axis=-1, keepdims=True)
    offset = values - center
    spread = jnp.mean(offset * offset, axis=-1, keepdims=True)
    inverse = lax.rsqrt(spread + EPS)
    return offset * inverse, inverse


def norm_pull(grad, hat, inverse, scale_row):
    grad_shift = jnp.sum(grad, axis=0, keepdims=True)
    grad_scale = jnp.sum(grad * hat, axis=0, keepdims=True)
    inner = grad * (1.0 + scale_row)
    mean_one = jnp.mean(inner, axis=-1, keepdims=True)
    mean_two = jnp.mean(inner * hat, axis=-1, keepdims=True)
    return inverse * (inner - mean_one - hat * mean_two), grad_shift, grad_scale


def store_by_parity(own_ref, other_ref, where, parity, block_index, value):
    own = parity == block_index % 2

    @pl.when(own)
    def _():
        own_ref[:, where] = value

    @pl.when(jnp.logical_not(own))
    def _():
        other_ref[:, where] = value


def half_columns(weight, groups, parity):
    rows, total = weight.shape
    view = weight.reshape(rows, 3, groups // 2, 2, total // (3 * groups))
    return lax.dynamic_index_in_dim(view, parity, 3, keepdims=False).reshape(rows, total // 2)


def half_specs(height, width, groups, aligned):
    specs = []
    for kind in range(3):
        for block in range(width // (2 * LANES)):
            if aligned:
                specs.append(
                    pl.BlockSpec(
                        (height, LANES), lambda t, m, k=kind, b=block: (0, k * groups + 2 * b + m[0] % 2)
                    )
                )
            else:
                specs.append(
                    pl.BlockSpec(
                        (height, LANES),
                        lambda t, m, k=kind, b=block: (0, k * (width // (2 * LANES)) + b),
                    )
                )
    return specs


def qkv_kernel(zs, head, meta, tokens, other_tokens, mod, cosine, sine, *refs):
    blocks = tokens.shape[-1] // (2 * LANES)
    weights, biases = refs[: 3 * blocks], refs[3 * blocks : 6 * blocks]
    outs = refs[6 * blocks : 6 * blocks + zs]
    normed_outs, (normed, held) = refs[6 * blocks + zs : -2], refs[-2:]
    clips, _, rows, width = tokens.shape
    lanes = width // (2 * zs)
    z = meta[0] // 2
    for row in range(2 * clips):
        role, clip = row // clips, row % clips
        source = (tokens, other_tokens)[role]
        hat, _ = norm_parts(source[clip, 0].astype(F32))
        low = (hat * (1.0 + mod[row, 1:2]) + mod[row, 0:1]).astype(BF16)
        normed[row * rows : (row + 1) * rows] = low
        normed_outs[row][...] = low
    for kind in range(3):
        pick = slice(kind * blocks, (kind + 1) * blocks)
        weight = jnp.concatenate([w[...] for w in weights[pick]], axis=1)
        bias = jnp.concatenate([b[...] for b in biases[pick]], axis=1).astype(F32)
        value = dot_nn(normed[...], weight) + bias
        for row in range(2 * clips):
            role, clip = row // clips, row % clips
            part = value[row * rows : (row + 1) * rows]
            if kind < 2:
                part = turn(part, cosine[row], sine[row], head, False)
            part = part.astype(BF16)
            if kind == 0:
                part = part * jnp.asarray(head**-0.5, BF16)
            for group in range(zs):
                held[group ^ z, clip, role, kind] = part[:, group * lanes : (group + 1) * lanes]
    for slot in range(zs):
        outs[slot][...] = held[slot]


def qkv_call(meta, tokens, other_tokens, mod, cosine, sine, weight, bias, zs, head, aligned):
    clips, _, rows, width = tokens.shape
    lanes = width // (2 * zs)
    whole = lambda shape: pl.BlockSpec(shape, lambda t, m: (0,) * len(shape))
    blocks = width // (2 * LANES)
    message = (clips, 2, 3, rows, lanes)
    out_shape = [shaped(message, BF16)] * zs + [shaped((rows, width), BF16)] * (2 * clips)
    return pl.pallas_call(
        functools.partial(qkv_kernel, zs, head),
        out_shape=out_shape,
        grid_spec=pltpu.PrefetchScalarGridSpec(
            num_scalar_prefetch=1,
            grid=(1,),
            in_specs=[whole(a.shape) for a in (tokens, other_tokens, mod, cosine, sine)]
            + half_specs(width, width, 2 * zs, aligned)
            + half_specs(1, width, 2 * zs, aligned),
            out_specs=[whole(o.shape) for o in out_shape],
            scratch_shapes=[
                pltpu.VMEM((2 * clips * rows, width), BF16),
                pltpu.VMEM((zs, *message), BF16),
            ],
        ),
        compiler_params=params(56),
        cost_estimate=cost(
            6 * clips * rows * width * width, 3 * width * width + 32 * rows * width
        ),
        name="norm_qkv",
    )(meta, tokens, other_tokens, mod, cosine, sine, *[weight] * (3 * blocks), *[bias] * (3 * blocks))


def attend_kernel(slots, head, clip, meta, *refs):
    zs = slots // 2
    parts, outs = refs[:zs], refs[zs:slots]
    exact, logs, held, scores, values, sems = refs[slots:]
    copies = [
        pltpu.make_async_copy(parts[k].at[clip], held.at[pl.ds(2 * k, 2)], sems.at[k])
        for k in range(zs)
    ]
    for copy in copies:
        copy.start()
    for copy in copies:
        copy.wait()
    me, context = meta[0], meta[1]
    rows, width = held.shape[2], held.shape[3]
    pairs = width // head

    def prepare(frame, _):
        split = split_heads(held[frame ^ me, 2], pairs, head)
        ones = split_heads(jnp.ones((rows, width), BF16), pairs, head)
        for h in range(pairs):
            values[frame, h] = jnp.concatenate([split[h], ones[h]], axis=1)
        return 0

    lax.fori_loop(0, slots, prepare, 0)

    def attend(slot, count):
        queries = split_heads(held[slot, 0], pairs, head)
        total, tops = None, []
        for h in range(pairs):
            peak = None
            for frame in range(count):
                score = dot_nt(queries[h], held[frame ^ me, 1])
                scores[frame, h * rows : (h + 1) * rows] = score
                for at in range(0, rows, LANES):
                    piece = score[:, at : at + LANES]
                    peak = piece if peak is None else jnp.maximum(peak, piece)
            top = jnp.max(peak, axis=1, keepdims=True)
            tops.append(top)
            for frame in range(count):
                power = jnp.exp(scores[frame, h * rows : (h + 1) * rows] - top).astype(BF16)
                term = dot_nn(power, values[frame, h])
                total = term if total is None else total + term
        weight_sum = total[:, width:]
        result = total[:, :width] / weight_sum
        exact[slot] = result
        top = jnp.broadcast_to(tops[0], (rows, width))
        if pairs > 1:
            lane = lax.broadcasted_iota(jnp.int32, (rows, width), 1)
            for h in range(1, pairs):
                top = jnp.where(lane // head >= h, tops[h], top)
        turned = (top + jnp.log(weight_sum)).T
        logs[slot] = jnp.concatenate(
            [turned[h * head : h * head + 1] for h in range(pairs)], axis=1
        )

    def one_frame(frame, _):
        count = jnp.maximum(frame, context - 1) + 1
        for known in range(1, slots + 1):

            @pl.when(count == known)
            def _():
                attend(frame ^ me, known)

        return 0

    lax.fori_loop(0, slots, one_frame, 0)
    for slot in range(slots):
        outs[slot // 2][slot % 2] = exact[slot].astype(BF16)


def attend_call(meta, clip, parts, head):
    zs = len(parts)
    slots = 2 * zs
    rows, width = parts[0].shape[-2:]
    pairs = width // head
    work = slots * slots * rows * rows
    return pl.pallas_call(
        functools.partial(attend_kernel, slots, head, clip),
        out_shape=[shaped((2, rows, width), BF16)] * zs
        + [shaped((slots, rows, width), F32), shaped((slots, 1, pairs * rows), F32)],
        in_specs=[SMEM] + [ANY] * zs,
        out_specs=[VMEM] * (zs + 2),
        scratch_shapes=[
            pltpu.VMEM((slots, 3, rows, width), BF16),
            pltpu.VMEM((slots, pairs * rows, rows), F32),
            pltpu.VMEM((slots, pairs, rows, 2 * width), BF16),
            pltpu.SemaphoreType.DMA((zs,)),
        ],
        compiler_params=params(40),
        cost_estimate=cost(work * 16 * width, slots * rows * width * 12, work * pairs),
        name="attend",
    )(meta, *parts)


def attend_grad_kernel(slots, head, clip, meta, *refs):
    zs = slots // 2
    parts, grads = refs[:zs], refs[zs:slots]
    exact, logs = refs[slots], refs[slots + 1]
    outs = refs[slots + 2 : slots + 2 + zs]
    held, grad, query_rows, grad_rows, delta, grad_q, grad_k, grad_v, sems, more = refs[
        slots + 2 + zs :
    ]
    copies = []
    for k in range(zs):
        pair = pl.ds(2 * k, 2)
        copies.append(pltpu.make_async_copy(parts[k].at[clip], held.at[pair], sems.at[k]))
        copies.append(pltpu.make_async_copy(grads[k], grad.at[pair], more.at[k]))
    for copy in copies:
        copy.start()
    for copy in copies:
        copy.wait()
    me, context = meta[0], meta[1]
    rows, width = held.shape[2], held.shape[3]
    pairs = width // head

    def prepare(slot, _):
        query_rows[slot] = jnp.concatenate(split_heads(held[slot, 0], pairs, head), axis=0)
        grad_rows[slot] = jnp.concatenate(split_heads(grad[slot], pairs, head), axis=0)
        product = (grad[slot].astype(F32) * exact[slot]).T
        delta[slot] = jnp.concatenate(
            [
                jnp.sum(product[h * head : (h + 1) * head], axis=0, keepdims=True)
                for h in range(pairs)
            ],
            axis=1,
        )
        grad_q[slot] = jnp.zeros((rows, width), F32)
        return 0

    lax.fori_loop(0, slots, prepare, 0)

    def key_frame(frame, _):
        place = frame ^ me
        keys, values = held[place, 1], held[place, 2]
        head_keys = split_heads(keys, pairs, head)
        grad_k[...] = jnp.zeros_like(grad_k)
        grad_v[...] = jnp.zeros_like(grad_v)

        def query_frame(query, _):
            slot = query ^ me
            score = dot_nt(keys, query_rows[slot])
            grad_weight = dot_nt(values, grad_rows[slot])
            weight = jnp.exp(score - logs[slot])
            grad_score = (weight * (grad_weight - delta[slot])).astype(BF16)
            grad_v[...] += dot_nn(weight.astype(BF16), grad_rows[slot])
            grad_k[...] += dot_nn(grad_score, query_rows[slot])
            total = grad_q[slot]
            for h in range(pairs):
                total = total + dot_tn(grad_score[:, h * rows : (h + 1) * rows], head_keys[h])
            grad_q[slot] = total
            return 0

        lax.fori_loop(jnp.where(frame < context, 0, frame), slots, query_frame, 0)
        held[place, 1] = grad_k[...].astype(BF16)
        held[place, 2] = grad_v[...].astype(BF16)
        return 0

    lax.fori_loop(0, slots, key_frame, 0)
    for slot in range(slots):
        out, role = outs[slot // 2], slot % 2
        out[role, 0] = (grad_q[slot] * head**-0.5).astype(BF16)
        out[role, 1] = held[slot, 1]
        out[role, 2] = held[slot, 2]


def attend_grad_call(meta, clip, parts, grads, exact, logs, head):
    zs = len(parts)
    slots = 2 * zs
    rows, width = parts[0].shape[-2:]
    pairs = width // head
    work = slots * slots * rows * rows
    return pl.pallas_call(
        functools.partial(attend_grad_kernel, slots, head, clip),
        out_shape=[shaped((2, 3, rows, width), BF16)] * zs,
        in_specs=[SMEM] + [ANY] * slots + [VMEM, VMEM],
        out_specs=[VMEM] * zs,
        scratch_shapes=[
            pltpu.VMEM((slots, 3, rows, width), BF16),
            pltpu.VMEM((slots, rows, width), BF16),
            pltpu.VMEM((slots, pairs * rows, width), BF16),
            pltpu.VMEM((slots, pairs * rows, width), BF16),
            pltpu.VMEM((slots, 1, pairs * rows), F32),
            pltpu.VMEM((slots, rows, width), F32),
            pltpu.VMEM((rows, width), F32),
            pltpu.VMEM((rows, width), F32),
            pltpu.SemaphoreType.DMA((zs,)),
            pltpu.SemaphoreType.DMA((zs,)),
        ],
        compiler_params=params(40),
        cost_estimate=cost(work * 40 * width, slots * rows * width * 20, work * pairs),
        name="attend_grad",
    )(meta, *parts, *grads, exact, logs)


def mixed_places(width, hidden):
    ends = [0]
    for columns in (width // 2, hidden // 2, width, hidden):
        ends.append(ends[-1] + columns)
    return ends


def forward_back_kernel(slots, clip, meta, tokens, cotangent, mod, proj_b, up_b, down_b, *refs):
    zs = slots // 2
    width, hidden_width = tokens.shape[-1], refs[zs + 2].shape[1]
    at_act, at_gtwo, at_hid = mixed_places(width, hidden_width)[1:4]
    parts, swapped, (proj_hbm, up_hbm, down_hbm) = refs[:zs], refs[zs], refs[zs + 1 : zs + 4]
    (
        layer_out, grad_middle_out, row_grads, up_bgrad,
        att_own, att_far, gone_low, n2_own, act_own, mixed,
        held, far, n2_other, gtwo_low, proj, up, down, slope, active, hid, sems,
    ) = refs[zs + 4 :]
    blocks = up.shape[1] // FF_BLOCK
    fetches = [pltpu.make_async_copy(proj_hbm, proj, sems.at[4])]
    for source, target, columns in ((up_hbm, up, True), (down_hbm, down, False)):
        for block in range(blocks):
            at = pl.ds(block * FF_BLOCK, FF_BLOCK)
            at = (slice(None), at) if columns else (at, slice(None))
            fetches.append(
                pltpu.make_async_copy(source.at[at], target.at[at], sems.at[4 + len(fetches)])
            )
    for fetch in fetches[:IN_FLIGHT]:
        fetch.start()

    def fetched(number):
        fetches[number].wait()
        if number + IN_FLIGHT < len(fetches):
            fetches[number + IN_FLIGHT].start()

    me = meta[0]
    parity = me % 2
    rows = tokens.shape[-2]
    lanes = width // slots
    gate_one, shift_two, scale_two, gate_two = (mod[clip, k : k + 1] for k in (2, 3, 4, 5))
    for k in range(zs):
        held[(2 * k) ^ me] = parts[k][0]
        held[(2 * k + 1) ^ me] = swapped[k]
        far[k ^ (me // 2)] = parts[k][1]
    attended = jnp.concatenate([held[k] for k in range(slots)], axis=1)
    att_own[...] = jnp.concatenate([held[2 * k + parity] for k in range(zs)], axis=1)
    att_far[...] = jnp.concatenate([far[k] for k in range(zs)], axis=1)
    fetched(0)
    branch_one = dot_nn(attended, proj[...]) + proj_b[...].astype(F32)
    middle = tokens[...].reshape(rows, width).astype(F32) + gate_one * branch_one
    hat_two, inverse_two = norm_parts(middle)
    low_two = (hat_two * (1.0 + scale_two) + shift_two).astype(BF16)
    for block in range(slots):
        store_by_parity(
            n2_own, n2_other, slice(block // 2 * lanes, (block // 2 + 1) * lanes), parity, block,
            low_two[:, block * lanes : (block + 1) * lanes],
        )
    n2_copy = pltpu.make_async_copy(n2_other, mixed.at[:, pl.ds(0, width // 2)], sems.at[2])
    n2_copy.start()
    chunk = hidden_width // slots
    for block in range(blocks):
        at = slice(block * FF_BLOCK, (block + 1) * FF_BLOCK)
        fetched(1 + block)
        hidden = dot_nn(low_two, up[:, at]) + up_b[:, at].astype(F32)
        square = hidden * hidden
        bent = jnp.tanh(GELU_A * (hidden + GELU_B * square * hidden))
        half = 0.5 * (1.0 + bent)
        low = (hidden * half).astype(BF16)
        slope[:, at] = half + (0.5 * GELU_A) * hidden * (1.0 - bent * bent) * (
            1.0 + (3.0 * GELU_B) * square
        )
        active[:, at] = low
        for index in range(block * FF_BLOCK // chunk, (block + 1) * FF_BLOCK // chunk):
            piece = active.at[:, pl.ds(index * chunk, chunk)]
            place = pl.ds(index // 2 * chunk, chunk)

            @pl.when(parity == index % 2)
            def _():
                pltpu.make_async_copy(piece, act_own.at[:, place], sems.at[0]).start()

            @pl.when(parity != index % 2)
            def _():
                pltpu.make_async_copy(
                    piece, mixed.at[:, pl.ds(at_act + index // 2 * chunk, chunk)], sems.at[0]
                ).start()

    branch_two = down_b[...].astype(F32)
    for block in range(blocks):
        at = slice(block * FF_BLOCK, (block + 1) * FF_BLOCK)
        fetched(1 + blocks + block)
        branch_two = branch_two + dot_nn(active[:, at], down[at, :])
    layer_out[...] = (middle + gate_two * branch_two).astype(BF16)
    grad_out = cotangent[...].reshape(rows, width).astype(F32)
    low_grad_two = (grad_out * gate_two).astype(BF16)
    gtwo_low[...] = low_grad_two
    gtwo_copy = pltpu.make_async_copy(gtwo_low, mixed.at[:, pl.ds(at_gtwo, width)], sems.at[3])
    gtwo_copy.start()
    row_grads[3:4] = jnp.sum(grad_out * branch_two, axis=0, keepdims=True)
    row_grads[4:5] = jnp.sum(low_grad_two.astype(F32), axis=0, keepdims=True)
    grad_normed = None
    for block in range(blocks):
        at = slice(block * FF_BLOCK, (block + 1) * FF_BLOCK)
        low = (dot_nt(low_grad_two, down[at, :]) * slope[:, at]).astype(BF16)
        hid[:, at] = low
        pltpu.make_async_copy(
            hid.at[:, at], mixed.at[:, pl.ds(at_hid + block * FF_BLOCK, FF_BLOCK)], sems.at[1]
        ).start()
        up_bgrad[:, at] = jnp.sum(low.astype(F32), axis=0, keepdims=True)
        term = dot_nt(low, up[:, at])
        grad_normed = term if grad_normed is None else grad_normed + term
    grad_middle, grad_shift, grad_scale = norm_pull(grad_normed, hat_two, inverse_two, scale_two)
    grad_middle = grad_middle + grad_out
    grad_middle_out[...] = grad_middle
    low_grad_one = (grad_middle * gate_one).astype(BF16)
    gone_low[...] = low_grad_one
    row_grads[0:1] = jnp.sum(grad_middle * branch_one, axis=0, keepdims=True)
    row_grads[1:2] = grad_shift
    row_grads[2:3] = grad_scale
    row_grads[5:6] = jnp.sum(low_grad_one.astype(F32), axis=0, keepdims=True)
    row_grads[6:8] = jnp.zeros((2, width), F32)
    n2_copy.wait()
    gtwo_copy.wait()
    pltpu.make_async_copy(active, active, sems.at[0]).wait()
    pltpu.make_async_copy(hid, hid, sems.at[1]).wait()


def forward_back_call(
    meta, clip, tokens, cotangent, mod, proj_b, up_b, down_b, parts, swapped, proj, up, down
):
    zs = len(parts)
    slots = 2 * zs
    rows, width = tokens.shape[-2:]
    lanes = width // slots
    hidden = up.shape[1]
    half, half_hidden = width // 2, hidden // 2
    out_shape = [
        shaped((rows, width), BF16),
        shaped((rows, width), F32),
        shaped((8, width), F32),
        shaped((1, hidden), F32),
        shaped((rows, half), BF16),
        shaped((rows, half), BF16),
        shaped((rows, width), BF16),
        shaped((rows, half), BF16),
        shaped((rows, half_hidden), BF16),
        shaped((rows, mixed_places(width, hidden)[4]), BF16),
    ]
    full = lambda shape: pl.BlockSpec(shape, lambda t: (0,) * len(shape))
    pick = pl.BlockSpec((1, 1, rows, width), lambda t: (clip, 0, 0, 0))
    return pl.pallas_call(
        functools.partial(forward_back_kernel, slots, clip),
        grid=(1,),
        out_shape=out_shape,
        in_specs=[SMEM, pick, pick]
        + [full(a.shape) for a in (mod, proj_b, up_b, down_b, *parts, swapped)]
        + [ANY] * 3,
        out_specs=[ANY if k in (8, 9) else full(o.shape) for k, o in enumerate(out_shape)],
        scratch_shapes=[
            pltpu.VMEM((slots, rows, lanes), BF16),
            pltpu.VMEM((zs, rows, lanes), BF16),
            pltpu.VMEM((rows, half), BF16),
            pltpu.VMEM((rows, width), BF16),
            pltpu.VMEM(proj.shape, BF16),
            pltpu.VMEM(up.shape, BF16),
            pltpu.VMEM(down.shape, BF16),
            pltpu.VMEM((rows, hidden), F32),
            pltpu.VMEM((rows, hidden), BF16),
            pltpu.VMEM((rows, hidden), BF16),
            pltpu.SemaphoreType.DMA((5 + 2 * hidden // FF_BLOCK,)),
        ],
        compiler_params=params(60),
        cost_estimate=cost(
            4 * rows * width * (width + 2 * hidden),
            4 * width * (width + 2 * hidden),
            rows * hidden,
        ),
        name="feed_forward",
    )(meta, tokens, cotangent, mod, proj_b, up_b, down_b, *parts, swapped, proj, up, down)


def proj_back_kernel(meta, near, far, proj, *outs):
    me = meta[0]
    rows, lanes = near.shape[0], outs[0].shape[2]
    for k, out in enumerate(outs):
        group = me ^ (2 * k)
        weight = proj[pl.ds(pl.multiple_of(group * lanes, lanes), lanes), :]
        out[0] = dot_nt(near[...], weight).astype(BF16)
        out[1] = dot_nt(far[...], weight).astype(BF16)


def proj_back_call(meta, near, far, proj, zs):
    rows, width = near.shape
    lanes = width // (2 * zs)
    return pl.pallas_call(
        proj_back_kernel,
        out_shape=[shaped((2, rows, lanes), BF16)] * zs,
        in_specs=[SMEM, VMEM, VMEM, VMEM],
        out_specs=[VMEM] * zs,
        compiler_params=params(32),
        cost_estimate=cost(2 * rows * width * width, 2 * width * width + 6 * rows * width),
        name="proj_back",
    )(meta, near, far, proj)


def qkv_grad_kernel(zs, head, clip, meta, cosine, sine, *refs):
    blocks = refs[zs].shape[0] // (2 * LANES)
    parts, weights = refs[:zs], refs[zs : zs + 3 * blocks]
    near_out, far_out, near_sum, far_sum, bias_out, held = refs[zs + 3 * blocks :]
    rows, width = near_sum.shape
    clips = cosine.shape[0] // 2
    z = meta[0] // 2
    for k in range(zs):
        held[k ^ z] = parts[k][...]
    totals = [None, None]
    bias_out[...] = jnp.zeros_like(bias_out)
    half = width // 2
    for kind in range(3):
        weight = jnp.concatenate([w[...] for w in weights[kind * blocks : (kind + 1) * blocks]], axis=1)
        sums = None
        for role, out in enumerate((near_out, far_out)):
            low = jnp.concatenate([held[k, role, kind] for k in range(zs)], axis=1)
            if kind < 2:
                row = role * clips + clip
                low = turn(low.astype(F32), cosine[row], sine[row], head, True).astype(BF16)
            out[:, kind * half : (kind + 1) * half] = low
            column = jnp.sum(low.astype(F32), axis=0, keepdims=True)
            sums = column if sums is None else sums + column
            term = dot_nt(low, weight)
            totals[role] = term if totals[role] is None else totals[role] + term
        bias_out[kind : kind + 1] = sums
    near_sum[...] = totals[0]
    far_sum[...] = totals[1]


def qkv_grad_call(meta, clip, cosine, sine, parts, weight, head, aligned):
    zs = len(parts)
    rows, lanes = parts[0].shape[-2:]
    width = 2 * zs * lanes
    blocks = width // (2 * LANES)
    whole = lambda shape: pl.BlockSpec(shape, lambda t, m: (0,) * len(shape))
    out_shape = [
        shaped((rows, 3 * width // 2), BF16),
        shaped((rows, 3 * width // 2), BF16),
        shaped((rows, width), F32),
        shaped((rows, width), F32),
        shaped((8, width // 2), F32),
    ]
    return pl.pallas_call(
        functools.partial(qkv_grad_kernel, zs, head, clip),
        out_shape=out_shape,
        grid_spec=pltpu.PrefetchScalarGridSpec(
            num_scalar_prefetch=1,
            grid=(1,),
            in_specs=[whole(a.shape) for a in (cosine, sine, *parts)]
            + half_specs(width, width, 2 * zs, aligned),
            out_specs=[whole(o.shape) for o in out_shape],
            scratch_shapes=[pltpu.VMEM((zs, 2, 3, rows, lanes), BF16)],
        ),
        compiler_params=params(48),
        cost_estimate=cost(6 * rows * width * width, 3 * width * width + 20 * rows * width),
        name="qkv_grad",
    )(meta, cosine, sine, *parts, *[weight] * (3 * blocks))


def norm_grad_kernel(tokens, mod, *refs):
    clips = tokens.shape[0]
    nears, fars, middles = refs[:clips], refs[clips : 2 * clips], refs[2 * clips : 3 * clips]
    tokens_grad, row_grads = refs[3 * clips :]
    for c in range(clips):
        hat, inverse = norm_parts(tokens[c, 0].astype(F32))
        grad, shift, scale = norm_pull(nears[c][...] + fars[c][...], hat, inverse, mod[c, 1:2])
        tokens_grad[c, 0] = grad + middles[c][...]
        row_grads[c, 0:1] = shift
        row_grads[c, 1:2] = scale
        row_grads[c, 2:8] = jnp.zeros((6, tokens.shape[-1]), F32)


def norm_grad_call(tokens, mod, nears, fars, middles):
    clips, _, rows, width = tokens.shape
    return pl.pallas_call(
        norm_grad_kernel,
        out_shape=[shaped(tokens.shape, F32), shaped((clips, 8, width), F32)],
        in_specs=[VMEM] * (2 + 3 * clips),
        out_specs=[VMEM, VMEM],
        compiler_params=params(40),
        cost_estimate=cost(clips * rows * width * 30, clips * rows * width * 18),
        name="norm_grad",
    )(tokens, mod, *nears, *fars, *middles)


def weight_grad_kernel(jobs, clip_size, zs, meta, *refs):
    arrays_n = sum(2 * job[0] for job in jobs)
    arrays, outs = refs[:arrays_n], refs[arrays_n : arrays_n + 4]
    held, out_sems, in_sems = refs[arrays_n + 4 : arrays_n + 7]
    scratch = refs[arrays_n + 7 :]
    _, _, _, height, cols = held.shape
    tile = zs * height
    z = meta[0] // 2
    clip = meta[2]

    def send_out(slot, tiles, repeat, first, tall):
        for e in range(clip_size):
            for half, first_bit in enumerate((1, clip_size // 2)):
                keep, send = outs[2 * half], outs[2 * half + 1]
                rest = [k for k in range(clip_size) if not k & first_bit]
                if e & first_bit:
                    out, place = send, rest.index(e ^ first_bit)
                else:
                    out, place = keep, rest.index(e)
                low, high = half * zs // 2, (half + 1) * zs // 2
                if not tall:
                    pltpu.make_async_copy(
                        held.at[slot, e, pl.ds(low, zs // 2)],
                        out.at[place, :, pl.ds(first, height)],
                        out_sems.at[slot],
                    ).start()
                    continue
                for block in range(zs):
                    row = repeat * zs + block
                    k = row // tiles
                    if low <= k < high:
                        pltpu.make_async_copy(
                            held.at[slot, e, block],
                            out.at[place, k - low, pl.ds(first + row % tiles * height, height)],
                            out_sems.at[slot],
                        ).start()

    copies = []
    at = 0
    for job, (count, _, _, _, _, places) in enumerate(jobs):
        left, right = scratch[2 * job : 2 * job + 2]
        depth = left.shape[0] // count
        for n in range(2 * count):
            target = left if n < count else right
            source = arrays[at + n]
            if source.shape[1] != target.shape[1]:
                source = source.at[:, pl.ds(places[n], target.shape[1])]
            copies.append(
                pltpu.make_async_copy(
                    source,
                    target.at[pl.ds(n % count * depth, depth)],
                    in_sems.at[at + n],
                )
            )
        at += 2 * count
    for copy in copies:
        copy.start()

    at = number = 0
    for job, (count, lane_parts, tall, tiles, first, _) in enumerate(jobs):
        left, right = scratch[2 * job : 2 * job + 2]
        block = left.shape[1] // zs
        for n in range(2 * count):
            copies[at + n].wait()
        at += 2 * count
        wide = right.shape[1] // (tiles * lane_parts if not tall else 1)
        part = wide // clip_size
        for repeat in range(tiles):
            slot = number % 2
            if number >= 2:
                pltpu.make_async_copy(held.at[slot], held.at[slot], out_sems.at[slot]).wait()
            for lane_part in range(lane_parts):
                if tall:
                    per = zs // tiles
                    rows = [
                        left[:, pl.ds(pl.multiple_of(((repeat * per + n) ^ z) * block, block), block)]
                        for n in range(per)
                    ]
                    rows = rows[0] if per == 1 else jnp.concatenate(rows, axis=1)
                    value = dot_tn(rows, right[...]).astype(BF16)
                else:
                    group = repeat + lane_part
                    value = dot_tn(
                        left[...], right[:, group * wide : (group + 1) * wide]
                    ).astype(BF16)
                for p in range(clip_size):
                    lanes = slice(lane_part * part, (lane_part + 1) * part)
                    piece = value[:, p * part : (p + 1) * part]
                    for k in range(zs):
                        source = piece[k * height : (k + 1) * height]
                        held[slot, p ^ clip, k if tall else k ^ z, :, lanes] = source
            send_out(slot, tiles, repeat, first if tall else first + repeat * height, tall)
            number += 1
    for slot in range(min(number, 2)):
        pltpu.make_async_copy(held.at[slot], held.at[slot], out_sems.at[slot]).wait()


def weight_grad_call(meta, products, clip_size, zs, name):
    jobs, arrays, scratch = [], [], []
    first = flops = 0
    tile = min(p[0][0][2] for p in products)
    height = tile // zs
    piece = None
    for lefts, rights, lane_parts, tall in products:
        depth, total = rights[0][0].shape[0], rights[0][2]
        rows = lefts[0][2]
        if tall:
            tiles, piece = rows // tile, total // clip_size
        elif lane_parts > 1:
            tiles, piece = 1, total // clip_size
        else:
            tiles, piece = total // (2 * tile), 2 * tile // clip_size
        count = len(lefts)
        places = tuple(a[1] for a in lefts + rights)
        jobs.append((count, lane_parts, tall, tiles, first, places))
        first += height * tiles
        arrays += [a[0] for a in lefts + rights]
        flops += 2 * count * depth * rows * total
        scratch += [
            pltpu.VMEM((count * depth, rows), BF16),
            pltpu.VMEM((count * depth, total), BF16),
        ]
    out = shaped((clip_size // 2, zs // 2, first, piece), BF16)
    return pl.pallas_call(
        functools.partial(weight_grad_kernel, tuple(jobs), clip_size, zs),
        out_shape=[out] * 4,
        in_specs=[SMEM] + [ANY] * len(arrays),
        out_specs=[ANY] * 4,
        scratch_shapes=[
            pltpu.VMEM((2, clip_size, zs, height, piece), BF16),
            pltpu.SemaphoreType.DMA((2,)),
            pltpu.SemaphoreType.DMA((len(arrays),)),
        ]
        + scratch,
        compiler_params=params(60),
        cost_estimate=cost(flops, flops / 512 + 8 * out.size),
        name=name,
    )(meta, *arrays)


def place_kernel(jobs, pieces, meta, *refs):
    parts, outs = refs[:pieces], refs[pieces:]
    clip = meta[2]
    cols = parts[0].shape[1]
    for e in range(pieces):
        first = 0
        for out, (height, repeats, tall) in zip(outs, jobs):
            for repeat in range(repeats):
                base = 0 if tall else repeat * cols * pieces
                target = pl.ds(pl.multiple_of(base + (clip ^ e) * cols, cols), cols)
                value = parts[e][first : first + height].astype(F32)
                if tall:
                    out[repeat * height : (repeat + 1) * height, target] = value
                else:
                    out[:, target] = value
                first += height


def place_call(meta, parts, jobs, outs):
    return pl.pallas_call(
        functools.partial(place_kernel, jobs, len(parts)),
        out_shape=outs,
        in_specs=[SMEM] + [VMEM] * len(parts),
        out_specs=[VMEM] * len(outs),
        compiler_params=params(32),
        cost_estimate=cost(0, sum(o.size * 4 for o in outs)),
        name="place_grads",
    )(meta, *parts)


def place_qkv_kernel(meta, *refs):
    parts, out = refs[:-1], refs[-1]
    parity, clip = meta[0] % 2, meta[2]
    thirds = out.shape[1] // 3
    for e, part in enumerate(parts):
        for role in range(2):
            block = 2 * (clip ^ e) + (parity ^ role)
            for kind in range(3):
                at = pl.ds(pl.multiple_of(kind * thirds + block * LANES, LANES), LANES)
                out[:, at] = part[role, :, kind * LANES : (kind + 1) * LANES].astype(F32)


def place_qkv_call(meta, parts, out):
    return pl.pallas_call(
        place_qkv_kernel,
        out_shape=out,
        in_specs=[SMEM] + [VMEM] * len(parts),
        out_specs=VMEM,
        compiler_params=params(32),
        cost_estimate=cost(0, out.size * 6),
        name="place_qkv_grad",
    )(meta, *parts)


def exchange(array, axis, size, distance):
    return lax.ppermute(array, axis, [(k, k ^ distance) for k in range(size)])


def after(value, *others):
    return lax.optimization_barrier((value, *others))


def spread(slots_out, seq_size):
    return [slots_out[0]] + [
        exchange(slots_out[k], "seq", seq_size, 2 * k) for k in range(1, seq_size // 2)
    ]


def add_low(left, right):
    return (left.astype(F32) + right.astype(F32)).astype(BF16)


def step_out(pairs, bits, size):
    return [exchange(send, "clip", size, bit) for (_, send), bit in zip(pairs, bits)]


def step_in(pairs, arrived):
    left = []
    for (keep, _), new in zip(pairs, arrived):
        half = keep.shape[0] // 2
        if half:
            left.append((add_low(keep[:half], new[:half]), add_low(keep[half:], new[half:])))
        else:
            left.append((add_low(keep[0], new[0]), None))
    return left


def clip_orders(clip_size):
    down = [1 << k for k in reversed(range(clip_size.bit_length() - 1))]
    return [1] + down[:-1], down


def z_out(pairs, seq_size):
    near, far = pairs[0][0], pairs[1][0]
    half = seq_size // 4
    return [
        exchange(near[k] if k < half else far[k - half], "seq", seq_size, 2 * k)
        for k in range(1, seq_size // 2)
    ]


def z_in(pairs, arrived):
    total = pairs[0][0][0].astype(F32)
    for part in arrived:
        total = total + part.astype(F32)
    return total.astype(BF16)


def gather_pieces(piece, clip_size):
    return [piece] + [exchange(piece, "clip", clip_size, d) for d in range(1, clip_size)]


def double(array, axis, size):
    bit = 1
    while bit < size:
        array = jnp.concatenate([array, exchange(array, axis, size, bit)])
        bit *= 2
    return array


def silu_act(values_in):
    return values_in * jax.nn.sigmoid(values_in)


def rotary_tables(stamps, patch_count, head):
    lane = jnp.arange(LANES, dtype=jnp.int32)
    quarter = head // 4
    pair = lane % (head // 2)
    freqs = 10000.0 ** (-(pair % quarter).astype(F32) / quarter)
    temporal = stamps.astype(F32)[:, None, None] * freqs[None, None, :]
    spatial = jnp.arange(patch_count).astype(F32)[None, :, None] * freqs[None, None, :]
    angles = jnp.where((pair < quarter)[None, None, :], temporal, spatial)
    sign = jnp.where(lane % head < head // 2, -1.0, 1.0).astype(F32)
    return jnp.cos(angles), jnp.sin(angles) * sign[None, None, :]


def on_device(
    tokens,
    cotangent,
    context_count,
    noise_level,
    frame_time,
    level_table,
    mod_weight,
    mod_bias,
    qkv_weight,
    qkv_bias,
    proj_weight,
    proj_bias,
    up_weight,
    up_bias,
    down_weight,
    down_bias,
):
    seq_size, clip_size = lax.axis_size("seq"), lax.axis_size("clip")
    me, mine = lax.axis_index("seq"), lax.axis_index("clip")
    clips, _, rows, width = tokens.shape
    head = width // HEADS
    hidden = up_weight.shape[1]
    zs = seq_size // 2
    me = me.astype(jnp.int32)
    mine = mine.astype(jnp.int32)
    parity = me % 2
    aligned = (width // seq_size) % LANES == 0
    metas = [jnp.stack([me, context_count[c], mine]) for c in range(clips)]
    stamps = jnp.stack([noise_level[:, 0], frame_time[:, 0]])
    other_stamps = exchange(stamps, "seq", seq_size, 1)
    other_tokens = exchange(tokens, "seq", seq_size, 1)
    both_levels = jnp.concatenate(
        [
            jnp.where(me < context_count, 0, stamps[0]),
            jnp.where((me ^ 1) < context_count, 0, other_stamps[0]),
        ]
    )
    levels_used = both_levels[:clips]
    picked = (
        both_levels[:, None] == jnp.arange(level_table.shape[0], dtype=jnp.int32)[None, :]
    ).astype(BF16)
    condition = jnp.dot(picked, level_table, preferred_element_type=F32)
    condition_low = silu_act(condition).astype(BF16)
    modulation = jnp.dot(
        condition_low, mod_weight, preferred_element_type=F32
    ) + mod_bias.astype(F32)
    mods = modulation.reshape(2 * clips, 6, width)
    cosine, sine = rotary_tables(jnp.concatenate([stamps[1], other_stamps[1]]), rows, head)
    qkv_bias_row = qkv_bias[None]
    if aligned:
        weight_half, bias_half = qkv_weight, qkv_bias_row
    else:
        weight_half = half_columns(qkv_weight, seq_size, parity)
        bias_half = half_columns(qkv_bias_row, seq_size, parity)

    out = qkv_call(
        metas[0], tokens, other_tokens, mods, cosine, sine, weight_half, bias_half, zs, head, aligned
    )
    parts = spread(out[:zs], seq_size)
    normed = out[zs:]
    swap = lambda array: exchange(array, "seq", seq_size, 1)
    full = lambda array: (array, 0, array.shape[1])
    at_n2, at_act, at_gtwo, at_hid, _ = mixed_places(width, hidden)
    exact, logs, attended, crossed = [], [], [], []
    for c in range(clips):
        meta = metas[c]
        if c:
            meta, logs[-1] = after(meta, logs[-1])
        out = attend_call(meta, c, parts, head)
        exact.append(out[zs])
        logs.append(out[zs + 1])
        sends = out[:zs]
        if c:
            sends, attended[-1] = after(sends, attended[-1])
            crossed.append(swap(jnp.stack([a[1] for a in attended[-1]])))
        attended.append(spread(sends, seq_size))
    layer, middles, row_grads, up_bgrads, saved, mixed, far_ones, grads = ([] for _ in range(8))
    for c in range(clips):
        meta = metas[c]
        if c:
            meta, grads[-1][0] = after(meta, grads[-1][0])
        out = forward_back_call(
            meta, c, tokens, cotangent, mods, proj_bias[None], up_bias[None],
            down_bias[None], attended[c], crossed[c], proj_weight, up_weight, down_weight,
        )
        layer.append(out[0])
        middles.append(out[1])
        row_grads.append(out[2])
        up_bgrads.append(out[3])
        gone, mine_mixed = out[6], out[9]
        if c < clips - 1:
            gone, mine_mixed, attended[c + 1] = after(gone, mine_mixed, attended[c + 1])
            crossed.append(swap(jnp.stack([a[1] for a in attended[c + 1]])))
        if c:
            gone, mine_mixed, grads[-1], mixed[-1] = after(gone, mine_mixed, grads[-1], mixed[-1])
        far_ones.append(swap(gone))
        mixed.append([mine_mixed, swap(mine_mixed)])
        saved.append((out[4], out[5], gone, out[7], out[8]))
        back = proj_back_call(metas[c], gone, far_ones[c], proj_weight, zs)
        grads.append(spread(back, seq_size))
    row = width // seq_size
    orders = clip_orders(clip_size)
    steps = len(orders[0])
    returned = []
    for c in range(clips):
        if c:
            meta, shares[0] = after(metas[c], shares[0])
        else:
            meta, grads[-1][0] = after(metas[c], grads[-1][0])
        out = attend_grad_call(meta, c, parts, grads[c], exact[c], logs[c], head)
        if c < clips - 1:
            out, grads[-1], mixed[-1] = after(out, grads[-1], mixed[-1])
        else:
            out, returned[-1] = after(out, returned[-1])
        returned.append(spread(out, seq_size))
        if c == 0:
            products = [([], [], 1, False), ([], [], 1, True), ([], [], 1, False)]
            for k in range(clips):
                att_own, att_far, gone, n2_own, act_own = saved[k]
                own, far = mixed[k]
                products[0][0].extend([full(att_own), full(att_far)])
                products[0][1].extend([full(gone), full(far_ones[k])])
                products[1][0].extend([full(act_own), (far, at_act, hidden // 2)])
                products[1][1].extend([(own, at_gtwo, width), (far, at_gtwo, width)])
                products[2][0].extend([full(n2_own), (far, at_n2, width // 2)])
                products[2][1].extend([(own, at_hid, hidden), (far, at_hid, hidden)])
            shares = weight_grad_call(metas[c], products, clip_size, zs, "weight_grads")
            shares = list(shares)
    pairs = [shares[:2], shares[2:]]
    turns = list(zip(*orders))
    grad_rights, nears, fars, qkv_bgrads = [], [], [], []
    for c in range(clips):
        if c:
            kept = [pair[0] for pair in pairs]
            kept, qkv_bgrads[0] = after(kept, qkv_bgrads[0])
            pairs = [(keep, pair[1]) for keep, pair in zip(kept, pairs)]
            pairs = step_in(pairs, step_out(pairs, turns[0], clip_size))
            meta, pairs = after(metas[c], pairs)
        else:
            meta, returned[-1][0] = after(metas[c], returned[-1][0])
        out = qkv_grad_call(meta, c, cosine, sine, returned[c], weight_half, head, aligned)
        grad_rights.extend(out[:2])
        nears.append(out[2])
        fars.append(swap(out[3]))
        qkv_bgrads.append(out[4][:3])
    tokens_grad, late_rows = norm_grad_call(tokens, mods, nears, fars, middles)
    lefts = [normed[role * clips + c] for c in range(clips) for role in range(2)]
    last_steps = turns[1:]
    if aligned:
        shares = weight_grad_call(
            metas[0],
            [([full(a) for a in lefts], [full(a) for a in grad_rights], 3, False)],
            clip_size,
            zs,
            "qkv_weight_grad",
        )
        if last_steps:
            arrived = step_out(pairs, last_steps[0], clip_size)
            arrived, shares = after(arrived, shares)
            pairs = step_in(pairs, arrived)
            last_steps = last_steps[1:]
    for bits in last_steps:
        pairs = step_in(pairs, step_out(pairs, bits, clip_size))
    landed = z_out(pairs, seq_size)
    if aligned:
        pairs_qkv = [shares[:2], shares[2:]]
        for bits in turns:
            pairs_qkv = step_in(pairs_qkv, step_out(pairs_qkv, bits, clip_size))
        pairs_qkv, landed = after(pairs_qkv, landed)
        pieces = gather_pieces(z_in(pairs, landed), clip_size)
        piece = z_in(pairs_qkv, z_out(pairs_qkv, seq_size)).reshape(2, row, 3 * LANES)
        own_rows = lax.dynamic_index_in_dim(piece, parity, 0, keepdims=False)
        far_rows = swap(lax.dynamic_index_in_dim(piece, 1 - parity, 0, keepdims=False))
        far_rows, pieces = after(far_rows, pieces)
        qkv_wgrad = place_qkv_call(
            metas[0],
            gather_pieces(jnp.stack([own_rows, far_rows]), clip_size),
            shaped((row, 3 * width), F32),
        )
    else:
        pieces = gather_pieces(z_in(pairs, landed), clip_size)
        share = sum(
            lax.dot_general(left, right, (((0,), (0,)), ((), ())), preferred_element_type=F32)
            for left, right in zip(lefts, grad_rights)
        ).astype(BF16)
        share = share.reshape(width, 3, zs, 1, width // seq_size)
        blank = jnp.zeros_like(share)
        share = jnp.where(
            parity == 0,
            jnp.concatenate([share, blank], axis=3),
            jnp.concatenate([blank, share], axis=3),
        ).reshape(width, 3 * width)
        qkv_wgrad = lax.psum(
            lax.psum_scatter(share, "seq", scatter_dimension=0, tiled=True), "clip"
        ).astype(F32)

    level_rows = jnp.stack([levels_used // 32, levels_used % 32]).astype(F32)
    level_rows = jnp.concatenate([level_rows, jnp.zeros((2, width - clips), F32)], axis=1)
    mod_rows = []
    for c in range(clips):
        mod_rows += [late_rows[c, 0:2], row_grads[c][0:4]]
    bias_rows = [
        sum(qkv_bgrads).reshape(3 * width // 2),
        jnp.zeros((width // 2,), F32),
        sum(up_bgrads).reshape(hidden),
        sum(r[4] for r in row_grads),
        sum(r[5] for r in row_grads),
    ]
    bias_rows = jnp.concatenate(bias_rows).reshape(-1, width)
    late = jnp.concatenate([condition[:clips], level_rows] + mod_rows + [bias_rows], axis=0)
    start, stop = clips + 2, clips + 2 + 6 * clips
    late = double(late.astype(BF16)[None], "seq", seq_size)
    own_sums = jnp.sum(
        late[:, stop:].astype(F32).reshape(zs, 2, late.shape[1] - stop, width), axis=0
    ).astype(BF16)
    sums_rows = 2 * own_sums.shape[1]
    message = jnp.concatenate(
        [late[:, :stop].reshape(seq_size * stop, width), own_sums.reshape(sums_rows, width)]
    )
    late = double(message[None], "clip", clip_size)
    own_sums = jnp.sum(late[:, seq_size * stop :].astype(F32), axis=0).reshape(2, -1)
    late = late[:, : seq_size * stop].reshape(clip_size * seq_size, stop, width)
    devices = clip_size * seq_size
    grad_modulation = late[:, start:].reshape(devices * clips, 6 * width)
    half_bias = own_sums[:, : 3 * width // 2].reshape(2, 3, zs, 1, width // seq_size)
    bias_sums = jnp.sum(own_sums, axis=0)[2 * width :]
    qkv_bias_sums = jnp.where(
        parity == 0,
        jnp.concatenate([half_bias[0], half_bias[1]], axis=2),
        jnp.concatenate([half_bias[1], half_bias[0]], axis=2),
    ).reshape(3 * width)
    all_condition = late[:, :clips].reshape(devices * clips, width).astype(F32)
    codes = late[:, clips:start, :clips].astype(jnp.int32)
    all_levels = (codes[:, 0] * 32 + codes[:, 1]).reshape(devices * clips)
    all_active, silu_pull = jax.vjp(silu_act, all_condition)
    my_active = lax.dynamic_slice_in_dim(all_active, me * row, row, axis=1).astype(BF16)
    mod_wgrad = lax.dot_general(
        my_active, grad_modulation, (((0,), (0,)), ((), ())), preferred_element_type=F32
    )
    (grad_condition,) = silu_pull(
        lax.dot_general(
            grad_modulation, mod_weight, (((1,), (1,)), ((), ())), preferred_element_type=F32
        )
    )
    table_row = level_table.shape[0] // seq_size
    onehot = (
        all_levels[:, None] == (me * table_row + jnp.arange(table_row, dtype=jnp.int32))[None, :]
    ).astype(F32)
    table_grad = lax.dot_general(
        onehot,
        grad_condition,
        (((0,), (0,)), ((), ())),
        precision=HIGHEST_PRECISION,
        preferred_element_type=F32,
    )
    mod_sums = jnp.sum(grad_modulation.astype(F32), axis=0)

    def own_part(vector):
        size = vector.shape[0] // seq_size
        return lax.dynamic_slice_in_dim(vector, me * size, size, axis=0)

    mod_bgrad = own_part(mod_sums)
    qkv_bgrad = own_part(qkv_bias_sums)
    up_bgrad = own_part(bias_sums[:hidden])
    down_bgrad = own_part(bias_sums[hidden : hidden + width])
    proj_bgrad = own_part(bias_sums[hidden + width : hidden + 2 * width])
    meta, mod_wgrad, table_grad, qkv_wgrad = after(metas[0], mod_wgrad, table_grad, qkv_wgrad)
    proj_wgrad, down_wgrad, up_wgrad = place_call(
        meta,
        pieces,
        (
            (row, 1, False),
            (row, hidden // width, True),
            (row, hidden // width, False),
        ),
        [shaped((row, width), F32), shaped((hidden // seq_size, width), F32), shaped((row, hidden), F32)],
    )
    layer_out = jnp.stack(layer)[:, None]
    return (
        layer_out,
        tokens_grad,
        table_grad,
        mod_wgrad,
        mod_bgrad,
        qkv_wgrad,
        qkv_bgrad,
        proj_wgrad,
        proj_bgrad,
        up_wgrad,
        up_bgrad,
        down_wgrad,
        down_bgrad,
    )


def solution(mesh):
    placed = (
        P("clip", "seq", None, None),
        P("clip", "seq", None, None),
        P("clip"),
        P("clip", "seq"),
        P("clip", "seq"),
    ) + (P(),) * 11
    return jax.shard_map(
        on_device,
        mesh=mesh,
        in_specs=placed,
        out_specs=(
            P("clip", "seq", None, None),
            P("clip", "seq", None, None),
            P("seq", None),
            P("seq", None),
            P("seq"),
            P("seq", None),
            P("seq"),
            P("seq", None),
            P("seq"),
            P("seq", None),
            P("seq"),
            P("seq", None),
            P("seq"),
        ),
        check_vma=False,
    )
```

```python
import functools

import jax
import jax.numpy as jnp
from jax import lax
from jax.experimental import pallas as pl
from jax.experimental.pallas import tpu as pltpu
from jax.sharding import PartitionSpec as P

HEADS = 16
EPS = 1e-06
HIGHEST_PRECISION = lax.Precision.HIGHEST
F32 = jnp.float32
BF16 = jnp.bfloat16
ANY = pl.BlockSpec(memory_space=pltpu.HBM)
VMEM = pl.BlockSpec(memory_space=pltpu.VMEM)
SMEM = pl.BlockSpec(memory_space=pltpu.SMEM)
LANES = 128
BLOCK = 256
FF_BLOCK = 1024
IN_FLIGHT = 3
GROUPS = (8, 4, 2, 1)
GELU_A = 0.7978845608028654
GELU_B = 0.044715
WEIGHT = 1.0
VMEM_BYTES = 62 << 20


def shaped(shape, dtype):
    return jax.ShapeDtypeStruct(shape, dtype)


def params():
    return pltpu.CompilerParams(vmem_limit_bytes=VMEM_BYTES)


def cost(flops, moved, transcendentals=0):
    return pl.CostEstimate(
        flops=int(flops * WEIGHT),
        bytes_accessed=int(moved * WEIGHT),
        transcendentals=int(transcendentals * WEIGHT),
    )


def dot_nn(left, right):
    return lax.dot_general(left, right, (((1,), (0,)), ((), ())), preferred_element_type=F32)


def dot_nt(left, right):
    return lax.dot_general(left, right, (((1,), (1,)), ((), ())), preferred_element_type=F32)


def dot_tn(left, right):
    return lax.dot_general(left, right, (((0,), (0,)), ((), ())), preferred_element_type=F32)


def split_heads(values, pairs, head):
    if pairs == 1:
        return [values]
    lane = lax.broadcasted_iota(jnp.int32, values.shape, 1)
    return [jnp.where(lane // head == h, values, jnp.zeros_like(values)) for h in range(pairs)]


def swap_halves(values, head):
    half = head // 2
    lane = lax.broadcasted_iota(jnp.int32, values.shape, 1)
    ahead = pltpu.roll(values, values.shape[1] - half, 1)
    behind = pltpu.roll(values, half, 1)
    return jnp.where(lax.rem(lane, head) < half, ahead, behind)


def turn(values, cosine, signed_sine, head, back):
    parts = []
    for at in range(0, values.shape[1], LANES):
        piece = values[:, at : at + LANES]
        other = swap_halves(piece, head) * signed_sine
        parts.append(piece * cosine - other if back else piece * cosine + other)
    return jnp.concatenate(parts, axis=1)


def norm_parts(values):
    center = jnp.mean(values, axis=-1, keepdims=True)
    offset = values - center
    spread = jnp.mean(offset * offset, axis=-1, keepdims=True)
    inverse = lax.rsqrt(spread + EPS)
    return offset * inverse, inverse


def norm_pull(grad, hat, inverse, scale_row):
    grad_shift = jnp.sum(grad, axis=0, keepdims=True)
    grad_scale = jnp.sum(grad * hat, axis=0, keepdims=True)
    inner = grad * (1.0 + scale_row)
    mean_one = jnp.mean(inner, axis=-1, keepdims=True)
    mean_two = jnp.mean(inner * hat, axis=-1, keepdims=True)
    return inverse * (inner - mean_one - hat * mean_two), grad_shift, grad_scale


def store_by_parity(own_ref, other_ref, where, parity, block_index, value):
    own = parity == block_index % 2

    @pl.when(own)
    def _():
        own_ref[:, where] = value

    @pl.when(jnp.logical_not(own))
    def _():
        other_ref[:, where] = value


def modulation_kernel(meta, table, weight, bias, out, condition_out, low):
    rows, levels = out.shape[1], table.shape[0]

    @pl.when(pl.program_id(0) == 0)
    def _():
        lane = lax.broadcasted_iota(jnp.int32, (1, levels), 1)
        picked = jnp.concatenate(
            [jnp.where(lane == meta[row], 1.0, 0.0) for row in range(rows)], axis=0
        )
        condition = dot_nn(picked.astype(BF16), table[...])
        condition_out[...] = condition
        low[...] = silu_act(condition).astype(BF16)

    out[0] = dot_nn(low[...], weight[...]) + bias[...].astype(F32)


def modulation_call(levels, table, weight, bias, first, parts):
    rows, width = levels.shape[0], table.shape[1]
    return pl.pallas_call(
        modulation_kernel,
        grid=(parts,),
        out_shape=[shaped((parts, rows, width), F32), shaped((rows, width), F32)],
        in_specs=[
            SMEM,
            pl.BlockSpec(table.shape, lambda t: (0, 0)),
            pl.BlockSpec((width, width), lambda t: (0, first + t)),
            pl.BlockSpec((1, width), lambda t: (0, first + t)),
        ],
        out_specs=[
            pl.BlockSpec((1, rows, width), lambda t: (t, 0, 0)),
            pl.BlockSpec((rows, width), lambda t: (0, 0)),
        ],
        scratch_shapes=[pltpu.VMEM((rows, width), BF16)],
        compiler_params=params(),
        cost_estimate=cost(0, 2 * (parts + 1) * width * width),
        name="modulation",
    )(levels, table, weight, bias)


def turn_table(temporal, spatial, row, head):
    lane = lax.broadcasted_iota(jnp.int32, spatial.shape, 1)
    timed = lax.rem(lane, head // 2) < head // 4
    return jnp.where(timed, temporal[row : row + 1], spatial[...])


def half_columns(weight, groups, parity):
    rows, total = weight.shape
    view = weight.reshape(rows, 3, groups // 2, 2, total // (3 * groups))
    return lax.dynamic_index_in_dim(view, parity, 3, keepdims=False).reshape(rows, total // 2)


def half_specs(height, width, groups, aligned):
    specs = []
    for kind in range(3):
        for block in range(width // (2 * LANES)):
            if aligned:
                specs.append(
                    pl.BlockSpec(
                        (height, LANES), lambda t, m, k=kind, b=block: (0, k * groups + 2 * b + m[0] % 2)
                    )
                )
            else:
                specs.append(
                    pl.BlockSpec(
                        (height, LANES),
                        lambda t, m, k=kind, b=block: (0, k * (width // (2 * LANES)) + b),
                    )
                )
    return specs


def qkv_kernel(zs, head, meta, tokens, other_tokens, mod, *refs):
    tables, refs = refs[:4], refs[4:]
    blocks = tokens.shape[-1] // (2 * LANES)
    weights, biases = refs[: 3 * blocks], refs[3 * blocks : 6 * blocks]
    clips, _, rows, width = tokens.shape
    outs = refs[6 * blocks : 6 * blocks + zs * clips]
    normed_outs, (normed, held) = refs[6 * blocks + zs * clips : -2], refs[-2:]
    cosines = [turn_table(tables[0], tables[2], row, head) for row in range(2 * clips)]
    sines = [turn_table(tables[1], tables[3], row, head) for row in range(2 * clips)]
    lanes = width // (2 * zs)
    z = meta[0] // 2
    for row in range(2 * clips):
        role, clip = row // clips, row % clips
        source = (tokens, other_tokens)[role]
        hat, _ = norm_parts(source[clip, 0].astype(F32))
        low = (hat * (1.0 + mod[1, row : row + 1]) + mod[0, row : row + 1]).astype(BF16)
        normed[row * rows : (row + 1) * rows] = low
        normed_outs[row][...] = low
    for kind in range(3):
        pick = slice(kind * blocks, (kind + 1) * blocks)
        weight = jnp.concatenate([w[...] for w in weights[pick]], axis=1)
        bias = jnp.concatenate([b[...] for b in biases[pick]], axis=1).astype(F32)
        value = dot_nn(normed[...], weight) + bias
        for row in range(2 * clips):
            role, clip = row // clips, row % clips
            part = value[row * rows : (row + 1) * rows]
            if kind < 2:
                part = turn(part, cosines[row], sines[row], head, False)
            part = part.astype(BF16)
            if kind == 0:
                part = part * jnp.asarray(head**-0.5, BF16)
            for group in range(zs):
                held[clip, group ^ z, role, kind] = part[:, group * lanes : (group + 1) * lanes]
    for n, out in enumerate(outs):
        out[...] = held[n // zs, n % zs]


def qkv_call(meta, tokens, other_tokens, mod, tables, weight, bias, zs, head, aligned):
    clips, _, rows, width = tokens.shape
    lanes = width // (2 * zs)
    whole = lambda shape: pl.BlockSpec(shape, lambda t, m: (0,) * len(shape))
    blocks = width // (2 * LANES)
    message = (2, 3, rows, lanes)
    out_shape = [shaped(message, BF16)] * (zs * clips)
    out_shape += [shaped((rows, width), BF16)] * (2 * clips)
    return pl.pallas_call(
        functools.partial(qkv_kernel, zs, head),
        out_shape=out_shape,
        grid_spec=pltpu.PrefetchScalarGridSpec(
            num_scalar_prefetch=1,
            grid=(1,),
            in_specs=[whole(a.shape) for a in (tokens, other_tokens, mod, *tables)]
            + half_specs(width, width, 2 * zs, aligned)
            + half_specs(1, width, 2 * zs, aligned),
            out_specs=[whole(o.shape) for o in out_shape],
            scratch_shapes=[
                pltpu.VMEM((2 * clips * rows, width), BF16),
                pltpu.VMEM((clips, zs, *message), BF16),
            ],
        ),
        compiler_params=params(),
        cost_estimate=cost(
            6 * clips * rows * width * width, 3 * width * width + 32 * rows * width
        ),
        name="norm_qkv",
    )(meta, tokens, other_tokens, mod, *tables, *[weight] * (3 * blocks), *[bias] * (3 * blocks))


def attend_kernel(slots, head, clip, meta, *refs):
    zs = slots // 2
    parts, outs = refs[:zs], refs[zs:slots]
    exact, logs, held, scores, values, sems = refs[slots:]
    copies = [
        pltpu.make_async_copy(parts[k], held.at[pl.ds(2 * k, 2)], sems.at[k])
        for k in range(zs)
    ]
    for copy in copies:
        copy.start()
    for copy in copies:
        copy.wait()
    me, context = meta[0], meta[2 + clip]
    rows, width = held.shape[2], held.shape[3]
    pairs = width // head

    def prepare(frame, _):
        split = split_heads(held[frame ^ me, 2], pairs, head)
        ones = split_heads(jnp.ones((rows, width), BF16), pairs, head)
        for h in range(pairs):
            values[frame, h] = jnp.concatenate([split[h], ones[h]], axis=1)
        return 0

    lax.fori_loop(0, slots, prepare, 0)

    def attend(slot, count):
        queries = split_heads(held[slot, 0], pairs, head)
        total, tops = None, []
        for h in range(pairs):
            peak = None
            for frame in range(count):
                score = dot_nt(queries[h], held[frame ^ me, 1])
                scores[frame, h * rows : (h + 1) * rows] = score
                for at in range(0, rows, LANES):
                    piece = score[:, at : at + LANES]
                    peak = piece if peak is None else jnp.maximum(peak, piece)
            top = jnp.max(peak, axis=1, keepdims=True)
            tops.append(top)
            for frame in range(count):
                power = jnp.exp(scores[frame, h * rows : (h + 1) * rows] - top).astype(BF16)
                term = dot_nn(power, values[frame, h])
                total = term if total is None else total + term
        weight_sum = total[:, width:]
        result = total[:, :width] / weight_sum
        exact[slot] = result
        top = jnp.broadcast_to(tops[0], (rows, width))
        if pairs > 1:
            lane = lax.broadcasted_iota(jnp.int32, (rows, width), 1)
            for h in range(1, pairs):
                top = jnp.where(lane // head >= h, tops[h], top)
        turned = (top + jnp.log(weight_sum)).T
        logs[slot] = jnp.concatenate(
            [turned[h * head : h * head + 1] for h in range(pairs)], axis=1
        )

    def one_frame(frame, _):
        count = jnp.maximum(frame, context - 1) + 1
        for known in range(1, slots + 1):

            @pl.when(count == known)
            def _():
                attend(frame ^ me, known)

        return 0

    lax.fori_loop(0, slots, one_frame, 0)
    for slot in range(slots):
        outs[slot // 2][slot % 2] = exact[slot].astype(BF16)


def attend_call(meta, clip, parts, head):
    zs = len(parts)
    slots = 2 * zs
    rows, width = parts[0].shape[-2:]
    pairs = width // head
    work = slots * slots * rows * rows
    return pl.pallas_call(
        functools.partial(attend_kernel, slots, head, clip),
        out_shape=[shaped((2, rows, width), BF16)] * zs
        + [shaped((slots, rows, width), F32), shaped((slots, 1, pairs * rows), F32)],
        in_specs=[SMEM] + [ANY] * zs,
        out_specs=[VMEM] * (zs + 2),
        scratch_shapes=[
            pltpu.VMEM((slots, 3, rows, width), BF16),
            pltpu.VMEM((slots, pairs * rows, rows), F32),
            pltpu.VMEM((slots, pairs, rows, 2 * width), BF16),
            pltpu.SemaphoreType.DMA((zs,)),
        ],
        compiler_params=params(),
        cost_estimate=cost(work * 16 * width, slots * rows * width * 12, work * pairs),
        name="attend",
    )(meta, *parts)


def attend_grad_kernel(slots, head, clip, meta, *refs):
    zs = slots // 2
    parts, grads = refs[:zs], refs[zs:slots]
    exact, logs = refs[slots], refs[slots + 1]
    outs = refs[slots + 2 : slots + 2 + zs]
    held, grad, query_rows, grad_rows, delta, grad_q, grad_k, grad_v, sems, more = refs[
        slots + 2 + zs :
    ]
    copies = []
    for k in range(zs):
        pair = pl.ds(2 * k, 2)
        copies.append(pltpu.make_async_copy(parts[k], held.at[pair], sems.at[k]))
        copies.append(pltpu.make_async_copy(grads[k], grad.at[pair], more.at[k]))
    for copy in copies:
        copy.start()
    for copy in copies:
        copy.wait()
    me, context = meta[0], meta[2 + clip]
    rows, width = held.shape[2], held.shape[3]
    pairs = width // head

    def prepare(slot, _):
        query_rows[slot] = jnp.concatenate(split_heads(held[slot, 0], pairs, head), axis=0)
        grad_rows[slot] = jnp.concatenate(split_heads(grad[slot], pairs, head), axis=0)
        product = (grad[slot].astype(F32) * exact[slot]).T
        delta[slot] = jnp.concatenate(
            [
                jnp.sum(product[h * head : (h + 1) * head], axis=0, keepdims=True)
                for h in range(pairs)
            ],
            axis=1,
        )
        grad_q[slot] = jnp.zeros((rows, width), F32)
        return 0

    lax.fori_loop(0, slots, prepare, 0)

    def key_frame(frame, _):
        place = frame ^ me
        keys, values = held[place, 1], held[place, 2]
        head_keys = split_heads(keys, pairs, head)
        grad_k[...] = jnp.zeros_like(grad_k)
        grad_v[...] = jnp.zeros_like(grad_v)

        def query_frames(first, count):
            add_k = add_v = None
            for n in range(count):
                slot = (first + n) ^ me
                score = dot_nt(keys, query_rows[slot])
                grad_weight = dot_nt(values, grad_rows[slot])
                weight = jnp.exp(score - logs[slot])
                grad_score = (weight * (grad_weight - delta[slot])).astype(BF16)
                term_v = dot_nn(weight.astype(BF16), grad_rows[slot])
                term_k = dot_nn(grad_score, query_rows[slot])
                add_v = term_v if add_v is None else add_v + term_v
                add_k = term_k if add_k is None else add_k + term_k
                total = grad_q[slot]
                for h in range(pairs):
                    total = total + dot_tn(grad_score[:, h * rows : (h + 1) * rows], head_keys[h])
                grad_q[slot] = total
            grad_v[...] += add_v
            grad_k[...] += add_k

        first = jnp.where(frame < context, 0, frame)
        for size in GROUPS:
            if size > slots:
                continue
            count = (slots - first) // size

            def group_step(n, _, first=first, size=size):
                query_frames(first + n * size, size)
                return 0

            lax.fori_loop(0, count, group_step, 0)
            first = first + count * size
        held[place, 1] = grad_k[...].astype(BF16)
        held[place, 2] = grad_v[...].astype(BF16)
        return 0

    lax.fori_loop(0, slots, key_frame, 0)
    for slot in range(slots):
        out, role = outs[slot // 2], slot % 2
        out[role, 0] = (grad_q[slot] * head**-0.5).astype(BF16)
        out[role, 1] = held[slot, 1]
        out[role, 2] = held[slot, 2]


def attend_grad_call(meta, clip, parts, grads, exact, logs, head):
    zs = len(parts)
    slots = 2 * zs
    rows, width = parts[0].shape[-2:]
    pairs = width // head
    work = slots * slots * rows * rows
    return pl.pallas_call(
        functools.partial(attend_grad_kernel, slots, head, clip),
        out_shape=[shaped((2, 3, rows, width), BF16)] * zs,
        in_specs=[SMEM] + [ANY] * slots + [VMEM, VMEM],
        out_specs=[VMEM] * zs,
        scratch_shapes=[
            pltpu.VMEM((slots, 3, rows, width), BF16),
            pltpu.VMEM((slots, rows, width), BF16),
            pltpu.VMEM((slots, pairs * rows, width), BF16),
            pltpu.VMEM((slots, pairs * rows, width), BF16),
            pltpu.VMEM((slots, 1, pairs * rows), F32),
            pltpu.VMEM((slots, rows, width), F32),
            pltpu.VMEM((rows, width), F32),
            pltpu.VMEM((rows, width), F32),
            pltpu.SemaphoreType.DMA((zs,)),
            pltpu.SemaphoreType.DMA((zs,)),
        ],
        compiler_params=params(),
        cost_estimate=cost(work * 40 * width, slots * rows * width * 20, work * pairs),
        name="attend_grad",
    )(meta, *parts, *grads, exact, logs)


def mixed_places(width, hidden):
    ends = [0]
    for columns in (width // 2, hidden // 2, width, hidden):
        ends.append(ends[-1] + columns)
    return ends


def forward_back_kernel(slots, clip, meta, tokens, cotangent, mod, proj_b, up_b, down_b, *refs):
    zs = slots // 2
    width, hidden_width = tokens.shape[-1], refs[zs + 2].shape[1]
    at_act, at_gtwo, at_hid = mixed_places(width, hidden_width)[1:4]
    parts, swapped, (proj_hbm, up_hbm, down_hbm) = refs[:zs], refs[zs], refs[zs + 1 : zs + 4]
    (
        layer_out, grad_middle_out, row_grads, up_bgrad,
        att_own, att_far, gone_low, n2_own, act_own, mixed,
        held, far, n2_other, gtwo_low, proj, up, down, slope, active, hid, sems,
    ) = refs[zs + 4 :]
    blocks = up.shape[1] // FF_BLOCK
    fetches = [pltpu.make_async_copy(proj_hbm, proj, sems.at[4])]
    for source, target, columns in ((up_hbm, up, True), (down_hbm, down, False)):
        for block in range(blocks):
            at = pl.ds(block * FF_BLOCK, FF_BLOCK)
            at = (slice(None), at) if columns else (at, slice(None))
            fetches.append(
                pltpu.make_async_copy(source.at[at], target.at[at], sems.at[4 + len(fetches)])
            )
    for fetch in fetches[:IN_FLIGHT]:
        fetch.start()

    def fetched(number):
        fetches[number].wait()
        if number + IN_FLIGHT < len(fetches):
            fetches[number + IN_FLIGHT].start()

    me = meta[0]
    parity = me % 2
    rows = tokens.shape[-2]
    lanes = width // slots
    gate_one, shift_two, scale_two, gate_two = (mod[k, clip : clip + 1] for k in range(4))
    for k in range(zs):
        held[(2 * k) ^ me] = parts[k][0]
        held[(2 * k + 1) ^ me] = swapped[k]
        far[k ^ (me // 2)] = parts[k][1]
    attended = jnp.concatenate([held[k] for k in range(slots)], axis=1)
    att_own[...] = jnp.concatenate([held[2 * k + parity] for k in range(zs)], axis=1)
    att_far[...] = jnp.concatenate([far[k] for k in range(zs)], axis=1)
    fetched(0)
    branch_one = dot_nn(attended, proj[...]) + proj_b[...].astype(F32)
    middle = tokens[...].reshape(rows, width).astype(F32) + gate_one * branch_one
    hat_two, inverse_two = norm_parts(middle)
    low_two = (hat_two * (1.0 + scale_two) + shift_two).astype(BF16)
    for block in range(slots):
        store_by_parity(
            n2_own, n2_other, slice(block // 2 * lanes, (block // 2 + 1) * lanes), parity, block,
            low_two[:, block * lanes : (block + 1) * lanes],
        )
    n2_copy = pltpu.make_async_copy(n2_other, mixed.at[:, pl.ds(0, width // 2)], sems.at[2])
    n2_copy.start()
    chunk = hidden_width // slots
    for block in range(blocks):
        at = slice(block * FF_BLOCK, (block + 1) * FF_BLOCK)
        fetched(1 + block)
        hidden = dot_nn(low_two, up[:, at]) + up_b[:, at].astype(F32)
        square = hidden * hidden
        bent = jnp.tanh(GELU_A * (hidden + GELU_B * square * hidden))
        half = 0.5 * (1.0 + bent)
        low = (hidden * half).astype(BF16)
        slope[:, at] = half + (0.5 * GELU_A) * hidden * (1.0 - bent * bent) * (
            1.0 + (3.0 * GELU_B) * square
        )
        active[:, at] = low
        for index in range(block * FF_BLOCK // chunk, (block + 1) * FF_BLOCK // chunk):
            piece = active.at[:, pl.ds(index * chunk, chunk)]
            place = pl.ds(index // 2 * chunk, chunk)

            @pl.when(parity == index % 2)
            def _():
                pltpu.make_async_copy(piece, act_own.at[:, place], sems.at[0]).start()

            @pl.when(parity != index % 2)
            def _():
                pltpu.make_async_copy(
                    piece, mixed.at[:, pl.ds(at_act + index // 2 * chunk, chunk)], sems.at[0]
                ).start()

    branch_two = down_b[...].astype(F32)
    for block in range(blocks):
        at = slice(block * FF_BLOCK, (block + 1) * FF_BLOCK)
        fetched(1 + blocks + block)
        branch_two = branch_two + dot_nn(active[:, at], down[at, :])
    layer_out[...] = (middle + gate_two * branch_two).astype(BF16)
    grad_out = cotangent[...].reshape(rows, width).astype(F32)
    low_grad_two = (grad_out * gate_two).astype(BF16)
    gtwo_low[...] = low_grad_two
    gtwo_copy = pltpu.make_async_copy(gtwo_low, mixed.at[:, pl.ds(at_gtwo, width)], sems.at[3])
    gtwo_copy.start()
    row_grads[3:4] = jnp.sum(grad_out * branch_two, axis=0, keepdims=True)
    row_grads[4:5] = jnp.sum(low_grad_two.astype(F32), axis=0, keepdims=True)
    grad_normed = None
    for block in range(blocks):
        at = slice(block * FF_BLOCK, (block + 1) * FF_BLOCK)
        low = (dot_nt(low_grad_two, down[at, :]) * slope[:, at]).astype(BF16)
        hid[:, at] = low
        pltpu.make_async_copy(
            hid.at[:, at], mixed.at[:, pl.ds(at_hid + block * FF_BLOCK, FF_BLOCK)], sems.at[1]
        ).start()
        up_bgrad[:, at] = jnp.sum(low.astype(F32), axis=0, keepdims=True)
        term = dot_nt(low, up[:, at])
        grad_normed = term if grad_normed is None else grad_normed + term
    grad_middle, grad_shift, grad_scale = norm_pull(grad_normed, hat_two, inverse_two, scale_two)
    grad_middle = grad_middle + grad_out
    grad_middle_out[...] = grad_middle
    low_grad_one = (grad_middle * gate_one).astype(BF16)
    gone_low[...] = low_grad_one
    row_grads[0:1] = jnp.sum(grad_middle * branch_one, axis=0, keepdims=True)
    row_grads[1:2] = grad_shift
    row_grads[2:3] = grad_scale
    row_grads[5:6] = jnp.sum(low_grad_one.astype(F32), axis=0, keepdims=True)
    row_grads[6:8] = jnp.zeros((2, width), F32)
    n2_copy.wait()
    gtwo_copy.wait()
    pltpu.make_async_copy(active, active, sems.at[0]).wait()
    pltpu.make_async_copy(hid, hid, sems.at[1]).wait()


def forward_back_call(
    meta, clip, tokens, cotangent, mod, proj_b, up_b, down_b, parts, swapped, proj, up, down
):
    zs = len(parts)
    slots = 2 * zs
    rows, width = tokens.shape[-2:]
    lanes = width // slots
    hidden = up.shape[1]
    half, half_hidden = width // 2, hidden // 2
    out_shape = [
        shaped((rows, width), BF16),
        shaped((rows, width), F32),
        shaped((8, width), F32),
        shaped((1, hidden), F32),
        shaped((rows, half), BF16),
        shaped((rows, half), BF16),
        shaped((rows, width), BF16),
        shaped((rows, half), BF16),
        shaped((rows, half_hidden), BF16),
        shaped((rows, mixed_places(width, hidden)[4]), BF16),
    ]
    full = lambda shape: pl.BlockSpec(shape, lambda t: (0,) * len(shape))
    pick = pl.BlockSpec((1, 1, rows, width), lambda t: (clip, 0, 0, 0))
    return pl.pallas_call(
        functools.partial(forward_back_kernel, slots, clip),
        grid=(1,),
        out_shape=out_shape,
        in_specs=[SMEM, pick, pick]
        + [full(a.shape) for a in (mod, proj_b, up_b, down_b, *parts, swapped)]
        + [ANY] * 3,
        out_specs=[ANY if k in (8, 9) else full(o.shape) for k, o in enumerate(out_shape)],
        scratch_shapes=[
            pltpu.VMEM((slots, rows, lanes), BF16),
            pltpu.VMEM((zs, rows, lanes), BF16),
            pltpu.VMEM((rows, half), BF16),
            pltpu.VMEM((rows, width), BF16),
            pltpu.VMEM(proj.shape, BF16),
            pltpu.VMEM(up.shape, BF16),
            pltpu.VMEM(down.shape, BF16),
            pltpu.VMEM((rows, hidden), F32),
            pltpu.VMEM((rows, hidden), BF16),
            pltpu.VMEM((rows, hidden), BF16),
            pltpu.SemaphoreType.DMA((5 + 2 * hidden // FF_BLOCK,)),
        ],
        compiler_params=params(),
        cost_estimate=cost(
            4 * rows * width * (width + 2 * hidden),
            4 * width * (width + 2 * hidden),
            rows * hidden,
        ),
        name="feed_forward",
    )(meta, tokens, cotangent, mod, proj_b, up_b, down_b, *parts, swapped, proj, up, down)


def proj_back_kernel(meta, near, far, proj, *outs):
    me = meta[0]
    rows, lanes = near.shape[0], outs[0].shape[2]
    groups = [pl.multiple_of((me ^ (2 * k)) * lanes, lanes) for k in range(len(outs))]
    weight = jnp.concatenate([proj[pl.ds(group, lanes), :] for group in groups], axis=0)
    both = jnp.concatenate([near[...], far[...]], axis=0)
    value = dot_nt(both, weight).astype(BF16)
    for k, out in enumerate(outs):
        for role in range(2):
            out[role] = value[role * rows : (role + 1) * rows, k * lanes : (k + 1) * lanes]


def proj_back_call(meta, near, far, proj, zs):
    rows, width = near.shape
    lanes = width // (2 * zs)
    return pl.pallas_call(
        proj_back_kernel,
        out_shape=[shaped((2, rows, lanes), BF16)] * zs,
        in_specs=[SMEM, VMEM, VMEM, VMEM],
        out_specs=[VMEM] * zs,
        compiler_params=params(),
        cost_estimate=cost(2 * rows * width * width, 2 * width * width + 6 * rows * width),
        name="proj_back",
    )(meta, near, far, proj)


def qkv_grad_kernel(zs, head, clip, meta, *refs):
    tables, refs = refs[:4], refs[4:]
    blocks = refs[zs].shape[0] // (2 * LANES)
    parts, weights = refs[:zs], refs[zs : zs + 3 * blocks]
    near_out, far_out, near_sum, far_sum, bias_out, held = refs[zs + 3 * blocks :]
    rows, width = near_sum.shape
    clips = tables[0].shape[0] // 2
    z = meta[0] // 2
    cosines = [turn_table(tables[0], tables[2], role * clips + clip, head) for role in range(2)]
    sines = [turn_table(tables[1], tables[3], role * clips + clip, head) for role in range(2)]
    for k in range(zs):
        held[k ^ z] = parts[k][...]
    totals = [None, None]
    bias_out[...] = jnp.zeros_like(bias_out)
    half = width // 2
    for kind in range(3):
        weight = jnp.concatenate([w[...] for w in weights[kind * blocks : (kind + 1) * blocks]], axis=1)
        sums = None
        for role, out in enumerate((near_out, far_out)):
            low = jnp.concatenate([held[k, role, kind] for k in range(zs)], axis=1)
            if kind < 2:
                low = turn(low.astype(F32), cosines[role], sines[role], head, True).astype(BF16)
            out[:, kind * half : (kind + 1) * half] = low
            column = jnp.sum(low.astype(F32), axis=0, keepdims=True)
            sums = column if sums is None else sums + column
            term = dot_nt(low, weight)
            totals[role] = term if totals[role] is None else totals[role] + term
        bias_out[kind : kind + 1] = sums
    near_sum[...] = totals[0]
    far_sum[...] = totals[1]


def qkv_grad_call(meta, clip, tables, parts, weight, head, aligned):
    zs = len(parts)
    rows, lanes = parts[0].shape[-2:]
    width = 2 * zs * lanes
    blocks = width // (2 * LANES)
    whole = lambda shape: pl.BlockSpec(shape, lambda t, m: (0,) * len(shape))
    out_shape = [
        shaped((rows, 3 * width // 2), BF16),
        shaped((rows, 3 * width // 2), BF16),
        shaped((rows, width), F32),
        shaped((rows, width), F32),
        shaped((8, width // 2), F32),
    ]
    return pl.pallas_call(
        functools.partial(qkv_grad_kernel, zs, head, clip),
        out_shape=out_shape,
        grid_spec=pltpu.PrefetchScalarGridSpec(
            num_scalar_prefetch=1,
            grid=(1,),
            in_specs=[whole(a.shape) for a in (*tables, *parts)]
            + half_specs(width, width, 2 * zs, aligned),
            out_specs=[whole(o.shape) for o in out_shape],
            scratch_shapes=[pltpu.VMEM((zs, 2, 3, rows, lanes), BF16)],
        ),
        compiler_params=params(),
        cost_estimate=cost(6 * rows * width * width, 3 * width * width + 20 * rows * width),
        name="qkv_grad",
    )(meta, *tables, *parts, *[weight] * (3 * blocks))


def norm_grad_kernel(tokens, mod, *refs):
    clips = tokens.shape[0]
    nears, fars, middles = refs[:clips], refs[clips : 2 * clips], refs[2 * clips : 3 * clips]
    tokens_grad, row_grads = refs[3 * clips :]
    for c in range(clips):
        hat, inverse = norm_parts(tokens[c, 0].astype(F32))
        grad, shift, scale = norm_pull(
            nears[c][...] + fars[c][...], hat, inverse, mod[1, c : c + 1]
        )
        tokens_grad[c, 0] = grad + middles[c][...]
        row_grads[c, 0:1] = shift
        row_grads[c, 1:2] = scale
        row_grads[c, 2:8] = jnp.zeros((6, tokens.shape[-1]), F32)


def norm_grad_call(tokens, mod, nears, fars, middles):
    clips, _, rows, width = tokens.shape
    return pl.pallas_call(
        norm_grad_kernel,
        out_shape=[shaped(tokens.shape, F32), shaped((clips, 8, width), F32)],
        in_specs=[VMEM] * (2 + 3 * clips),
        out_specs=[VMEM, VMEM],
        compiler_params=params(),
        cost_estimate=cost(clips * rows * width * 30, clips * rows * width * 18),
        name="norm_grad",
    )(tokens, mod, *nears, *fars, *middles)


def weight_grad_kernel(jobs, clip_size, zs, meta, *refs):
    arrays_n = sum(2 * job[0] for job in jobs)
    arrays, outs = refs[:arrays_n], refs[arrays_n : arrays_n + 4]
    held, out_sems, in_sems = refs[arrays_n + 4 : arrays_n + 7]
    scratch = refs[arrays_n + 7 :]
    _, _, _, height, cols = held.shape
    tile = zs * height
    z = meta[0] // 2
    clip = meta[1]

    def send_out(slot, tiles, repeat, first, tall):
        for e in range(clip_size):
            for half, first_bit in enumerate((1, clip_size // 2)):
                keep, send = outs[2 * half], outs[2 * half + 1]
                rest = [k for k in range(clip_size) if not k & first_bit]
                if e & first_bit:
                    out, place = send, rest.index(e ^ first_bit)
                else:
                    out, place = keep, rest.index(e)
                low, high = half * zs // 2, (half + 1) * zs // 2
                if not tall:
                    pltpu.make_async_copy(
                        held.at[slot, e, pl.ds(low, zs // 2)],
                        out.at[place, :, pl.ds(first, height)],
                        out_sems.at[slot],
                    ).start()
                    continue
                for block in range(zs):
                    row = repeat * zs + block
                    k = row // tiles
                    if low <= k < high:
                        pltpu.make_async_copy(
                            held.at[slot, e, block],
                            out.at[place, k - low, pl.ds(first + row % tiles * height, height)],
                            out_sems.at[slot],
                        ).start()

    copies = []
    at = 0
    for job, (count, _, _, _, _, places) in enumerate(jobs):
        left, right = scratch[2 * job : 2 * job + 2]
        depth = left.shape[0] // count
        for n in range(2 * count):
            target = left if n < count else right
            source = arrays[at + n]
            if source.shape[1] != target.shape[1]:
                source = source.at[:, pl.ds(places[n], target.shape[1])]
            copies.append(
                pltpu.make_async_copy(
                    source,
                    target.at[pl.ds(n % count * depth, depth)],
                    in_sems.at[at + n],
                )
            )
        at += 2 * count
    for copy in copies:
        copy.start()

    at = number = 0
    for job, (count, lane_parts, tall, tiles, first, _) in enumerate(jobs):
        left, right = scratch[2 * job : 2 * job + 2]
        block = left.shape[1] // zs
        for n in range(2 * count):
            copies[at + n].wait()
        at += 2 * count
        wide = right.shape[1] // (tiles * lane_parts if not tall else 1)
        part = wide // clip_size
        for repeat in range(tiles):
            slot = number % 2
            if number >= 2:
                pltpu.make_async_copy(held.at[slot], held.at[slot], out_sems.at[slot]).wait()
            for lane_part in range(lane_parts):
                if tall:
                    per = zs // tiles
                    rows = [
                        left[:, pl.ds(pl.multiple_of(((repeat * per + n) ^ z) * block, block), block)]
                        for n in range(per)
                    ]
                    rows = rows[0] if per == 1 else jnp.concatenate(rows, axis=1)
                    value = dot_tn(rows, right[...]).astype(BF16)
                else:
                    group = repeat + lane_part
                    value = dot_tn(
                        left[...], right[:, group * wide : (group + 1) * wide]
                    ).astype(BF16)
                for p in range(clip_size):
                    lanes = slice(lane_part * part, (lane_part + 1) * part)
                    piece = value[:, p * part : (p + 1) * part]
                    for k in range(zs):
                        source = piece[k * height : (k + 1) * height]
                        held[slot, p ^ clip, k if tall else k ^ z, :, lanes] = source
            send_out(slot, tiles, repeat, first if tall else first + repeat * height, tall)
            number += 1
    for slot in range(min(number, 2)):
        pltpu.make_async_copy(held.at[slot], held.at[slot], out_sems.at[slot]).wait()


def weight_grad_call(meta, products, clip_size, zs, name):
    jobs, arrays, scratch = [], [], []
    first = flops = 0
    tile = min(p[0][0][2] for p in products)
    height = tile // zs
    piece = None
    for lefts, rights, lane_parts, tall in products:
        depth, total = rights[0][0].shape[0], rights[0][2]
        rows = lefts[0][2]
        if tall:
            tiles, piece = rows // tile, total // clip_size
        elif lane_parts > 1:
            tiles, piece = 1, total // clip_size
        else:
            tiles, piece = total // (2 * tile), 2 * tile // clip_size
        count = len(lefts)
        places = tuple(a[1] for a in lefts + rights)
        jobs.append((count, lane_parts, tall, tiles, first, places))
        first += height * tiles
        arrays += [a[0] for a in lefts + rights]
        flops += 2 * count * depth * rows * total
        scratch += [
            pltpu.VMEM((count * depth, rows), BF16),
            pltpu.VMEM((count * depth, total), BF16),
        ]
    out = shaped((clip_size // 2, zs // 2, first, piece), BF16)
    return pl.pallas_call(
        functools.partial(weight_grad_kernel, tuple(jobs), clip_size, zs),
        out_shape=[out] * 4,
        in_specs=[SMEM] + [ANY] * len(arrays),
        out_specs=[ANY] * 4,
        scratch_shapes=[
            pltpu.VMEM((2, clip_size, zs, height, piece), BF16),
            pltpu.SemaphoreType.DMA((2,)),
            pltpu.SemaphoreType.DMA((len(arrays),)),
        ]
        + scratch,
        compiler_params=params(),
        cost_estimate=cost(flops, flops / 512 + 8 * out.size),
        name=name,
    )(meta, *arrays)


def place_kernel(jobs, pieces, meta, *refs):
    parts, outs = refs[:pieces], refs[pieces:]
    clip = meta[1]
    cols = parts[0].shape[1]
    for e in range(pieces):
        first = 0
        for out, (height, repeats, tall) in zip(outs, jobs):
            for repeat in range(repeats):
                base = 0 if tall else repeat * cols * pieces
                target = pl.ds(pl.multiple_of(base + (clip ^ e) * cols, cols), cols)
                value = parts[e][first : first + height].astype(F32)
                if tall:
                    out[repeat * height : (repeat + 1) * height, target] = value
                else:
                    out[:, target] = value
                first += height


def place_call(meta, parts, jobs, outs):
    return pl.pallas_call(
        functools.partial(place_kernel, jobs, len(parts)),
        out_shape=outs,
        in_specs=[SMEM] + [VMEM] * len(parts),
        out_specs=[VMEM] * len(outs),
        compiler_params=params(),
        cost_estimate=cost(0, sum(o.size * 4 for o in outs)),
        name="place_grads",
    )(meta, *parts)


def place_qkv_kernel(meta, *refs):
    parts, out = refs[:-1], refs[-1]
    parity, clip = meta[0] % 2, meta[1]
    thirds = out.shape[1] // 3
    for e, part in enumerate(parts):
        for role in range(2):
            block = 2 * (clip ^ e) + (parity ^ role)
            for kind in range(3):
                at = pl.ds(pl.multiple_of(kind * thirds + block * LANES, LANES), LANES)
                out[:, at] = part[role, :, kind * LANES : (kind + 1) * LANES].astype(F32)


def place_qkv_call(meta, parts, out):
    return pl.pallas_call(
        place_qkv_kernel,
        out_shape=out,
        in_specs=[SMEM] + [VMEM] * len(parts),
        out_specs=VMEM,
        compiler_params=params(),
        cost_estimate=cost(0, out.size * 6),
        name="place_qkv_grad",
    )(meta, *parts)


def exchange(array, axis, size, distance):
    return lax.ppermute(array, axis, [(k, k ^ distance) for k in range(size)])


def after(value, *others):
    return lax.optimization_barrier((value, *others))


def spread(slots_out, seq_size):
    return [slots_out[0]] + [
        exchange(slots_out[k], "seq", seq_size, 2 * k) for k in range(1, seq_size // 2)
    ]


def add_low(left, right):
    return (left.astype(F32) + right.astype(F32)).astype(BF16)


def step_out(pairs, bits, size):
    return [exchange(send, "clip", size, bit) for (_, send), bit in zip(pairs, bits)]


def step_in(pairs, arrived):
    left = []
    for (keep, _), new in zip(pairs, arrived):
        half = keep.shape[0] // 2
        if half:
            left.append((add_low(keep[:half], new[:half]), add_low(keep[half:], new[half:])))
        else:
            left.append((add_low(keep[0], new[0]), None))
    return left


def clip_orders(clip_size):
    down = [1 << k for k in reversed(range(clip_size.bit_length() - 1))]
    return [1] + down[:-1], down


def sum_z(pairs, seq_size):
    blocks = [*pairs[0][0], *pairs[1][0]]
    bit = 1
    while len(blocks) > 1:
        kept, sent = blocks[0::2], blocks[1::2]
        arrived = exchange(jnp.stack(sent), "seq", seq_size, 2 * bit)
        blocks = [add_low(keep, new) for keep, new in zip(kept, arrived)]
        bit *= 2
    return blocks[0]


def gather_pieces(piece, clip_size):
    return [piece] + [exchange(piece, "clip", clip_size, d) for d in range(1, clip_size)]


def double(array, axis, size):
    bit = 1
    while bit < size:
        array = jnp.concatenate([array, exchange(array, axis, size, bit)])
        bit *= 2
    return array


def silu_act(values_in):
    return values_in * jax.nn.sigmoid(values_in)


def rotary_tables(stamps, patch_count, head):
    lane = jnp.arange(LANES, dtype=jnp.int32)
    quarter = head // 4
    freqs = 10000.0 ** (-(lane % quarter).astype(F32) / quarter)
    sign = jnp.where(lane % head < head // 2, -1.0, 1.0).astype(F32)
    tables = []
    for places in (stamps, jnp.arange(patch_count, dtype=jnp.int32)):
        angles = places.astype(F32)[:, None] * freqs[None, :]
        tables += [jnp.cos(angles), jnp.sin(angles) * sign[None, :]]
    return tables


def on_device(
    tokens,
    cotangent,
    context_count,
    noise_level,
    frame_time,
    level_table,
    mod_weight,
    mod_bias,
    qkv_weight,
    qkv_bias,
    proj_weight,
    proj_bias,
    up_weight,
    up_bias,
    down_weight,
    down_bias,
):
    seq_size, clip_size = lax.axis_size("seq"), lax.axis_size("clip")
    me, mine = lax.axis_index("seq"), lax.axis_index("clip")
    clips, _, rows, width = tokens.shape
    head = width // HEADS
    hidden = up_weight.shape[1]
    zs = seq_size // 2
    me = me.astype(jnp.int32)
    mine = mine.astype(jnp.int32)
    parity = me % 2
    aligned = (width // seq_size) % LANES == 0
    stamps = jnp.stack([noise_level[:, 0], frame_time[:, 0]])
    other_stamps = exchange(stamps, "seq", seq_size, 1)
    other_tokens = exchange(tokens, "seq", seq_size, 1)
    meta = jnp.concatenate([jnp.stack([me, mine]), context_count])
    levels = jnp.concatenate(
        [
            jnp.where(me < context_count, 0, stamps[0]),
            jnp.where((me ^ 1) < context_count, 0, other_stamps[0]),
        ]
    )
    levels_used = levels[:clips]
    mod_bias_row = mod_bias[None]
    mod_one, condition = modulation_call(levels, level_table, mod_weight, mod_bias_row, 0, 2)
    condition = condition[:clips]
    tables = rotary_tables(jnp.concatenate([stamps[1], other_stamps[1]]), rows, head)
    qkv_bias_row = qkv_bias[None]
    if aligned:
        weight_half, bias_half = qkv_weight, qkv_bias_row
    else:
        weight_half = half_columns(qkv_weight, seq_size, parity)
        bias_half = half_columns(qkv_bias_row, seq_size, parity)

    swap = lambda array: exchange(array, "seq", seq_size, 1)
    full = lambda array: (array, 0, array.shape[1])
    at_n2, at_act, at_gtwo, at_hid, _ = mixed_places(width, hidden)
    out = qkv_call(
        meta, tokens, other_tokens, mod_one, tables, weight_half, bias_half, zs, head, aligned
    )
    normed = out[zs * clips :]
    parts = [spread(out[:zs], seq_size)]
    mod_two, _ = modulation_call(
        levels[:clips], level_table, mod_weight, mod_bias_row, 2, 4
    )
    parts[0], mod_two = after(parts[0], mod_two)
    exact, logs, attended, crossed = [], [], [], []
    for c in range(clips):
        sends = out[(c + 1) * zs : (c + 2) * zs] if c < clips - 1 else None
        if c < clips - 1:
            parts[c], sends = after(parts[c], sends)
            parts.append(spread(sends, seq_size))
        done = attend_call(meta, c, parts[c], head)
        exact.append(done[zs])
        logs.append(done[zs + 1])
        sends = done[:zs]
        if c < clips - 1:
            sends, parts[c + 1] = after(sends, parts[c + 1])
        if c:
            sends, attended[-1] = after(sends, attended[-1])
            crossed.append(swap(jnp.stack([a[1] for a in attended[-1]])))
        attended.append(spread(sends, seq_size))
    layer, middles, row_grads, up_bgrads, saved, mixed, far_ones, grads = ([] for _ in range(8))
    for c in range(clips):
        if c:
            meta, grads[-1][0] = after(meta, grads[-1][0])
        out = forward_back_call(
            meta, c, tokens, cotangent, mod_two, proj_bias[None], up_bias[None],
            down_bias[None], attended[c], crossed[c], proj_weight, up_weight, down_weight,
        )
        layer.append(out[0])
        middles.append(out[1])
        row_grads.append(out[2])
        up_bgrads.append(out[3])
        gone, mine_mixed = out[6], out[9]
        if c < clips - 1:
            gone, mine_mixed, attended[c + 1] = after(gone, mine_mixed, attended[c + 1])
            crossed.append(swap(jnp.stack([a[1] for a in attended[c + 1]])))
        if c:
            gone, mine_mixed, grads[-1], mixed[-1] = after(gone, mine_mixed, grads[-1], mixed[-1])
        far_ones.append(swap(gone))
        if c < clips - 1:
            far_ones[-1], crossed[-1] = after(far_ones[-1], crossed[-1])
        saved.append((out[4], out[5], gone, out[7], out[8]))
        back = list(proj_back_call(meta, gone, far_ones[c], proj_weight, zs))
        back[0], mine_mixed = after(back[0], mine_mixed)
        mixed.append([mine_mixed, swap(mine_mixed)])
        grads.append(spread(back, seq_size))
    row = width // seq_size
    orders = clip_orders(clip_size)
    steps = len(orders[0])
    returned = []
    for c in range(clips):
        if c:
            meta, shares[0] = after(meta, shares[0])
        else:
            meta, grads[-1][0] = after(meta, grads[-1][0])
        out = attend_grad_call(meta, c, parts[c], grads[c], exact[c], logs[c], head)
        if c < clips - 1:
            out, grads[-1], mixed[-1] = after(out, grads[-1], mixed[-1])
        else:
            out, returned[-1] = after(out, returned[-1])
        returned.append(spread(out, seq_size))
        if c == 0:
            products = [([], [], 1, False), ([], [], 1, True), ([], [], 1, False)]
            for k in range(clips):
                att_own, att_far, gone, n2_own, act_own = saved[k]
                own, far = mixed[k]
                products[0][0].extend([full(att_own), full(att_far)])
                products[0][1].extend([full(gone), full(far_ones[k])])
                products[1][0].extend([full(act_own), (far, at_act, hidden // 2)])
                products[1][1].extend([(own, at_gtwo, width), (far, at_gtwo, width)])
                products[2][0].extend([full(n2_own), (far, at_n2, width // 2)])
                products[2][1].extend([(own, at_hid, hidden), (far, at_hid, hidden)])
            shares = weight_grad_call(meta, products, clip_size, zs, "weight_grads")
            shares = list(shares)
    pairs = [shares[:2], shares[2:]]
    turns = list(zip(*orders))
    grad_rights, nears, fars, qkv_bgrads = [], [], [], []
    for c in range(clips):
        if c:
            kept = [pair[0] for pair in pairs]
            kept, qkv_bgrads[0] = after(kept, qkv_bgrads[0])
            pairs = [(keep, pair[1]) for keep, pair in zip(kept, pairs)]
            pairs = step_in(pairs, step_out(pairs, turns[0], clip_size))
            meta, pairs, returned[c] = after(meta, pairs, returned[c])
        else:
            meta, returned[-1][0] = after(meta, returned[-1][0])
        out = qkv_grad_call(meta, c, tables, returned[c], weight_half, head, aligned)
        grad_rights.extend(out[:2])
        nears.append(out[2])
        fars.append(swap(out[3]))
        qkv_bgrads.append(out[4][:3])
    tokens_grad, late_rows = norm_grad_call(tokens, mod_one, nears, fars, middles)
    if len(turns) > 1:
        arrived = step_out(pairs, turns[1], clip_size)
        tokens_grad, arrived = after(tokens_grad, arrived)
        pairs = step_in(pairs, arrived)
    for bits in turns[2:]:
        pairs = step_in(pairs, step_out(pairs, bits, clip_size))
    level_rows = jnp.stack([levels_used // 32, levels_used % 32]).astype(F32)
    level_rows = jnp.concatenate([level_rows, jnp.zeros((2, width - clips), F32)], axis=1)
    mod_rows = []
    for c in range(clips):
        mod_rows += [late_rows[c, 0:2], row_grads[c][0:4]]
    bias_rows = [
        sum(qkv_bgrads).reshape(3 * width // 2),
        jnp.zeros((width // 2,), F32),
        sum(up_bgrads).reshape(hidden),
        sum(r[4] for r in row_grads),
        sum(r[5] for r in row_grads),
    ]
    bias_rows = jnp.concatenate(bias_rows).reshape(-1, width)
    late = jnp.concatenate([condition, level_rows] + mod_rows + [bias_rows], axis=0)
    start, stop = clips + 2, clips + 2 + 6 * clips
    late = double(late.astype(BF16)[None], "seq", seq_size)
    pairs, late = after(pairs, late)
    piece = sum_z(pairs, seq_size)
    lefts = [normed[role * clips + c] for c in range(clips) for role in range(2)]
    if aligned:
        meta, late_rows = after(meta, late_rows)
        shares = weight_grad_call(
            meta,
            [([full(a) for a in lefts], [full(a) for a in grad_rights], 3, False)],
            clip_size,
            zs,
            "qkv_weight_grad",
        )
        pairs_qkv = [shares[:2], shares[2:]]
        arrived = step_out(pairs_qkv, turns[0], clip_size)
        arrived, late = after(arrived, late)
        pairs_qkv = step_in(pairs_qkv, arrived)
        for bits in turns[1:]:
            pairs_qkv = step_in(pairs_qkv, step_out(pairs_qkv, bits, clip_size))
    own_sums = jnp.sum(
        late[:, stop:].astype(F32).reshape(zs, 2, late.shape[1] - stop, width), axis=0
    ).astype(BF16)
    sums_rows = 2 * own_sums.shape[1]
    message = jnp.concatenate(
        [late[:, :stop].reshape(seq_size * stop, width), own_sums.reshape(sums_rows, width)]
    )
    late = double(message[None], "clip", clip_size)
    if aligned:
        pairs_qkv, piece, late = after(pairs_qkv, piece, late)
    own_sums = jnp.sum(late[:, seq_size * stop :].astype(F32), axis=0).reshape(2, -1)
    late = late[:, : seq_size * stop].reshape(clip_size * seq_size, stop, width)
    devices = clip_size * seq_size
    grad_modulation = late[:, start:].reshape(devices * clips, 6 * width)
    half_bias = own_sums[:, : 3 * width // 2].reshape(2, 3, zs, 1, width // seq_size)
    bias_sums = jnp.sum(own_sums, axis=0)[2 * width :]
    qkv_bias_sums = jnp.where(
        parity == 0,
        jnp.concatenate([half_bias[0], half_bias[1]], axis=2),
        jnp.concatenate([half_bias[1], half_bias[0]], axis=2),
    ).reshape(3 * width)
    all_condition = late[:, :clips].reshape(devices * clips, width).astype(F32)
    codes = late[:, clips:start, :clips].astype(jnp.int32)
    all_levels = (codes[:, 0] * 32 + codes[:, 1]).reshape(devices * clips)
    all_active, silu_pull = jax.vjp(silu_act, all_condition)
    my_active = lax.dynamic_slice_in_dim(all_active, me * row, row, axis=1).astype(BF16)
    mod_wgrad = lax.dot_general(
        my_active, grad_modulation, (((0,), (0,)), ((), ())), preferred_element_type=F32
    )
    (grad_condition,) = silu_pull(
        lax.dot_general(
            grad_modulation, mod_weight, (((1,), (1,)), ((), ())), preferred_element_type=F32
        )
    )
    table_row = level_table.shape[0] // seq_size
    onehot = (
        all_levels[:, None] == (me * table_row + jnp.arange(table_row, dtype=jnp.int32))[None, :]
    ).astype(F32)
    table_grad = lax.dot_general(
        onehot,
        grad_condition,
        (((0,), (0,)), ((), ())),
        precision=HIGHEST_PRECISION,
        preferred_element_type=F32,
    )
    mod_sums = jnp.sum(grad_modulation.astype(F32), axis=0)

    def own_part(vector):
        size = vector.shape[0] // seq_size
        return lax.dynamic_slice_in_dim(vector, me * size, size, axis=0)

    mod_bgrad = own_part(mod_sums)
    qkv_bgrad = own_part(qkv_bias_sums)
    up_bgrad = own_part(bias_sums[:hidden])
    down_bgrad = own_part(bias_sums[hidden : hidden + width])
    proj_bgrad = own_part(bias_sums[hidden + width : hidden + 2 * width])
    if aligned:
        pieces = gather_pieces(piece, clip_size)
        piece = sum_z(pairs_qkv, seq_size).reshape(2, row, 3 * LANES)
        own_rows = lax.dynamic_index_in_dim(piece, parity, 0, keepdims=False)
        far_rows = swap(lax.dynamic_index_in_dim(piece, 1 - parity, 0, keepdims=False))
        far_rows, pieces, mod_wgrad, table_grad = after(far_rows, pieces, mod_wgrad, table_grad)
        pieces_qkv = gather_pieces(jnp.stack([own_rows, far_rows]), clip_size)
    else:
        pieces = gather_pieces(piece, clip_size)
        share = sum(
            lax.dot_general(left, right, (((0,), (0,)), ((), ())), preferred_element_type=F32)
            for left, right in zip(lefts, grad_rights)
        ).astype(BF16)
        share = share.reshape(width, 3, zs, 1, width // seq_size)
        blank = jnp.zeros_like(share)
        share = jnp.where(
            parity == 0,
            jnp.concatenate([share, blank], axis=3),
            jnp.concatenate([blank, share], axis=3),
        ).reshape(width, 3 * width)
        qkv_wgrad = lax.psum(
            lax.psum_scatter(share, "seq", scatter_dimension=0, tiled=True), "clip"
        ).astype(F32)

    proj_wgrad, down_wgrad, up_wgrad = place_call(
        meta,
        pieces,
        (
            (row, 1, False),
            (row, hidden // width, True),
            (row, hidden // width, False),
        ),
        [shaped((row, width), F32), shaped((hidden // seq_size, width), F32), shaped((row, hidden), F32)],
    )
    if aligned:
        pieces_qkv, proj_wgrad = after(pieces_qkv, proj_wgrad)
        qkv_wgrad = place_qkv_call(meta, pieces_qkv, shaped((row, 3 * width), F32))
    layer_out = jnp.stack(layer)[:, None]
    return (
        layer_out,
        tokens_grad,
        table_grad,
        mod_wgrad,
        mod_bgrad,
        qkv_wgrad,
        qkv_bgrad,
        proj_wgrad,
        proj_bgrad,
        up_wgrad,
        up_bgrad,
        down_wgrad,
        down_bgrad,
    )


def solution(mesh):
    placed = (
        P("clip", "seq", None, None),
        P("clip", "seq", None, None),
        P("clip"),
        P("clip", "seq"),
        P("clip", "seq"),
    ) + (P(),) * 11
    return jax.shard_map(
        on_device,
        mesh=mesh,
        in_specs=placed,
        out_specs=(
            P("clip", "seq", None, None),
            P("clip", "seq", None, None),
            P("seq", None),
            P("seq", None),
            P("seq"),
            P("seq", None),
            P("seq"),
            P("seq", None),
            P("seq"),
            P("seq", None),
            P("seq"),
            P("seq", None),
            P("seq"),
        ),
        check_vma=False,
    )
```

```python
import functools

import jax
import jax.numpy as jnp
from jax import lax
from jax.experimental import pallas as pl
from jax.experimental.pallas import tpu as pltpu
from jax.sharding import PartitionSpec as P

HEADS = 16
EPS = 1e-06
HIGHEST_PRECISION = lax.Precision.HIGHEST
F32 = jnp.float32
BF16 = jnp.bfloat16
ANY = pl.BlockSpec(memory_space=pltpu.HBM)
VMEM = pl.BlockSpec(memory_space=pltpu.VMEM)
SMEM = pl.BlockSpec(memory_space=pltpu.SMEM)
LANES = 128
BLOCK = 256
FF_BLOCK = 1024
IN_FLIGHT = 3
GROUPS = (8, 4, 2, 1)
GELU_A = 0.7978845608028654
GELU_B = 0.044715
WEIGHT = 1.0
VMEM_BYTES = 62 << 20


def shaped(shape, dtype):
    return jax.ShapeDtypeStruct(shape, dtype)


def params():
    return pltpu.CompilerParams(vmem_limit_bytes=VMEM_BYTES)


def cost(flops, moved, transcendentals=0):
    return pl.CostEstimate(
        flops=int(flops * WEIGHT),
        bytes_accessed=int(moved * WEIGHT),
        transcendentals=int(transcendentals * WEIGHT),
    )


def dot_nn(left, right):
    return lax.dot_general(left, right, (((1,), (0,)), ((), ())), preferred_element_type=F32)


def dot_nt(left, right):
    return lax.dot_general(left, right, (((1,), (1,)), ((), ())), preferred_element_type=F32)


def dot_tn(left, right):
    return lax.dot_general(left, right, (((0,), (0,)), ((), ())), preferred_element_type=F32)


def split_heads(values, pairs, head):
    if pairs == 1:
        return [values]
    lane = lax.broadcasted_iota(jnp.int32, values.shape, 1)
    return [jnp.where(lane // head == h, values, jnp.zeros_like(values)) for h in range(pairs)]


def swap_halves(values, head):
    half = head // 2
    lane = lax.broadcasted_iota(jnp.int32, values.shape, 1)
    ahead = pltpu.roll(values, values.shape[1] - half, 1)
    behind = pltpu.roll(values, half, 1)
    return jnp.where(lax.rem(lane, head) < half, ahead, behind)


def turn(values, cosine, signed_sine, head, back):
    parts = []
    for at in range(0, values.shape[1], LANES):
        piece = values[:, at : at + LANES]
        other = swap_halves(piece, head) * signed_sine
        parts.append(piece * cosine - other if back else piece * cosine + other)
    return jnp.concatenate(parts, axis=1)


def norm_parts(values):
    center = jnp.mean(values, axis=-1, keepdims=True)
    offset = values - center
    spread = jnp.mean(offset * offset, axis=-1, keepdims=True)
    inverse = lax.rsqrt(spread + EPS)
    return offset * inverse, inverse


def norm_pull(grad, hat, inverse, scale_row):
    grad_shift = jnp.sum(grad, axis=0, keepdims=True)
    grad_scale = jnp.sum(grad * hat, axis=0, keepdims=True)
    inner = grad * (1.0 + scale_row)
    mean_one = jnp.mean(inner, axis=-1, keepdims=True)
    mean_two = jnp.mean(inner * hat, axis=-1, keepdims=True)
    return inverse * (inner - mean_one - hat * mean_two), grad_shift, grad_scale


def store_by_parity(own_ref, other_ref, where, parity, block_index, value):
    own = parity == block_index % 2

    @pl.when(own)
    def _():
        own_ref[:, where] = value

    @pl.when(jnp.logical_not(own))
    def _():
        other_ref[:, where] = value


def modulation_kernel(meta, table, weight, bias, out, condition_out, low):
    rows, levels = out.shape[1], table.shape[0]

    @pl.when(pl.program_id(0) == 0)
    def _():
        lane = lax.broadcasted_iota(jnp.int32, (1, levels), 1)
        picked = jnp.concatenate(
            [jnp.where(lane == meta[row], 1.0, 0.0) for row in range(rows)], axis=0
        )
        condition = dot_nn(picked.astype(BF16), table[...])
        condition_out[...] = condition
        low[...] = silu_act(condition).astype(BF16)

    out[0] = dot_nn(low[...], weight[...]) + bias[...].astype(F32)


def modulation_call(levels, table, weight, bias, first, parts):
    rows, width = levels.shape[0], table.shape[1]
    return pl.pallas_call(
        modulation_kernel,
        grid=(parts,),
        out_shape=[shaped((parts, rows, width), F32), shaped((rows, width), F32)],
        in_specs=[
            SMEM,
            pl.BlockSpec(table.shape, lambda t: (0, 0)),
            pl.BlockSpec((width, width), lambda t: (0, first + t)),
            pl.BlockSpec((1, width), lambda t: (0, first + t)),
        ],
        out_specs=[
            pl.BlockSpec((1, rows, width), lambda t: (t, 0, 0)),
            pl.BlockSpec((rows, width), lambda t: (0, 0)),
        ],
        scratch_shapes=[pltpu.VMEM((rows, width), BF16)],
        compiler_params=params(),
        cost_estimate=cost(0, 2 * (parts + 1) * width * width),
        name="modulation",
    )(levels, table, weight, bias)


def turn_table(temporal, spatial, row, head):
    lane = lax.broadcasted_iota(jnp.int32, spatial.shape, 1)
    timed = lax.rem(lane, head // 2) < head // 4
    return jnp.where(timed, temporal[row : row + 1], spatial[...])


def half_columns(weight, groups, parity):
    rows, total = weight.shape
    view = weight.reshape(rows, 3, groups // 2, 2, total // (3 * groups))
    return lax.dynamic_index_in_dim(view, parity, 3, keepdims=False).reshape(rows, total // 2)


def half_specs(height, width, groups, aligned):
    specs = []
    for kind in range(3):
        for block in range(width // (2 * LANES)):
            if aligned:
                specs.append(
                    pl.BlockSpec(
                        (height, LANES), lambda t, m, k=kind, b=block: (0, k * groups + 2 * b + m[0] % 2)
                    )
                )
            else:
                specs.append(
                    pl.BlockSpec(
                        (height, LANES),
                        lambda t, m, k=kind, b=block: (0, k * (width // (2 * LANES)) + b),
                    )
                )
    return specs


def qkv_kernel(zs, head, meta, tokens, other_tokens, mod, *refs):
    tables, refs = refs[:4], refs[4:]
    blocks = tokens.shape[-1] // (2 * LANES)
    weights, biases = refs[: 3 * blocks], refs[3 * blocks : 6 * blocks]
    clips, _, rows, width = tokens.shape
    outs = refs[6 * blocks : 6 * blocks + zs * clips]
    normed_outs, (normed, held) = refs[6 * blocks + zs * clips : -2], refs[-2:]
    cosines = [turn_table(tables[0], tables[2], row, head) for row in range(2 * clips)]
    sines = [turn_table(tables[1], tables[3], row, head) for row in range(2 * clips)]
    lanes = width // (2 * zs)
    z = meta[0] // 2
    for row in range(2 * clips):
        role, clip = row // clips, row % clips
        source = (tokens, other_tokens)[role]
        hat, _ = norm_parts(source[clip, 0].astype(F32))
        low = (hat * (1.0 + mod[1, row : row + 1]) + mod[0, row : row + 1]).astype(BF16)
        normed[row * rows : (row + 1) * rows] = low
        normed_outs[row][...] = low
    for kind in range(3):
        pick = slice(kind * blocks, (kind + 1) * blocks)
        weight = jnp.concatenate([w[...] for w in weights[pick]], axis=1)
        bias = jnp.concatenate([b[...] for b in biases[pick]], axis=1).astype(F32)
        value = dot_nn(normed[...], weight) + bias
        for row in range(2 * clips):
            role, clip = row // clips, row % clips
            part = value[row * rows : (row + 1) * rows]
            if kind < 2:
                part = turn(part, cosines[row], sines[row], head, False)
            part = part.astype(BF16)
            if kind == 0:
                part = part * jnp.asarray(head**-0.5, BF16)
            for group in range(zs):
                held[clip, group ^ z, role, kind] = part[:, group * lanes : (group + 1) * lanes]
    for n, out in enumerate(outs):
        out[...] = held[n // zs, n % zs]


def qkv_call(meta, tokens, other_tokens, mod, tables, weight, bias, zs, head, aligned):
    clips, _, rows, width = tokens.shape
    lanes = width // (2 * zs)
    whole = lambda shape: pl.BlockSpec(shape, lambda t, m: (0,) * len(shape))
    blocks = width // (2 * LANES)
    message = (2, 3, rows, lanes)
    out_shape = [shaped(message, BF16)] * (zs * clips)
    out_shape += [shaped((rows, width), BF16)] * (2 * clips)
    return pl.pallas_call(
        functools.partial(qkv_kernel, zs, head),
        out_shape=out_shape,
        grid_spec=pltpu.PrefetchScalarGridSpec(
            num_scalar_prefetch=1,
            grid=(1,),
            in_specs=[whole(a.shape) for a in (tokens, other_tokens, mod, *tables)]
            + half_specs(width, width, 2 * zs, aligned)
            + half_specs(1, width, 2 * zs, aligned),
            out_specs=[whole(o.shape) for o in out_shape],
            scratch_shapes=[
                pltpu.VMEM((2 * clips * rows, width), BF16),
                pltpu.VMEM((clips, zs, *message), BF16),
            ],
        ),
        compiler_params=params(),
        cost_estimate=cost(
            6 * clips * rows * width * width, 3 * width * width + 32 * rows * width
        ),
        name="norm_qkv",
    )(meta, tokens, other_tokens, mod, *tables, *[weight] * (3 * blocks), *[bias] * (3 * blocks))


def attend_kernel(slots, head, clip, meta, *refs):
    zs = slots // 2
    parts, outs = refs[:zs], refs[zs:slots]
    exact, logs, held, scores, values, sems = refs[slots:]
    copies = [
        pltpu.make_async_copy(parts[k], held.at[pl.ds(2 * k, 2)], sems.at[k])
        for k in range(zs)
    ]
    for copy in copies:
        copy.start()
    for copy in copies:
        copy.wait()
    me, context = meta[0], meta[2 + clip]
    rows, width = held.shape[2], held.shape[3]
    pairs = width // head

    def prepare(frame, _):
        split = split_heads(held[frame ^ me, 2], pairs, head)
        ones = split_heads(jnp.ones((rows, width), BF16), pairs, head)
        for h in range(pairs):
            values[frame, h] = jnp.concatenate([split[h], ones[h]], axis=1)
        return 0

    lax.fori_loop(0, slots, prepare, 0)

    def attend(slot, count):
        queries = split_heads(held[slot, 0], pairs, head)
        total, tops = None, []
        for h in range(pairs):
            peak = None
            for frame in range(count):
                score = dot_nt(queries[h], held[frame ^ me, 1])
                scores[frame, h * rows : (h + 1) * rows] = score
                for at in range(0, rows, LANES):
                    piece = score[:, at : at + LANES]
                    peak = piece if peak is None else jnp.maximum(peak, piece)
            top = jnp.max(peak, axis=1, keepdims=True)
            tops.append(top)
            for frame in range(count):
                power = jnp.exp(scores[frame, h * rows : (h + 1) * rows] - top).astype(BF16)
                term = dot_nn(power, values[frame, h])
                total = term if total is None else total + term
        weight_sum = total[:, width:]
        result = total[:, :width] / weight_sum
        exact[slot] = result
        top = jnp.broadcast_to(tops[0], (rows, width))
        if pairs > 1:
            lane = lax.broadcasted_iota(jnp.int32, (rows, width), 1)
            for h in range(1, pairs):
                top = jnp.where(lane // head >= h, tops[h], top)
        turned = (top + jnp.log(weight_sum)).T
        logs[slot] = jnp.concatenate(
            [turned[h * head : h * head + 1] for h in range(pairs)], axis=1
        )

    def one_frame(frame, _):
        count = jnp.maximum(frame, context - 1) + 1
        for known in range(1, slots + 1):

            @pl.when(count == known)
            def _():
                attend(frame ^ me, known)

        return 0

    lax.fori_loop(0, slots, one_frame, 0)
    for slot in range(slots):
        outs[slot // 2][slot % 2] = exact[slot].astype(BF16)


def attend_call(meta, clip, parts, head):
    zs = len(parts)
    slots = 2 * zs
    rows, width = parts[0].shape[-2:]
    pairs = width // head
    work = slots * slots * rows * rows
    return pl.pallas_call(
        functools.partial(attend_kernel, slots, head, clip),
        out_shape=[shaped((2, rows, width), BF16)] * zs
        + [shaped((slots, rows, width), F32), shaped((slots, 1, pairs * rows), F32)],
        in_specs=[SMEM] + [ANY] * zs,
        out_specs=[VMEM] * (zs + 2),
        scratch_shapes=[
            pltpu.VMEM((slots, 3, rows, width), BF16),
            pltpu.VMEM((slots, pairs * rows, rows), F32),
            pltpu.VMEM((slots, pairs, rows, 2 * width), BF16),
            pltpu.SemaphoreType.DMA((zs,)),
        ],
        compiler_params=params(),
        cost_estimate=cost(work * 16 * width, slots * rows * width * 12, work * pairs),
        name="attend",
    )(meta, *parts)


def attend_grad_kernel(slots, head, clip, meta, *refs):
    zs = slots // 2
    parts, grads = refs[:zs], refs[zs:slots]
    exact, logs = refs[slots], refs[slots + 1]
    outs = refs[slots + 2 : slots + 2 + zs]
    held, grad, query_rows, grad_rows, delta, grad_q, grad_k, grad_v, sems, more = refs[
        slots + 2 + zs :
    ]
    copies = []
    for k in range(zs):
        pair = pl.ds(2 * k, 2)
        copies.append(pltpu.make_async_copy(parts[k], held.at[pair], sems.at[k]))
        copies.append(pltpu.make_async_copy(grads[k], grad.at[pair], more.at[k]))
    for copy in copies:
        copy.start()
    for copy in copies:
        copy.wait()
    me, context = meta[0], meta[2 + clip]
    rows, width = held.shape[2], held.shape[3]
    pairs = width // head

    def prepare(slot, _):
        query_rows[slot] = jnp.concatenate(split_heads(held[slot, 0], pairs, head), axis=0)
        grad_rows[slot] = jnp.concatenate(split_heads(grad[slot], pairs, head), axis=0)
        product = (grad[slot].astype(F32) * exact[slot]).T
        delta[slot] = jnp.concatenate(
            [
                jnp.sum(product[h * head : (h + 1) * head], axis=0, keepdims=True)
                for h in range(pairs)
            ],
            axis=1,
        )
        grad_q[slot] = jnp.zeros((rows, width), F32)
        return 0

    lax.fori_loop(0, slots, prepare, 0)

    def key_frame(frame, _):
        place = frame ^ me
        keys, values = held[place, 1], held[place, 2]
        head_keys = split_heads(keys, pairs, head)
        grad_k[...] = jnp.zeros_like(grad_k)
        grad_v[...] = jnp.zeros_like(grad_v)

        def query_frames(first, count):
            add_k = add_v = None
            for n in range(count):
                slot = (first + n) ^ me
                score = dot_nt(keys, query_rows[slot])
                grad_weight = dot_nt(values, grad_rows[slot])
                weight = jnp.exp(score - logs[slot])
                grad_score = (weight * (grad_weight - delta[slot])).astype(BF16)
                term_v = dot_nn(weight.astype(BF16), grad_rows[slot])
                term_k = dot_nn(grad_score, query_rows[slot])
                add_v = term_v if add_v is None else add_v + term_v
                add_k = term_k if add_k is None else add_k + term_k
                total = grad_q[slot]
                for h in range(pairs):
                    total = total + dot_tn(grad_score[:, h * rows : (h + 1) * rows], head_keys[h])
                grad_q[slot] = total
            grad_v[...] += add_v
            grad_k[...] += add_k

        first = jnp.where(frame < context, 0, frame)
        for size in GROUPS:
            if size > slots:
                continue
            count = (slots - first) // size

            def group_step(n, _, first=first, size=size):
                query_frames(first + n * size, size)
                return 0

            lax.fori_loop(0, count, group_step, 0)
            first = first + count * size
        held[place, 1] = grad_k[...].astype(BF16)
        held[place, 2] = grad_v[...].astype(BF16)
        return 0

    lax.fori_loop(0, slots, key_frame, 0)
    for slot in range(slots):
        out, role = outs[slot // 2], slot % 2
        out[role, 0] = (grad_q[slot] * head**-0.5).astype(BF16)
        out[role, 1] = held[slot, 1]
        out[role, 2] = held[slot, 2]


def attend_grad_call(meta, clip, parts, grads, exact, logs, head):
    zs = len(parts)
    slots = 2 * zs
    rows, width = parts[0].shape[-2:]
    pairs = width // head
    work = slots * slots * rows * rows
    return pl.pallas_call(
        functools.partial(attend_grad_kernel, slots, head, clip),
        out_shape=[shaped((2, 3, rows, width), BF16)] * zs,
        in_specs=[SMEM] + [ANY] * slots + [VMEM, VMEM],
        out_specs=[VMEM] * zs,
        scratch_shapes=[
            pltpu.VMEM((slots, 3, rows, width), BF16),
            pltpu.VMEM((slots, rows, width), BF16),
            pltpu.VMEM((slots, pairs * rows, width), BF16),
            pltpu.VMEM((slots, pairs * rows, width), BF16),
            pltpu.VMEM((slots, 1, pairs * rows), F32),
            pltpu.VMEM((slots, rows, width), F32),
            pltpu.VMEM((rows, width), F32),
            pltpu.VMEM((rows, width), F32),
            pltpu.SemaphoreType.DMA((zs,)),
            pltpu.SemaphoreType.DMA((zs,)),
        ],
        compiler_params=params(),
        cost_estimate=cost(work * 4 * width, slots * rows * width * 2, work * pairs / 10),
        name="attend_grad",
    )(meta, *parts, *grads, exact, logs)


def mixed_places(width, hidden):
    ends = [0]
    for columns in (width // 2, hidden // 2, width, hidden):
        ends.append(ends[-1] + columns)
    return ends


def forward_back_kernel(slots, clip, meta, tokens, cotangent, mod, proj_b, up_b, down_b, *refs):
    zs = slots // 2
    width, hidden_width = tokens.shape[-1], refs[zs + 2].shape[1]
    at_act, at_gtwo, at_hid = mixed_places(width, hidden_width)[1:4]
    parts, swapped, (proj_hbm, up_hbm, down_hbm) = refs[:zs], refs[zs], refs[zs + 1 : zs + 4]
    (
        layer_out, grad_middle_out, row_grads, up_bgrad,
        att_own, att_far, gone_low, n2_own, act_own, mixed,
        held, far, n2_other, gtwo_low, proj, up, down, slope, active, hid, sems,
    ) = refs[zs + 4 :]
    blocks = up.shape[1] // FF_BLOCK
    fetches = [pltpu.make_async_copy(proj_hbm, proj, sems.at[4])]
    for source, target, columns in ((up_hbm, up, True), (down_hbm, down, False)):
        for block in range(blocks):
            at = pl.ds(block * FF_BLOCK, FF_BLOCK)
            at = (slice(None), at) if columns else (at, slice(None))
            fetches.append(
                pltpu.make_async_copy(source.at[at], target.at[at], sems.at[4 + len(fetches)])
            )
    for fetch in fetches[:IN_FLIGHT]:
        fetch.start()

    def fetched(number):
        fetches[number].wait()
        if number + IN_FLIGHT < len(fetches):
            fetches[number + IN_FLIGHT].start()

    me = meta[0]
    parity = me % 2
    rows = tokens.shape[-2]
    lanes = width // slots
    gate_one, shift_two, scale_two, gate_two = (mod[k, clip : clip + 1] for k in range(4))
    for k in range(zs):
        held[(2 * k) ^ me] = parts[k][0]
        held[(2 * k + 1) ^ me] = swapped[k]
        far[k ^ (me // 2)] = parts[k][1]
    attended = jnp.concatenate([held[k] for k in range(slots)], axis=1)
    att_own[...] = jnp.concatenate([held[2 * k + parity] for k in range(zs)], axis=1)
    att_far[...] = jnp.concatenate([far[k] for k in range(zs)], axis=1)
    fetched(0)
    branch_one = dot_nn(attended, proj[...]) + proj_b[...].astype(F32)
    middle = tokens[...].reshape(rows, width).astype(F32) + gate_one * branch_one
    hat_two, inverse_two = norm_parts(middle)
    low_two = (hat_two * (1.0 + scale_two) + shift_two).astype(BF16)
    for block in range(slots):
        store_by_parity(
            n2_own, n2_other, slice(block // 2 * lanes, (block // 2 + 1) * lanes), parity, block,
            low_two[:, block * lanes : (block + 1) * lanes],
        )
    n2_copy = pltpu.make_async_copy(n2_other, mixed.at[:, pl.ds(0, width // 2)], sems.at[2])
    n2_copy.start()
    chunk = hidden_width // slots
    for block in range(blocks):
        at = slice(block * FF_BLOCK, (block + 1) * FF_BLOCK)
        fetched(1 + block)
        hidden = dot_nn(low_two, up[:, at]) + up_b[:, at].astype(F32)
        square = hidden * hidden
        bent = jnp.tanh(GELU_A * (hidden + GELU_B * square * hidden))
        half = 0.5 * (1.0 + bent)
        low = (hidden * half).astype(BF16)
        slope[:, at] = half + (0.5 * GELU_A) * hidden * (1.0 - bent * bent) * (
            1.0 + (3.0 * GELU_B) * square
        )
        active[:, at] = low
        for index in range(block * FF_BLOCK // chunk, (block + 1) * FF_BLOCK // chunk):
            piece = active.at[:, pl.ds(index * chunk, chunk)]
            place = pl.ds(index // 2 * chunk, chunk)

            @pl.when(parity == index % 2)
            def _():
                pltpu.make_async_copy(piece, act_own.at[:, place], sems.at[0]).start()

            @pl.when(parity != index % 2)
            def _():
                pltpu.make_async_copy(
                    piece, mixed.at[:, pl.ds(at_act + index // 2 * chunk, chunk)], sems.at[0]
                ).start()

    branch_two = down_b[...].astype(F32)
    for block in range(blocks):
        at = slice(block * FF_BLOCK, (block + 1) * FF_BLOCK)
        fetched(1 + blocks + block)
        branch_two = branch_two + dot_nn(active[:, at], down[at, :])
    layer_out[...] = (middle + gate_two * branch_two).astype(BF16)
    grad_out = cotangent[...].reshape(rows, width).astype(F32)
    low_grad_two = (grad_out * gate_two).astype(BF16)
    gtwo_low[...] = low_grad_two
    gtwo_copy = pltpu.make_async_copy(gtwo_low, mixed.at[:, pl.ds(at_gtwo, width)], sems.at[3])
    gtwo_copy.start()
    row_grads[3:4] = jnp.sum(grad_out * branch_two, axis=0, keepdims=True)
    row_grads[4:5] = jnp.sum(low_grad_two.astype(F32), axis=0, keepdims=True)
    grad_normed = None
    for block in range(blocks):
        at = slice(block * FF_BLOCK, (block + 1) * FF_BLOCK)
        low = (dot_nt(low_grad_two, down[at, :]) * slope[:, at]).astype(BF16)
        hid[:, at] = low
        pltpu.make_async_copy(
            hid.at[:, at], mixed.at[:, pl.ds(at_hid + block * FF_BLOCK, FF_BLOCK)], sems.at[1]
        ).start()
        up_bgrad[:, at] = jnp.sum(low.astype(F32), axis=0, keepdims=True)
        term = dot_nt(low, up[:, at])
        grad_normed = term if grad_normed is None else grad_normed + term
    grad_middle, grad_shift, grad_scale = norm_pull(grad_normed, hat_two, inverse_two, scale_two)
    grad_middle = grad_middle + grad_out
    grad_middle_out[...] = grad_middle
    low_grad_one = (grad_middle * gate_one).astype(BF16)
    gone_low[...] = low_grad_one
    row_grads[0:1] = jnp.sum(grad_middle * branch_one, axis=0, keepdims=True)
    row_grads[1:2] = grad_shift
    row_grads[2:3] = grad_scale
    row_grads[5:6] = jnp.sum(low_grad_one.astype(F32), axis=0, keepdims=True)
    row_grads[6:8] = jnp.zeros((2, width), F32)
    n2_copy.wait()
    gtwo_copy.wait()
    pltpu.make_async_copy(active, active, sems.at[0]).wait()
    pltpu.make_async_copy(hid, hid, sems.at[1]).wait()


def forward_back_call(
    meta, clip, tokens, cotangent, mod, proj_b, up_b, down_b, parts, swapped, proj, up, down
):
    zs = len(parts)
    slots = 2 * zs
    rows, width = tokens.shape[-2:]
    lanes = width // slots
    hidden = up.shape[1]
    half, half_hidden = width // 2, hidden // 2
    out_shape = [
        shaped((rows, width), BF16),
        shaped((rows, width), F32),
        shaped((8, width), F32),
        shaped((1, hidden), F32),
        shaped((rows, half), BF16),
        shaped((rows, half), BF16),
        shaped((rows, width), BF16),
        shaped((rows, half), BF16),
        shaped((rows, half_hidden), BF16),
        shaped((rows, mixed_places(width, hidden)[4]), BF16),
    ]
    full = lambda shape: pl.BlockSpec(shape, lambda t: (0,) * len(shape))
    pick = pl.BlockSpec((1, 1, rows, width), lambda t: (clip, 0, 0, 0))
    return pl.pallas_call(
        functools.partial(forward_back_kernel, slots, clip),
        grid=(1,),
        out_shape=out_shape,
        in_specs=[SMEM, pick, pick]
        + [full(a.shape) for a in (mod, proj_b, up_b, down_b, *parts, swapped)]
        + [ANY] * 3,
        out_specs=[ANY if k in (8, 9) else full(o.shape) for k, o in enumerate(out_shape)],
        scratch_shapes=[
            pltpu.VMEM((slots, rows, lanes), BF16),
            pltpu.VMEM((zs, rows, lanes), BF16),
            pltpu.VMEM((rows, half), BF16),
            pltpu.VMEM((rows, width), BF16),
            pltpu.VMEM(proj.shape, BF16),
            pltpu.VMEM(up.shape, BF16),
            pltpu.VMEM(down.shape, BF16),
            pltpu.VMEM((rows, hidden), F32),
            pltpu.VMEM((rows, hidden), BF16),
            pltpu.VMEM((rows, hidden), BF16),
            pltpu.SemaphoreType.DMA((5 + 2 * hidden // FF_BLOCK,)),
        ],
        compiler_params=params(),
        cost_estimate=cost(
            4 * rows * width * (width + 2 * hidden),
            4 * width * (width + 2 * hidden),
            rows * hidden,
        ),
        name="feed_forward",
    )(meta, tokens, cotangent, mod, proj_b, up_b, down_b, *parts, swapped, proj, up, down)


def proj_back_kernel(meta, near, far, proj, *outs):
    me = meta[0]
    rows, lanes = near.shape[0], outs[0].shape[2]
    groups = [pl.multiple_of((me ^ (2 * k)) * lanes, lanes) for k in range(len(outs))]
    weight = jnp.concatenate([proj[pl.ds(group, lanes), :] for group in groups], axis=0)
    both = jnp.concatenate([near[...], far[...]], axis=0)
    value = dot_nt(both, weight).astype(BF16)
    for k, out in enumerate(outs):
        for role in range(2):
            out[role] = value[role * rows : (role + 1) * rows, k * lanes : (k + 1) * lanes]


def proj_back_call(meta, near, far, proj, zs):
    rows, width = near.shape
    lanes = width // (2 * zs)
    return pl.pallas_call(
        proj_back_kernel,
        out_shape=[shaped((2, rows, lanes), BF16)] * zs,
        in_specs=[SMEM, VMEM, VMEM, VMEM],
        out_specs=[VMEM] * zs,
        compiler_params=params(),
        cost_estimate=cost(2 * rows * width * width, 2 * width * width + 6 * rows * width),
        name="proj_back",
    )(meta, near, far, proj)


def qkv_grad_kernel(zs, head, clip, meta, *refs):
    tables, refs = refs[:4], refs[4:]
    blocks = refs[zs].shape[0] // (2 * LANES)
    parts, weights = refs[:zs], refs[zs : zs + 3 * blocks]
    near_out, far_out, near_sum, far_sum, bias_out, held = refs[zs + 3 * blocks :]
    rows, width = near_sum.shape
    clips = tables[0].shape[0] // 2
    z = meta[0] // 2
    cosines = [turn_table(tables[0], tables[2], role * clips + clip, head) for role in range(2)]
    sines = [turn_table(tables[1], tables[3], role * clips + clip, head) for role in range(2)]
    for k in range(zs):
        held[k ^ z] = parts[k][...]
    totals = [None, None]
    bias_out[...] = jnp.zeros_like(bias_out)
    half = width // 2
    for kind in range(3):
        weight = jnp.concatenate([w[...] for w in weights[kind * blocks : (kind + 1) * blocks]], axis=1)
        sums = None
        for role, out in enumerate((near_out, far_out)):
            low = jnp.concatenate([held[k, role, kind] for k in range(zs)], axis=1)
            if kind < 2:
                low = turn(low.astype(F32), cosines[role], sines[role], head, True).astype(BF16)
            out[:, kind * half : (kind + 1) * half] = low
            column = jnp.sum(low.astype(F32), axis=0, keepdims=True)
            sums = column if sums is None else sums + column
            term = dot_nt(low, weight)
            totals[role] = term if totals[role] is None else totals[role] + term
        bias_out[kind : kind + 1] = sums
    near_sum[...] = totals[0]
    far_sum[...] = totals[1]


def qkv_grad_call(meta, clip, tables, parts, weight, head, aligned):
    zs = len(parts)
    rows, lanes = parts[0].shape[-2:]
    width = 2 * zs * lanes
    blocks = width // (2 * LANES)
    whole = lambda shape: pl.BlockSpec(shape, lambda t, m: (0,) * len(shape))
    out_shape = [
        shaped((rows, 3 * width // 2), BF16),
        shaped((rows, 3 * width // 2), BF16),
        shaped((rows, width), F32),
        shaped((rows, width), F32),
        shaped((8, width // 2), F32),
    ]
    return pl.pallas_call(
        functools.partial(qkv_grad_kernel, zs, head, clip),
        out_shape=out_shape,
        grid_spec=pltpu.PrefetchScalarGridSpec(
            num_scalar_prefetch=1,
            grid=(1,),
            in_specs=[whole(a.shape) for a in (*tables, *parts)]
            + half_specs(width, width, 2 * zs, aligned),
            out_specs=[whole(o.shape) for o in out_shape],
            scratch_shapes=[pltpu.VMEM((zs, 2, 3, rows, lanes), BF16)],
        ),
        compiler_params=params(),
        cost_estimate=cost(0.6 * rows * width * width, width * width),
        name="qkv_grad",
    )(meta, *tables, *parts, *[weight] * (3 * blocks))


def norm_grad_kernel(tokens, mod, *refs):
    clips = tokens.shape[0]
    nears, fars, middles = refs[:clips], refs[clips : 2 * clips], refs[2 * clips : 3 * clips]
    tokens_grad, row_grads = refs[3 * clips :]
    for c in range(clips):
        hat, inverse = norm_parts(tokens[c, 0].astype(F32))
        grad, shift, scale = norm_pull(
            nears[c][...] + fars[c][...], hat, inverse, mod[1, c : c + 1]
        )
        tokens_grad[c, 0] = grad + middles[c][...]
        row_grads[c, 0:1] = shift
        row_grads[c, 1:2] = scale
        row_grads[c, 2:8] = jnp.zeros((6, tokens.shape[-1]), F32)


def norm_grad_call(tokens, mod, nears, fars, middles):
    clips, _, rows, width = tokens.shape
    return pl.pallas_call(
        norm_grad_kernel,
        out_shape=[shaped(tokens.shape, F32), shaped((clips, 8, width), F32)],
        in_specs=[VMEM] * (2 + 3 * clips),
        out_specs=[VMEM, VMEM],
        compiler_params=params(),
        cost_estimate=cost(clips * rows * width * 3, clips * rows * width * 2),
        name="norm_grad",
    )(tokens, mod, *nears, *fars, *middles)


def weight_grad_kernel(jobs, clip_size, zs, split, meta, *refs):
    arrays_n = sum(2 * job[0] for job in jobs)
    outs_n = 4 if split else 1
    arrays, outs = refs[:arrays_n], refs[arrays_n : arrays_n + outs_n]
    held, out_sems, in_sems = refs[arrays_n + outs_n : arrays_n + outs_n + 3]
    scratch = refs[arrays_n + outs_n + 3 :]
    _, _, _, height, cols = held.shape
    tile = zs * height
    z = meta[0] // 2
    clip = meta[1] if split else 0

    def send_out(slot, tiles, repeat, first, tall):
        for e in range(clip_size):
            for half, first_bit in enumerate((1, clip_size // 2) if split else (0,)):
                keep, send = (outs[2 * half], outs[2 * half + 1]) if split else (outs[0], None)
                rest = [k for k in range(clip_size) if not k & first_bit]
                if e & first_bit:
                    out, place = send, rest.index(e ^ first_bit)
                else:
                    out, place = keep, rest.index(e)
                span = zs // 2 if split else zs
                low, high = half * span, (half + 1) * span
                if not tall:
                    pltpu.make_async_copy(
                        held.at[slot, e, pl.ds(low, span)],
                        out.at[place, :, pl.ds(first, height)],
                        out_sems.at[slot],
                    ).start()
                    continue
                for block in range(zs):
                    row = repeat * zs + block
                    k = row // tiles
                    if low <= k < high:
                        pltpu.make_async_copy(
                            held.at[slot, e, block],
                            out.at[place, k - low, pl.ds(first + row % tiles * height, height)],
                            out_sems.at[slot],
                        ).start()

    copies = []
    at = 0
    for job, (count, _, _, _, _, places) in enumerate(jobs):
        left, right = scratch[2 * job : 2 * job + 2]
        depth = left.shape[0] // count
        for n in range(2 * count):
            target = left if n < count else right
            source = arrays[at + n]
            if source.shape[1] != target.shape[1]:
                source = source.at[:, pl.ds(places[n], target.shape[1])]
            copies.append(
                pltpu.make_async_copy(
                    source,
                    target.at[pl.ds(n % count * depth, depth)],
                    in_sems.at[at + n],
                )
            )
        at += 2 * count
    for copy in copies:
        copy.start()

    at = number = 0
    for job, (count, lane_parts, tall, tiles, first, _) in enumerate(jobs):
        left, right = scratch[2 * job : 2 * job + 2]
        block = left.shape[1] // zs
        for n in range(2 * count):
            copies[at + n].wait()
        at += 2 * count
        wide = right.shape[1] // (tiles * lane_parts if not tall else 1)
        part = wide // clip_size
        for repeat in range(tiles):
            slot = number % 2
            if number >= 2:
                pltpu.make_async_copy(held.at[slot], held.at[slot], out_sems.at[slot]).wait()
            for lane_part in range(lane_parts):
                if tall:
                    per = zs // tiles
                    rows = [
                        left[:, pl.ds(pl.multiple_of(((repeat * per + n) ^ z) * block, block), block)]
                        for n in range(per)
                    ]
                    rows = rows[0] if per == 1 else jnp.concatenate(rows, axis=1)
                    value = dot_tn(rows, right[...]).astype(BF16)
                else:
                    group = repeat + lane_part
                    value = dot_tn(
                        left[...], right[:, group * wide : (group + 1) * wide]
                    ).astype(BF16)
                for p in range(clip_size):
                    lanes = slice(lane_part * part, (lane_part + 1) * part)
                    piece = value[:, p * part : (p + 1) * part]
                    for k in range(zs):
                        source = piece[k * height : (k + 1) * height]
                        held[slot, p ^ clip, k if tall else k ^ z, :, lanes] = source
            send_out(slot, tiles, repeat, first if tall else first + repeat * height, tall)
            number += 1
    for slot in range(min(number, 2)):
        pltpu.make_async_copy(held.at[slot], held.at[slot], out_sems.at[slot]).wait()


def weight_grad_call(meta, products, clip_size, zs, split, name):
    jobs, arrays, scratch = [], [], []
    first = flops = 0
    tile = min(p[0][0][2] for p in products)
    height = tile // zs
    piece = None
    for lefts, rights, lane_parts, tall in products:
        depth, total = rights[0][0].shape[0], rights[0][2]
        rows = lefts[0][2]
        if tall:
            tiles, piece = rows // tile, total // clip_size
        elif lane_parts > 1:
            tiles, piece = 1, total // clip_size
        else:
            tiles, piece = total // (2 * tile), 2 * tile // clip_size
        count = len(lefts)
        places = tuple(a[1] for a in lefts + rights)
        jobs.append((count, lane_parts, tall, tiles, first, places))
        first += height * tiles
        arrays += [a[0] for a in lefts + rights]
        flops += 2 * count * depth * rows * total
        scratch += [
            pltpu.VMEM((count * depth, rows), BF16),
            pltpu.VMEM((count * depth, total), BF16),
        ]
    if split:
        outs = [shaped((clip_size // 2, zs // 2, first, piece), BF16)] * 4
    else:
        outs = [shaped((clip_size, zs, first, piece), BF16)]
    return pl.pallas_call(
        functools.partial(weight_grad_kernel, tuple(jobs), clip_size, zs, split),
        out_shape=outs,
        in_specs=[SMEM] + [ANY] * len(arrays),
        out_specs=[ANY] * len(outs),
        scratch_shapes=[
            pltpu.VMEM((2, clip_size, zs, height, piece), BF16),
            pltpu.SemaphoreType.DMA((2,)),
            pltpu.SemaphoreType.DMA((len(arrays),)),
        ]
        + scratch,
        compiler_params=params(),
        cost_estimate=cost(flops, flops / 512),
        name=name,
    )(meta, *arrays)


def place_kernel(jobs, pieces, meta, *refs):
    parts, outs = refs[:pieces], refs[pieces:]
    clip = meta[1]
    cols = parts[0].shape[1]
    for e in range(pieces):
        first = 0
        for out, (height, repeats, tall) in zip(outs, jobs):
            for repeat in range(repeats):
                base = 0 if tall else repeat * cols * pieces
                target = pl.ds(pl.multiple_of(base + (clip ^ e) * cols, cols), cols)
                value = parts[e][first : first + height].astype(F32)
                if tall:
                    out[repeat * height : (repeat + 1) * height, target] = value
                else:
                    out[:, target] = value
                first += height


def place_call(meta, parts, jobs, outs):
    return pl.pallas_call(
        functools.partial(place_kernel, jobs, len(parts)),
        out_shape=outs,
        in_specs=[SMEM] + [VMEM] * len(parts),
        out_specs=[VMEM] * len(outs),
        compiler_params=params(),
        cost_estimate=cost(0, sum(o.size * 4 for o in outs)),
        name="place_grads",
    )(meta, *parts)


def place_qkv_kernel(meta, *refs):
    parts, out = refs[:-1], refs[-1]
    parity, clip = meta[0] % 2, meta[1]
    thirds = out.shape[1] // 3
    for e, part in enumerate(parts):
        for role in range(2):
            block = 2 * (clip ^ e) + (parity ^ role)
            for kind in range(3):
                at = pl.ds(pl.multiple_of(kind * thirds + block * LANES, LANES), LANES)
                out[:, at] = part[role, :, kind * LANES : (kind + 1) * LANES].astype(F32)


def place_qkv_call(meta, parts, out):
    return pl.pallas_call(
        place_qkv_kernel,
        out_shape=out,
        in_specs=[SMEM] + [VMEM] * len(parts),
        out_specs=VMEM,
        compiler_params=params(),
        cost_estimate=cost(0, out.size * 6),
        name="place_qkv_grad",
    )(meta, *parts)


def exchange(array, axis, size, distance):
    return lax.ppermute(array, axis, [(k, k ^ distance) for k in range(size)])


def after(value, *others):
    return lax.optimization_barrier((value, *others))


def spread(slots_out, seq_size):
    return [slots_out[0]] + [
        exchange(slots_out[k], "seq", seq_size, 2 * k) for k in range(1, seq_size // 2)
    ]


def add_low(left, right):
    return (left.astype(F32) + right.astype(F32)).astype(BF16)


def step_out(pairs, bits, size):
    return [exchange(send, "clip", size, bit) for (_, send), bit in zip(pairs, bits)]


def step_in(pairs, arrived):
    left = []
    for (keep, _), new in zip(pairs, arrived):
        half = keep.shape[0] // 2
        if half:
            left.append((add_low(keep[:half], new[:half]), add_low(keep[half:], new[half:])))
        else:
            left.append((add_low(keep[0], new[0]), None))
    return left


def clip_orders(clip_size):
    down = [1 << k for k in reversed(range(clip_size.bit_length() - 1))]
    return [1] + down[:-1], down


def z_out(blocks, seq_size):
    return exchange(jnp.stack(blocks[1::2]), "seq", seq_size, seq_size // len(blocks))


def z_in(blocks, arrived):
    return [add_low(keep, new) for keep, new in zip(blocks[0::2], arrived)]


def sum_z(blocks, seq_size):
    while len(blocks) > 1:
        blocks = z_in(blocks, z_out(blocks, seq_size))
    return blocks[0]


def gather_pieces(piece, clip_size):
    return [piece] + [exchange(piece, "clip", clip_size, d) for d in range(1, clip_size)]


def double(array, axis, size):
    bit = 1
    while bit < size:
        array = jnp.concatenate([array, exchange(array, axis, size, bit)])
        bit *= 2
    return array


def silu_act(values_in):
    return values_in * jax.nn.sigmoid(values_in)


def rotary_tables(stamps, patch_count, head):
    lane = jnp.arange(LANES, dtype=jnp.int32)
    quarter = head // 4
    freqs = 10000.0 ** (-(lane % quarter).astype(F32) / quarter)
    sign = jnp.where(lane % head < head // 2, -1.0, 1.0).astype(F32)
    tables = []
    for places in (stamps, jnp.arange(patch_count, dtype=jnp.int32)):
        angles = places.astype(F32)[:, None] * freqs[None, :]
        tables += [jnp.cos(angles), jnp.sin(angles) * sign[None, :]]
    return tables


def on_device(
    tokens,
    cotangent,
    context_count,
    noise_level,
    frame_time,
    level_table,
    mod_weight,
    mod_bias,
    qkv_weight,
    qkv_bias,
    proj_weight,
    proj_bias,
    up_weight,
    up_bias,
    down_weight,
    down_bias,
):
    seq_size, clip_size = lax.axis_size("seq"), lax.axis_size("clip")
    me, mine = lax.axis_index("seq"), lax.axis_index("clip")
    clips, _, rows, width = tokens.shape
    head = width // HEADS
    hidden = up_weight.shape[1]
    zs = seq_size // 2
    me = me.astype(jnp.int32)
    mine = mine.astype(jnp.int32)
    parity = me % 2
    aligned = (width // seq_size) % LANES == 0
    stamps = jnp.stack([noise_level[:, 0], frame_time[:, 0]])
    other_stamps = exchange(stamps, "seq", seq_size, 1)
    other_tokens = exchange(tokens, "seq", seq_size, 1)
    meta = jnp.concatenate([jnp.stack([me, mine]), context_count])
    levels = jnp.concatenate(
        [
            jnp.where(me < context_count, 0, stamps[0]),
            jnp.where((me ^ 1) < context_count, 0, other_stamps[0]),
        ]
    )
    levels_used = levels[:clips]
    mod_bias_row = mod_bias[None]
    mod_one, condition = modulation_call(levels, level_table, mod_weight, mod_bias_row, 0, 2)
    condition = condition[:clips]
    tables = rotary_tables(jnp.concatenate([stamps[1], other_stamps[1]]), rows, head)
    qkv_bias_row = qkv_bias[None]
    if aligned:
        weight_half, bias_half = qkv_weight, qkv_bias_row
    else:
        weight_half = half_columns(qkv_weight, seq_size, parity)
        bias_half = half_columns(qkv_bias_row, seq_size, parity)

    swap = lambda array: exchange(array, "seq", seq_size, 1)
    full = lambda array: (array, 0, array.shape[1])
    at_n2, at_act, at_gtwo, at_hid, _ = mixed_places(width, hidden)
    out = qkv_call(
        meta, tokens, other_tokens, mod_one, tables, weight_half, bias_half, zs, head, aligned
    )
    normed = out[zs * clips :]
    parts = [spread(out[:zs], seq_size)]
    mod_two, _ = modulation_call(
        levels[:clips], level_table, mod_weight, mod_bias_row, 2, 4
    )
    proj_row, up_row, down_row = proj_bias[None], up_bias[None], down_bias[None]
    parts[0], mod_two, proj_row, up_row, down_row = after(
        parts[0], mod_two, proj_row, up_row, down_row
    )
    exact, logs, attended, crossed = [], [], [], []
    for c in range(clips):
        sends = out[(c + 1) * zs : (c + 2) * zs] if c < clips - 1 else None
        if c < clips - 1:
            parts.append(spread(sends, seq_size))
        done = attend_call(meta, c, parts[c], head)
        exact.append(done[zs])
        logs.append(done[zs + 1])
        sends = done[:zs]
        if c < clips - 1:
            sends, parts[c + 1] = after(sends, parts[c + 1])
        if c:
            sends, attended[-1] = after(sends, attended[-1])
            crossed.append(swap(jnp.stack([a[1] for a in attended[-1]])))
        attended.append(spread(sends, seq_size))
    layer, middles, row_grads, up_bgrads, saved, mixed, far_ones, grads = ([] for _ in range(8))
    for c in range(clips):
        if c:
            meta, grads[-1][0] = after(meta, grads[-1][0])
        out = forward_back_call(
            meta, c, tokens, cotangent, mod_two, proj_row, up_row, down_row, attended[c],
            crossed[c], proj_weight, up_weight, down_weight,
        )
        layer.append(out[0])
        middles.append(out[1])
        row_grads.append(out[2])
        up_bgrads.append(out[3])
        gone, mine_mixed = out[6], out[9]
        if c < clips - 1:
            gone, mine_mixed, attended[c + 1] = after(gone, mine_mixed, attended[c + 1])
            crossed.append(swap(jnp.stack([a[1] for a in attended[c + 1]])))
        if c:
            gone, mine_mixed, grads[-1], mixed[-1] = after(gone, mine_mixed, grads[-1], mixed[-1])
        far_ones.append(swap(gone))
        if c < clips - 1:
            far_ones[-1], crossed[-1] = after(far_ones[-1], crossed[-1])
        saved.append((out[4], out[5], gone, out[7], out[8]))
        back = list(proj_back_call(meta, gone, far_ones[c], proj_weight, zs))
        back[0], mine_mixed = after(back[0], mine_mixed)
        mixed.append([mine_mixed, swap(mine_mixed)])
        grads.append(spread(back, seq_size))
    row = width // seq_size
    orders = clip_orders(clip_size)
    steps = len(orders[0])
    products = [([], [], 1, False), ([], [], 1, True), ([], [], 1, False)]
    for c in range(clips):
        att_own, att_far, gone, n2_own, act_own = saved[c]
        own, far = mixed[c]
        products[0][0].extend([full(att_own), full(att_far)])
        products[0][1].extend([full(gone), full(far_ones[c])])
        products[1][0].extend([full(act_own), (far, at_act, hidden // 2)])
        products[1][1].extend([(own, at_gtwo, width), (far, at_gtwo, width)])
        products[2][0].extend([full(n2_own), (far, at_n2, width // 2)])
        products[2][1].extend([(own, at_hid, hidden), (far, at_hid, hidden)])
    meta, grads[-1][0] = after(meta, grads[-1][0])
    (shares,) = weight_grad_call(meta, products, clip_size, zs, False, "weight_grads")
    meta, shares = after(meta, shares)
    summed = lax.psum_scatter(
        shares.reshape(-1, shares.shape[-1]), "clip", scatter_dimension=0, tiled=True
    ).reshape(shares.shape[1:])
    returned = []
    for c in range(clips):
        if c:
            meta, returned[-1][0] = after(meta, returned[-1][0])
        out = attend_grad_call(meta, c, parts[c], grads[c], exact[c], logs[c], head)
        if c < clips - 1:
            out, grads[c + 1] = after(out, grads[c + 1])
        else:
            out, returned[-1] = after(out, returned[-1])
        returned.append(spread(out, seq_size))
    turns = list(zip(*orders))
    grad_rights, nears, fars, qkv_bgrads = [], [], [], []
    for c in range(clips):
        if c == 0:
            meta, returned[-1][0] = after(meta, returned[-1][0])
        out = qkv_grad_call(meta, c, tables, returned[c], weight_half, head, aligned)
        grad_rights.extend(out[:2])
        nears.append(out[2])
        fars.append(swap(out[3]))
        qkv_bgrads.append(out[4][:3])
    tokens_grad, late_rows = norm_grad_call(tokens, mod_one, nears, fars, middles)
    blocks = list(summed)
    if len(blocks) > 1:
        landed = z_out(blocks, seq_size)
        late_rows, landed = after(late_rows, landed)
        blocks = z_in(blocks, landed)
    level_rows = jnp.stack([levels_used // 32, levels_used % 32]).astype(F32)
    level_rows = jnp.concatenate([level_rows, jnp.zeros((2, width - clips), F32)], axis=1)
    mod_rows = []
    for c in range(clips):
        mod_rows += [late_rows[c, 0:2], row_grads[c][0:4]]
    bias_rows = [
        sum(qkv_bgrads).reshape(3 * width // 2),
        jnp.zeros((width // 2,), F32),
        sum(up_bgrads).reshape(hidden),
        sum(r[4] for r in row_grads),
        sum(r[5] for r in row_grads),
    ]
    bias_rows = jnp.concatenate(bias_rows).reshape(-1, width)
    late = jnp.concatenate([condition, level_rows] + mod_rows + [bias_rows], axis=0)
    start, stop = clips + 2, clips + 2 + 6 * clips
    late = double(late.astype(BF16)[None], "seq", seq_size)
    blocks = list(summed)
    lefts = [normed[role * clips + c] for c in range(clips) for role in range(2)]
    if aligned:
        shares = weight_grad_call(
            meta,
            [([full(a) for a in lefts], [full(a) for a in grad_rights], 3, False)],
            clip_size,
            zs,
            True,
            "qkv_weight_grad",
        )
        pairs_qkv = [shares[:2], shares[2:]]
        pairs_qkv = step_in(pairs_qkv, step_out(pairs_qkv, turns[0], clip_size))
        for bits in turns[1:]:
            pairs_qkv = step_in(pairs_qkv, step_out(pairs_qkv, bits, clip_size))
    own_sums = jnp.sum(
        late[:, stop:].astype(F32).reshape(zs, 2, late.shape[1] - stop, width), axis=0
    ).astype(BF16)
    sums_rows = 2 * own_sums.shape[1]
    message = jnp.concatenate(
        [late[:, :stop].reshape(seq_size * stop, width), own_sums.reshape(sums_rows, width)]
    )
    late = double(message[None], "clip", clip_size)
    piece = sum_z(blocks, seq_size)
    if aligned:
        pairs_qkv, piece, late = after(pairs_qkv, piece, late)
    own_sums = jnp.sum(late[:, seq_size * stop :].astype(F32), axis=0).reshape(2, -1)
    late = late[:, : seq_size * stop].reshape(clip_size * seq_size, stop, width)
    devices = clip_size * seq_size
    grad_modulation = late[:, start:].reshape(devices * clips, 6 * width)
    half_bias = own_sums[:, : 3 * width // 2].reshape(2, 3, zs, 1, width // seq_size)
    bias_sums = jnp.sum(own_sums, axis=0)[2 * width :]
    qkv_bias_sums = jnp.where(
        parity == 0,
        jnp.concatenate([half_bias[0], half_bias[1]], axis=2),
        jnp.concatenate([half_bias[1], half_bias[0]], axis=2),
    ).reshape(3 * width)
    all_condition = late[:, :clips].reshape(devices * clips, width).astype(F32)
    codes = late[:, clips:start, :clips].astype(jnp.int32)
    all_levels = (codes[:, 0] * 32 + codes[:, 1]).reshape(devices * clips)
    all_active, silu_pull = jax.vjp(silu_act, all_condition)
    my_active = lax.dynamic_slice_in_dim(all_active, me * row, row, axis=1).astype(BF16)
    mod_wgrad = lax.dot_general(
        my_active, grad_modulation, (((0,), (0,)), ((), ())), preferred_element_type=F32
    )
    (grad_condition,) = silu_pull(
        lax.dot_general(
            grad_modulation, mod_weight, (((1,), (1,)), ((), ())), preferred_element_type=F32
        )
    )
    table_row = level_table.shape[0] // seq_size
    onehot = (
        all_levels[:, None] == (me * table_row + jnp.arange(table_row, dtype=jnp.int32))[None, :]
    ).astype(F32)
    table_grad = lax.dot_general(
        onehot,
        grad_condition,
        (((0,), (0,)), ((), ())),
        precision=HIGHEST_PRECISION,
        preferred_element_type=F32,
    )
    mod_sums = jnp.sum(grad_modulation.astype(F32), axis=0)

    def own_part(vector):
        size = vector.shape[0] // seq_size
        return lax.dynamic_slice_in_dim(vector, me * size, size, axis=0)

    mod_bgrad = own_part(mod_sums)
    qkv_bgrad = own_part(qkv_bias_sums)
    up_bgrad = own_part(bias_sums[:hidden])
    down_bgrad = own_part(bias_sums[hidden : hidden + width])
    proj_bgrad = own_part(bias_sums[hidden + width : hidden + 2 * width])
    if aligned:
        pieces = gather_pieces(piece, clip_size)
        piece = sum_z([*pairs_qkv[0][0], *pairs_qkv[1][0]], seq_size)
        piece = piece.reshape(2, row, 3 * LANES)
        own_rows = lax.dynamic_index_in_dim(piece, parity, 0, keepdims=False)
        far_rows = swap(lax.dynamic_index_in_dim(piece, 1 - parity, 0, keepdims=False))
        far_rows, pieces, mod_wgrad, table_grad = after(far_rows, pieces, mod_wgrad, table_grad)
        pieces_qkv = gather_pieces(jnp.stack([own_rows, far_rows]), clip_size)
    else:
        pieces = gather_pieces(piece, clip_size)
        share = sum(
            lax.dot_general(left, right, (((0,), (0,)), ((), ())), preferred_element_type=F32)
            for left, right in zip(lefts, grad_rights)
        ).astype(BF16)
        share = share.reshape(width, 3, zs, 1, width // seq_size)
        blank = jnp.zeros_like(share)
        share = jnp.where(
            parity == 0,
            jnp.concatenate([share, blank], axis=3),
            jnp.concatenate([blank, share], axis=3),
        ).reshape(width, 3 * width)
        qkv_wgrad = lax.psum(
            lax.psum_scatter(share, "seq", scatter_dimension=0, tiled=True), "clip"
        ).astype(F32)

    proj_wgrad, down_wgrad, up_wgrad = place_call(
        meta,
        pieces,
        (
            (row, 1, False),
            (row, hidden // width, True),
            (row, hidden // width, False),
        ),
        [shaped((row, width), F32), shaped((hidden // seq_size, width), F32), shaped((row, hidden), F32)],
    )
    if aligned:
        pieces_qkv, proj_wgrad = after(pieces_qkv, proj_wgrad)
        qkv_wgrad = place_qkv_call(meta, pieces_qkv, shaped((row, 3 * width), F32))
    layer_out = jnp.stack(layer)[:, None]
    return (
        layer_out,
        tokens_grad,
        table_grad,
        mod_wgrad,
        mod_bgrad,
        qkv_wgrad,
        qkv_bgrad,
        proj_wgrad,
        proj_bgrad,
        up_wgrad,
        up_bgrad,
        down_wgrad,
        down_bgrad,
    )


def solution(mesh):
    placed = (
        P("clip", "seq", None, None),
        P("clip", "seq", None, None),
        P("clip"),
        P("clip", "seq"),
        P("clip", "seq"),
    ) + (P(),) * 11
    return jax.shard_map(
        on_device,
        mesh=mesh,
        in_specs=placed,
        out_specs=(
            P("clip", "seq", None, None),
            P("clip", "seq", None, None),
            P("seq", None),
            P("seq", None),
            P("seq"),
            P("seq", None),
            P("seq"),
            P("seq", None),
            P("seq"),
            P("seq", None),
            P("seq"),
            P("seq", None),
            P("seq"),
        ),
        check_vma=False,
    )
```

```python
import functools

import jax
import jax.numpy as jnp
from jax import lax
from jax.experimental import pallas as pl
from jax.experimental.pallas import tpu as pltpu
from jax.sharding import PartitionSpec as P

HEADS = 16
EPS = 1e-06
HIGHEST_PRECISION = lax.Precision.HIGHEST
F32 = jnp.float32
BF16 = jnp.bfloat16
ANY = pl.BlockSpec(memory_space=pltpu.HBM)
VMEM = pl.BlockSpec(memory_space=pltpu.VMEM)
SMEM = pl.BlockSpec(memory_space=pltpu.SMEM)
LANES = 128
BLOCK = 256
FF_BLOCK = 1024
IN_FLIGHT = 3
GROUPS = (8, 4, 2, 1)
GELU_A = 0.7978845608028654
GELU_B = 0.044715
WEIGHT = 1.0
VMEM_BYTES = 62 << 20


def shaped(shape, dtype):
    return jax.ShapeDtypeStruct(shape, dtype)


def params():
    return pltpu.CompilerParams(vmem_limit_bytes=VMEM_BYTES)


def cost(flops, moved, transcendentals=0):
    return pl.CostEstimate(
        flops=int(flops * WEIGHT),
        bytes_accessed=int(moved * WEIGHT),
        transcendentals=int(transcendentals * WEIGHT),
    )


def dot_nn(left, right):
    return lax.dot_general(left, right, (((1,), (0,)), ((), ())), preferred_element_type=F32)


def dot_nt(left, right):
    return lax.dot_general(left, right, (((1,), (1,)), ((), ())), preferred_element_type=F32)


def dot_tn(left, right):
    return lax.dot_general(left, right, (((0,), (0,)), ((), ())), preferred_element_type=F32)


def split_heads(values, pairs, head):
    if pairs == 1:
        return [values]
    lane = lax.broadcasted_iota(jnp.int32, values.shape, 1)
    return [jnp.where(lane // head == h, values, jnp.zeros_like(values)) for h in range(pairs)]


def swap_halves(values, head):
    half = head // 2
    lane = lax.broadcasted_iota(jnp.int32, values.shape, 1)
    ahead = pltpu.roll(values, values.shape[1] - half, 1)
    behind = pltpu.roll(values, half, 1)
    return jnp.where(lax.rem(lane, head) < half, ahead, behind)


def turn(values, cosine, signed_sine, head, back):
    parts = []
    for at in range(0, values.shape[1], LANES):
        piece = values[:, at : at + LANES]
        other = swap_halves(piece, head) * signed_sine
        parts.append(piece * cosine - other if back else piece * cosine + other)
    return jnp.concatenate(parts, axis=1)


def norm_parts(values):
    center = jnp.mean(values, axis=-1, keepdims=True)
    offset = values - center
    spread = jnp.mean(offset * offset, axis=-1, keepdims=True)
    inverse = lax.rsqrt(spread + EPS)
    return offset * inverse, inverse


def norm_pull(grad, hat, inverse, scale_row):
    grad_shift = jnp.sum(grad, axis=0, keepdims=True)
    grad_scale = jnp.sum(grad * hat, axis=0, keepdims=True)
    inner = grad * (1.0 + scale_row)
    mean_one = jnp.mean(inner, axis=-1, keepdims=True)
    mean_two = jnp.mean(inner * hat, axis=-1, keepdims=True)
    return inverse * (inner - mean_one - hat * mean_two), grad_shift, grad_scale


def store_by_parity(own_ref, other_ref, where, parity, block_index, value):
    own = parity == block_index % 2

    @pl.when(own)
    def _():
        own_ref[:, where] = value

    @pl.when(jnp.logical_not(own))
    def _():
        other_ref[:, where] = value


def modulation_kernel(meta, table, weight, bias, out, condition_out, low):
    rows, levels = out.shape[1], table.shape[0]

    @pl.when(pl.program_id(0) == 0)
    def _():
        lane = lax.broadcasted_iota(jnp.int32, (1, levels), 1)
        picked = jnp.concatenate(
            [jnp.where(lane == meta[row], 1.0, 0.0) for row in range(rows)], axis=0
        )
        condition = dot_nn(picked.astype(BF16), table[...])
        condition_out[...] = condition
        low[...] = silu_act(condition).astype(BF16)

    out[0] = dot_nn(low[...], weight[...]) + bias[...].astype(F32)


def modulation_call(levels, table, weight, bias, first, parts):
    rows, width = levels.shape[0], table.shape[1]
    return pl.pallas_call(
        modulation_kernel,
        grid=(parts,),
        out_shape=[shaped((parts, rows, width), F32), shaped((rows, width), F32)],
        in_specs=[
            SMEM,
            pl.BlockSpec(table.shape, lambda t: (0, 0)),
            pl.BlockSpec((width, width), lambda t: (0, first + t)),
            pl.BlockSpec((1, width), lambda t: (0, first + t)),
        ],
        out_specs=[
            pl.BlockSpec((1, rows, width), lambda t: (t, 0, 0)),
            pl.BlockSpec((rows, width), lambda t: (0, 0)),
        ],
        scratch_shapes=[pltpu.VMEM((rows, width), BF16)],
        compiler_params=params(),
        cost_estimate=cost(0, 2 * (parts + 1) * width * width),
        name="modulation",
    )(levels, table, weight, bias)


def turn_table(temporal, spatial, row, head):
    lane = lax.broadcasted_iota(jnp.int32, spatial.shape, 1)
    timed = lax.rem(lane, head // 2) < head // 4
    return jnp.where(timed, temporal[row : row + 1], spatial[...])


def half_columns(weight, groups, parity):
    rows, total = weight.shape
    view = weight.reshape(rows, 3, groups // 2, 2, total // (3 * groups))
    return lax.dynamic_index_in_dim(view, parity, 3, keepdims=False).reshape(rows, total // 2)


def half_specs(height, width, groups, aligned):
    specs = []
    for kind in range(3):
        for block in range(width // (2 * LANES)):
            if aligned:
                specs.append(
                    pl.BlockSpec(
                        (height, LANES), lambda t, m, k=kind, b=block: (0, k * groups + 2 * b + m[0] % 2)
                    )
                )
            else:
                specs.append(
                    pl.BlockSpec(
                        (height, LANES),
                        lambda t, m, k=kind, b=block: (0, k * (width // (2 * LANES)) + b),
                    )
                )
    return specs


def qkv_kernel(zs, head, meta, tokens, other_tokens, mod, *refs):
    tables, refs = refs[:4], refs[4:]
    blocks = tokens.shape[-1] // (2 * LANES)
    weights, biases = refs[: 3 * blocks], refs[3 * blocks : 6 * blocks]
    clips, _, rows, width = tokens.shape
    outs = refs[6 * blocks : 6 * blocks + zs * clips]
    normed_outs, (normed, held) = refs[6 * blocks + zs * clips : -2], refs[-2:]
    cosines = [turn_table(tables[0], tables[2], row, head) for row in range(2 * clips)]
    sines = [turn_table(tables[1], tables[3], row, head) for row in range(2 * clips)]
    lanes = width // (2 * zs)
    z = meta[0] // 2
    for row in range(2 * clips):
        role, clip = row // clips, row % clips
        source = (tokens, other_tokens)[role]
        hat, _ = norm_parts(source[clip, 0].astype(F32))
        low = (hat * (1.0 + mod[1, row : row + 1]) + mod[0, row : row + 1]).astype(BF16)
        normed[row * rows : (row + 1) * rows] = low
        normed_outs[row][...] = low
    for kind in range(3):
        pick = slice(kind * blocks, (kind + 1) * blocks)
        weight = jnp.concatenate([w[...] for w in weights[pick]], axis=1)
        bias = jnp.concatenate([b[...] for b in biases[pick]], axis=1).astype(F32)
        value = dot_nn(normed[...], weight) + bias
        for row in range(2 * clips):
            role, clip = row // clips, row % clips
            part = value[row * rows : (row + 1) * rows]
            if kind < 2:
                part = turn(part, cosines[row], sines[row], head, False)
            part = part.astype(BF16)
            if kind == 0:
                part = part * jnp.asarray(head**-0.5, BF16)
            for group in range(zs):
                held[clip, group ^ z, role, kind] = part[:, group * lanes : (group + 1) * lanes]
    for n, out in enumerate(outs):
        out[...] = held[n // zs, n % zs]


def qkv_call(meta, tokens, other_tokens, mod, tables, weight, bias, zs, head, aligned):
    clips, _, rows, width = tokens.shape
    lanes = width // (2 * zs)
    whole = lambda shape: pl.BlockSpec(shape, lambda t, m: (0,) * len(shape))
    blocks = width // (2 * LANES)
    message = (2, 3, rows, lanes)
    out_shape = [shaped(message, BF16)] * (zs * clips)
    out_shape += [shaped((rows, width), BF16)] * (2 * clips)
    return pl.pallas_call(
        functools.partial(qkv_kernel, zs, head),
        out_shape=out_shape,
        grid_spec=pltpu.PrefetchScalarGridSpec(
            num_scalar_prefetch=1,
            grid=(1,),
            in_specs=[whole(a.shape) for a in (tokens, other_tokens, mod, *tables)]
            + half_specs(width, width, 2 * zs, aligned)
            + half_specs(1, width, 2 * zs, aligned),
            out_specs=[whole(o.shape) for o in out_shape],
            scratch_shapes=[
                pltpu.VMEM((2 * clips * rows, width), BF16),
                pltpu.VMEM((clips, zs, *message), BF16),
            ],
        ),
        compiler_params=params(),
        cost_estimate=cost(
            6 * clips * rows * width * width, 3 * width * width + 32 * rows * width
        ),
        name="norm_qkv",
    )(meta, tokens, other_tokens, mod, *tables, *[weight] * (3 * blocks), *[bias] * (3 * blocks))


def attend_kernel(slots, head, clip, meta, *refs):
    zs = slots // 2
    parts, outs = refs[:zs], refs[zs:slots]
    exact, logs, held, scores, values, sems = refs[slots:]
    copies = [
        pltpu.make_async_copy(parts[k], held.at[pl.ds(2 * k, 2)], sems.at[k])
        for k in range(zs)
    ]
    for copy in copies:
        copy.start()
    for copy in copies:
        copy.wait()
    me, context = meta[0], meta[2 + clip]
    rows, width = held.shape[2], held.shape[3]
    pairs = width // head

    def prepare(frame, _):
        split = split_heads(held[frame ^ me, 2], pairs, head)
        ones = split_heads(jnp.ones((rows, width), BF16), pairs, head)
        for h in range(pairs):
            values[frame, h] = jnp.concatenate([split[h], ones[h]], axis=1)
        return 0

    lax.fori_loop(0, slots, prepare, 0)

    def attend(slot, count):
        queries = split_heads(held[slot, 0], pairs, head)
        total, tops = None, []
        for h in range(pairs):
            peak = None
            for frame in range(count):
                score = dot_nt(queries[h], held[frame ^ me, 1])
                scores[frame, h * rows : (h + 1) * rows] = score
                for at in range(0, rows, LANES):
                    piece = score[:, at : at + LANES]
                    peak = piece if peak is None else jnp.maximum(peak, piece)
            top = jnp.max(peak, axis=1, keepdims=True)
            tops.append(top)
            for frame in range(count):
                power = jnp.exp(scores[frame, h * rows : (h + 1) * rows] - top).astype(BF16)
                term = dot_nn(power, values[frame, h])
                total = term if total is None else total + term
        weight_sum = total[:, width:]
        result = total[:, :width] / weight_sum
        exact[slot] = result
        top = jnp.broadcast_to(tops[0], (rows, width))
        if pairs > 1:
            lane = lax.broadcasted_iota(jnp.int32, (rows, width), 1)
            for h in range(1, pairs):
                top = jnp.where(lane // head >= h, tops[h], top)
        turned = (top + jnp.log(weight_sum)).T
        logs[slot] = jnp.concatenate(
            [turned[h * head : h * head + 1] for h in range(pairs)], axis=1
        )

    def one_frame(frame, _):
        count = jnp.maximum(frame, context - 1) + 1
        for known in range(1, slots + 1):

            @pl.when(count == known)
            def _():
                attend(frame ^ me, known)

        return 0

    lax.fori_loop(0, slots, one_frame, 0)
    for slot in range(slots):
        outs[slot // 2][slot % 2] = exact[slot].astype(BF16)


def attend_call(meta, clip, parts, head):
    zs = len(parts)
    slots = 2 * zs
    rows, width = parts[0].shape[-2:]
    pairs = width // head
    work = slots * slots * rows * rows
    return pl.pallas_call(
        functools.partial(attend_kernel, slots, head, clip),
        out_shape=[shaped((2, rows, width), BF16)] * zs
        + [shaped((slots, rows, width), F32), shaped((slots, 1, pairs * rows), F32)],
        in_specs=[SMEM] + [ANY] * zs,
        out_specs=[VMEM] * (zs + 2),
        scratch_shapes=[
            pltpu.VMEM((slots, 3, rows, width), BF16),
            pltpu.VMEM((slots, pairs * rows, rows), F32),
            pltpu.VMEM((slots, pairs, rows, 2 * width), BF16),
            pltpu.SemaphoreType.DMA((zs,)),
        ],
        compiler_params=params(),
        cost_estimate=cost(work * 16 * width, slots * rows * width * 12, work * pairs),
        name="attend",
    )(meta, *parts)


def attend_grad_kernel(slots, head, clip, meta, *refs):
    zs = slots // 2
    parts, grads = refs[:zs], refs[zs:slots]
    exact, logs = refs[slots], refs[slots + 1]
    outs = refs[slots + 2 : slots + 2 + zs]
    held, grad, query_rows, grad_rows, delta, grad_q, grad_k, grad_v, sems, more = refs[
        slots + 2 + zs :
    ]
    copies = []
    for k in range(zs):
        pair = pl.ds(2 * k, 2)
        copies.append(pltpu.make_async_copy(parts[k], held.at[pair], sems.at[k]))
        copies.append(pltpu.make_async_copy(grads[k], grad.at[pair], more.at[k]))
    for copy in copies:
        copy.start()
    for copy in copies:
        copy.wait()
    me, context = meta[0], meta[2 + clip]
    rows, width = held.shape[2], held.shape[3]
    pairs = width // head

    def prepare(slot, _):
        query_rows[slot] = jnp.concatenate(split_heads(held[slot, 0], pairs, head), axis=0)
        grad_rows[slot] = jnp.concatenate(split_heads(grad[slot], pairs, head), axis=0)
        product = (grad[slot].astype(F32) * exact[slot]).T
        delta[slot] = jnp.concatenate(
            [
                jnp.sum(product[h * head : (h + 1) * head], axis=0, keepdims=True)
                for h in range(pairs)
            ],
            axis=1,
        )
        grad_q[slot] = jnp.zeros((rows, width), F32)
        return 0

    lax.fori_loop(0, slots, prepare, 0)

    def key_frame(frame, _):
        place = frame ^ me
        keys, values = held[place, 1], held[place, 2]
        head_keys = split_heads(keys, pairs, head)
        grad_k[...] = jnp.zeros_like(grad_k)
        grad_v[...] = jnp.zeros_like(grad_v)

        def query_frames(first, count):
            add_k = add_v = None
            for n in range(count):
                slot = (first + n) ^ me
                score = dot_nt(keys, query_rows[slot])
                grad_weight = dot_nt(values, grad_rows[slot])
                weight = jnp.exp(score - logs[slot])
                grad_score = (weight * (grad_weight - delta[slot])).astype(BF16)
                term_v = dot_nn(weight.astype(BF16), grad_rows[slot])
                term_k = dot_nn(grad_score, query_rows[slot])
                add_v = term_v if add_v is None else add_v + term_v
                add_k = term_k if add_k is None else add_k + term_k
                total = grad_q[slot]
                for h in range(pairs):
                    total = total + dot_tn(grad_score[:, h * rows : (h + 1) * rows], head_keys[h])
                grad_q[slot] = total
            grad_v[...] += add_v
            grad_k[...] += add_k

        first = jnp.where(frame < context, 0, frame)
        for size in GROUPS:
            if size > slots:
                continue
            count = (slots - first) // size

            def group_step(n, _, first=first, size=size):
                query_frames(first + n * size, size)
                return 0

            lax.fori_loop(0, count, group_step, 0)
            first = first + count * size
        held[place, 1] = grad_k[...].astype(BF16)
        held[place, 2] = grad_v[...].astype(BF16)
        return 0

    lax.fori_loop(0, slots, key_frame, 0)
    for slot in range(slots):
        out, role = outs[slot // 2], slot % 2
        out[role, 0] = (grad_q[slot] * head**-0.5).astype(BF16)
        out[role, 1] = held[slot, 1]
        out[role, 2] = held[slot, 2]


def attend_grad_call(meta, clip, parts, grads, exact, logs, head):
    zs = len(parts)
    slots = 2 * zs
    rows, width = parts[0].shape[-2:]
    pairs = width // head
    work = slots * slots * rows * rows
    return pl.pallas_call(
        functools.partial(attend_grad_kernel, slots, head, clip),
        out_shape=[shaped((2, 3, rows, width), BF16)] * zs,
        in_specs=[SMEM] + [ANY] * slots + [VMEM, VMEM],
        out_specs=[VMEM] * zs,
        scratch_shapes=[
            pltpu.VMEM((slots, 3, rows, width), BF16),
            pltpu.VMEM((slots, rows, width), BF16),
            pltpu.VMEM((slots, pairs * rows, width), BF16),
            pltpu.VMEM((slots, pairs * rows, width), BF16),
            pltpu.VMEM((slots, 1, pairs * rows), F32),
            pltpu.VMEM((slots, rows, width), F32),
            pltpu.VMEM((rows, width), F32),
            pltpu.VMEM((rows, width), F32),
            pltpu.SemaphoreType.DMA((zs,)),
            pltpu.SemaphoreType.DMA((zs,)),
        ],
        compiler_params=params(),
        cost_estimate=cost(work * 4 * width, slots * rows * width * 2, work * pairs / 10),
        name="attend_grad",
    )(meta, *parts, *grads, exact, logs)


def mixed_places(width, hidden):
    ends = [0]
    for columns in (width // 2, hidden // 2, width, hidden):
        ends.append(ends[-1] + columns)
    return ends


def forward_back_kernel(slots, clip, meta, tokens, cotangent, mod, proj_b, up_b, down_b, *refs):
    zs = slots // 2
    width, hidden_width = tokens.shape[-1], refs[zs + 2].shape[1]
    at_act, at_gtwo, at_hid = mixed_places(width, hidden_width)[1:4]
    parts, swapped, (proj_hbm, up_hbm, down_hbm) = refs[:zs], refs[zs], refs[zs + 1 : zs + 4]
    (
        layer_out, grad_middle_out, row_grads, up_bgrad,
        att_own, att_far, gone_low, n2_own, act_own, mixed,
        held, far, n2_other, gtwo_low, proj, up, down, slope, active, hid, sems,
    ) = refs[zs + 4 :]
    blocks = up.shape[1] // FF_BLOCK
    fetches = [pltpu.make_async_copy(proj_hbm, proj, sems.at[4])]
    for source, target, columns in ((up_hbm, up, True), (down_hbm, down, False)):
        for block in range(blocks):
            at = pl.ds(block * FF_BLOCK, FF_BLOCK)
            at = (slice(None), at) if columns else (at, slice(None))
            fetches.append(
                pltpu.make_async_copy(source.at[at], target.at[at], sems.at[4 + len(fetches)])
            )
    for fetch in fetches[:IN_FLIGHT]:
        fetch.start()

    def fetched(number):
        fetches[number].wait()
        if number + IN_FLIGHT < len(fetches):
            fetches[number + IN_FLIGHT].start()

    me = meta[0]
    parity = me % 2
    rows = tokens.shape[-2]
    lanes = width // slots
    gate_one, shift_two, scale_two, gate_two = (mod[k, clip : clip + 1] for k in range(4))
    for k in range(zs):
        held[(2 * k) ^ me] = parts[k][0]
        held[(2 * k + 1) ^ me] = swapped[k]
        far[k ^ (me // 2)] = parts[k][1]
    attended = jnp.concatenate([held[k] for k in range(slots)], axis=1)
    att_own[...] = jnp.concatenate([held[2 * k + parity] for k in range(zs)], axis=1)
    att_far[...] = jnp.concatenate([far[k] for k in range(zs)], axis=1)
    fetched(0)
    branch_one = dot_nn(attended, proj[...]) + proj_b[...].astype(F32)
    middle = tokens[...].reshape(rows, width).astype(F32) + gate_one * branch_one
    hat_two, inverse_two = norm_parts(middle)
    low_two = (hat_two * (1.0 + scale_two) + shift_two).astype(BF16)
    for block in range(slots):
        store_by_parity(
            n2_own, n2_other, slice(block // 2 * lanes, (block // 2 + 1) * lanes), parity, block,
            low_two[:, block * lanes : (block + 1) * lanes],
        )
    n2_copy = pltpu.make_async_copy(n2_other, mixed.at[:, pl.ds(0, width // 2)], sems.at[2])
    n2_copy.start()
    chunk = hidden_width // slots
    for block in range(blocks):
        at = slice(block * FF_BLOCK, (block + 1) * FF_BLOCK)
        fetched(1 + block)
        hidden = dot_nn(low_two, up[:, at]) + up_b[:, at].astype(F32)
        square = hidden * hidden
        bent = jnp.tanh(GELU_A * (hidden + GELU_B * square * hidden))
        half = 0.5 * (1.0 + bent)
        low = (hidden * half).astype(BF16)
        slope[:, at] = half + (0.5 * GELU_A) * hidden * (1.0 - bent * bent) * (
            1.0 + (3.0 * GELU_B) * square
        )
        active[:, at] = low
        for index in range(block * FF_BLOCK // chunk, (block + 1) * FF_BLOCK // chunk):
            piece = active.at[:, pl.ds(index * chunk, chunk)]
            place = pl.ds(index // 2 * chunk, chunk)

            @pl.when(parity == index % 2)
            def _():
                pltpu.make_async_copy(piece, act_own.at[:, place], sems.at[0]).start()

            @pl.when(parity != index % 2)
            def _():
                pltpu.make_async_copy(
                    piece, mixed.at[:, pl.ds(at_act + index // 2 * chunk, chunk)], sems.at[0]
                ).start()

    branch_two = down_b[...].astype(F32)
    for block in range(blocks):
        at = slice(block * FF_BLOCK, (block + 1) * FF_BLOCK)
        fetched(1 + blocks + block)
        branch_two = branch_two + dot_nn(active[:, at], down[at, :])
    layer_out[...] = (middle + gate_two * branch_two).astype(BF16)
    grad_out = cotangent[...].reshape(rows, width).astype(F32)
    low_grad_two = (grad_out * gate_two).astype(BF16)
    gtwo_low[...] = low_grad_two
    gtwo_copy = pltpu.make_async_copy(gtwo_low, mixed.at[:, pl.ds(at_gtwo, width)], sems.at[3])
    gtwo_copy.start()
    row_grads[3:4] = jnp.sum(grad_out * branch_two, axis=0, keepdims=True)
    row_grads[4:5] = jnp.sum(low_grad_two.astype(F32), axis=0, keepdims=True)
    grad_normed = None
    for block in range(blocks):
        at = slice(block * FF_BLOCK, (block + 1) * FF_BLOCK)
        low = (dot_nt(low_grad_two, down[at, :]) * slope[:, at]).astype(BF16)
        hid[:, at] = low
        pltpu.make_async_copy(
            hid.at[:, at], mixed.at[:, pl.ds(at_hid + block * FF_BLOCK, FF_BLOCK)], sems.at[1]
        ).start()
        up_bgrad[:, at] = jnp.sum(low.astype(F32), axis=0, keepdims=True)
        term = dot_nt(low, up[:, at])
        grad_normed = term if grad_normed is None else grad_normed + term
    grad_middle, grad_shift, grad_scale = norm_pull(grad_normed, hat_two, inverse_two, scale_two)
    grad_middle = grad_middle + grad_out
    grad_middle_out[...] = grad_middle
    low_grad_one = (grad_middle * gate_one).astype(BF16)
    gone_low[...] = low_grad_one
    row_grads[0:1] = jnp.sum(grad_middle * branch_one, axis=0, keepdims=True)
    row_grads[1:2] = grad_shift
    row_grads[2:3] = grad_scale
    row_grads[5:6] = jnp.sum(low_grad_one.astype(F32), axis=0, keepdims=True)
    row_grads[6:8] = jnp.zeros((2, width), F32)
    n2_copy.wait()
    gtwo_copy.wait()
    pltpu.make_async_copy(active, active, sems.at[0]).wait()
    pltpu.make_async_copy(hid, hid, sems.at[1]).wait()


def forward_back_call(
    meta, clip, tokens, cotangent, mod, proj_b, up_b, down_b, parts, swapped, proj, up, down
):
    zs = len(parts)
    slots = 2 * zs
    rows, width = tokens.shape[-2:]
    lanes = width // slots
    hidden = up.shape[1]
    half, half_hidden = width // 2, hidden // 2
    out_shape = [
        shaped((rows, width), BF16),
        shaped((rows, width), F32),
        shaped((8, width), F32),
        shaped((1, hidden), F32),
        shaped((rows, half), BF16),
        shaped((rows, half), BF16),
        shaped((rows, width), BF16),
        shaped((rows, half), BF16),
        shaped((rows, half_hidden), BF16),
        shaped((rows, mixed_places(width, hidden)[4]), BF16),
    ]
    full = lambda shape: pl.BlockSpec(shape, lambda t: (0,) * len(shape))
    pick = pl.BlockSpec((1, 1, rows, width), lambda t: (clip, 0, 0, 0))
    return pl.pallas_call(
        functools.partial(forward_back_kernel, slots, clip),
        grid=(1,),
        out_shape=out_shape,
        in_specs=[SMEM, pick, pick]
        + [full(a.shape) for a in (mod, proj_b, up_b, down_b, *parts, swapped)]
        + [ANY] * 3,
        out_specs=[ANY if k in (8, 9) else full(o.shape) for k, o in enumerate(out_shape)],
        scratch_shapes=[
            pltpu.VMEM((slots, rows, lanes), BF16),
            pltpu.VMEM((zs, rows, lanes), BF16),
            pltpu.VMEM((rows, half), BF16),
            pltpu.VMEM((rows, width), BF16),
            pltpu.VMEM(proj.shape, BF16),
            pltpu.VMEM(up.shape, BF16),
            pltpu.VMEM(down.shape, BF16),
            pltpu.VMEM((rows, hidden), F32),
            pltpu.VMEM((rows, hidden), BF16),
            pltpu.VMEM((rows, hidden), BF16),
            pltpu.SemaphoreType.DMA((5 + 2 * hidden // FF_BLOCK,)),
        ],
        compiler_params=params(),
        cost_estimate=cost(
            4 * rows * width * (width + 2 * hidden),
            4 * width * (width + 2 * hidden),
            rows * hidden,
        ),
        name="feed_forward",
    )(meta, tokens, cotangent, mod, proj_b, up_b, down_b, *parts, swapped, proj, up, down)


def proj_back_kernel(meta, near, far, proj, *outs):
    me = meta[0]
    rows, lanes = near.shape[0], outs[0].shape[2]
    groups = [pl.multiple_of((me ^ (2 * k)) * lanes, lanes) for k in range(len(outs))]
    weight = jnp.concatenate([proj[pl.ds(group, lanes), :] for group in groups], axis=0)
    both = jnp.concatenate([near[...], far[...]], axis=0)
    value = dot_nt(both, weight).astype(BF16)
    for k, out in enumerate(outs):
        for role in range(2):
            out[role] = value[role * rows : (role + 1) * rows, k * lanes : (k + 1) * lanes]


def proj_back_call(meta, near, far, proj, zs):
    rows, width = near.shape
    lanes = width // (2 * zs)
    return pl.pallas_call(
        proj_back_kernel,
        out_shape=[shaped((2, rows, lanes), BF16)] * zs,
        in_specs=[SMEM, VMEM, VMEM, VMEM],
        out_specs=[VMEM] * zs,
        compiler_params=params(),
        cost_estimate=cost(2 * rows * width * width, 2 * width * width + 6 * rows * width),
        name="proj_back",
    )(meta, near, far, proj)


def qkv_grad_kernel(zs, head, clip, meta, *refs):
    tables, refs = refs[:4], refs[4:]
    blocks = refs[zs].shape[0] // (2 * LANES)
    parts, weights = refs[:zs], refs[zs : zs + 3 * blocks]
    near_out, far_out, near_sum, far_sum, bias_out, held = refs[zs + 3 * blocks :]
    rows, width = near_sum.shape
    clips = tables[0].shape[0] // 2
    z = meta[0] // 2
    cosines = [turn_table(tables[0], tables[2], role * clips + clip, head) for role in range(2)]
    sines = [turn_table(tables[1], tables[3], role * clips + clip, head) for role in range(2)]
    for k in range(zs):
        held[k ^ z] = parts[k][...]
    totals = [None, None]
    bias_out[...] = jnp.zeros_like(bias_out)
    half = width // 2
    for kind in range(3):
        weight = jnp.concatenate([w[...] for w in weights[kind * blocks : (kind + 1) * blocks]], axis=1)
        sums = None
        for role, out in enumerate((near_out, far_out)):
            low = jnp.concatenate([held[k, role, kind] for k in range(zs)], axis=1)
            if kind < 2:
                low = turn(low.astype(F32), cosines[role], sines[role], head, True).astype(BF16)
            out[:, kind * half : (kind + 1) * half] = low
            column = jnp.sum(low.astype(F32), axis=0, keepdims=True)
            sums = column if sums is None else sums + column
            term = dot_nt(low, weight)
            totals[role] = term if totals[role] is None else totals[role] + term
        bias_out[kind : kind + 1] = sums
    near_sum[...] = totals[0]
    far_sum[...] = totals[1]


def qkv_grad_call(meta, clip, tables, parts, weight, head, aligned):
    zs = len(parts)
    rows, lanes = parts[0].shape[-2:]
    width = 2 * zs * lanes
    blocks = width // (2 * LANES)
    whole = lambda shape: pl.BlockSpec(shape, lambda t, m: (0,) * len(shape))
    out_shape = [
        shaped((rows, 3 * width // 2), BF16),
        shaped((rows, 3 * width // 2), BF16),
        shaped((rows, width), F32),
        shaped((rows, width), F32),
        shaped((8, width // 2), F32),
    ]
    return pl.pallas_call(
        functools.partial(qkv_grad_kernel, zs, head, clip),
        out_shape=out_shape,
        grid_spec=pltpu.PrefetchScalarGridSpec(
            num_scalar_prefetch=1,
            grid=(1,),
            in_specs=[whole(a.shape) for a in (*tables, *parts)]
            + half_specs(width, width, 2 * zs, aligned),
            out_specs=[whole(o.shape) for o in out_shape],
            scratch_shapes=[pltpu.VMEM((zs, 2, 3, rows, lanes), BF16)],
        ),
        compiler_params=params(),
        cost_estimate=cost(0.6 * rows * width * width, width * width),
        name="qkv_grad",
    )(meta, *tables, *parts, *[weight] * (3 * blocks))


def norm_grad_kernel(tokens, mod, *refs):
    clips = tokens.shape[0]
    nears, fars, middles = refs[:clips], refs[clips : 2 * clips], refs[2 * clips : 3 * clips]
    tokens_grad, row_grads = refs[3 * clips :]
    for c in range(clips):
        hat, inverse = norm_parts(tokens[c, 0].astype(F32))
        grad, shift, scale = norm_pull(
            nears[c][...] + fars[c][...], hat, inverse, mod[1, c : c + 1]
        )
        tokens_grad[c, 0] = grad + middles[c][...]
        row_grads[c, 0:1] = shift
        row_grads[c, 1:2] = scale
        row_grads[c, 2:8] = jnp.zeros((6, tokens.shape[-1]), F32)


def norm_grad_call(tokens, mod, nears, fars, middles):
    clips, _, rows, width = tokens.shape
    return pl.pallas_call(
        norm_grad_kernel,
        out_shape=[shaped(tokens.shape, F32), shaped((clips, 8, width), F32)],
        in_specs=[VMEM] * (2 + 3 * clips),
        out_specs=[VMEM, VMEM],
        compiler_params=params(),
        cost_estimate=cost(clips * rows * width * 3, clips * rows * width * 2),
        name="norm_grad",
    )(tokens, mod, *nears, *fars, *middles)


def weight_grad_kernel(jobs, clip_size, zs, split, meta, *refs):
    arrays_n = sum(2 * job[0] for job in jobs)
    outs_n = 4 if split else 1
    arrays, outs = refs[:arrays_n], refs[arrays_n : arrays_n + outs_n]
    held, out_sems, in_sems = refs[arrays_n + outs_n : arrays_n + outs_n + 3]
    scratch = refs[arrays_n + outs_n + 3 :]
    _, _, _, height, cols = held.shape
    tile = zs * height
    z = meta[0] // 2
    clip = meta[1] if split else 0

    def send_out(slot, tiles, repeat, first, tall):
        for e in range(clip_size):
            for half, first_bit in enumerate((1, clip_size // 2) if split else (0,)):
                keep, send = (outs[2 * half], outs[2 * half + 1]) if split else (outs[0], None)
                rest = [k for k in range(clip_size) if not k & first_bit]
                if e & first_bit:
                    out, place = send, rest.index(e ^ first_bit)
                else:
                    out, place = keep, rest.index(e)
                span = zs // 2 if split else zs
                low, high = half * span, (half + 1) * span
                if not tall:
                    pltpu.make_async_copy(
                        held.at[slot, e, pl.ds(low, span)],
                        out.at[place, :, pl.ds(first, height)],
                        out_sems.at[slot],
                    ).start()
                    continue
                for block in range(zs):
                    row = repeat * zs + block
                    k = row // tiles
                    if low <= k < high:
                        pltpu.make_async_copy(
                            held.at[slot, e, block],
                            out.at[place, k - low, pl.ds(first + row % tiles * height, height)],
                            out_sems.at[slot],
                        ).start()

    copies = []
    at = 0
    for job, (count, _, _, _, _, places) in enumerate(jobs):
        left, right = scratch[2 * job : 2 * job + 2]
        depth = left.shape[0] // count
        for n in range(2 * count):
            target = left if n < count else right
            source = arrays[at + n]
            if source.shape[1] != target.shape[1]:
                source = source.at[:, pl.ds(places[n], target.shape[1])]
            copies.append(
                pltpu.make_async_copy(
                    source,
                    target.at[pl.ds(n % count * depth, depth)],
                    in_sems.at[at + n],
                )
            )
        at += 2 * count
    for copy in copies:
        copy.start()

    at = number = 0
    for job, (count, lane_parts, tall, tiles, first, _) in enumerate(jobs):
        left, right = scratch[2 * job : 2 * job + 2]
        block = left.shape[1] // zs
        for n in range(2 * count):
            copies[at + n].wait()
        at += 2 * count
        wide = right.shape[1] // (tiles * lane_parts if not tall else 1)
        part = wide // clip_size
        for repeat in range(tiles):
            slot = number % 2
            if number >= 2:
                pltpu.make_async_copy(held.at[slot], held.at[slot], out_sems.at[slot]).wait()
            for lane_part in range(lane_parts):
                if tall:
                    per = zs // tiles
                    rows = [
                        left[:, pl.ds(pl.multiple_of(((repeat * per + n) ^ z) * block, block), block)]
                        for n in range(per)
                    ]
                    rows = rows[0] if per == 1 else jnp.concatenate(rows, axis=1)
                    value = dot_tn(rows, right[...]).astype(BF16)
                else:
                    group = repeat + lane_part
                    value = dot_tn(
                        left[...], right[:, group * wide : (group + 1) * wide]
                    ).astype(BF16)
                for p in range(clip_size):
                    lanes = slice(lane_part * part, (lane_part + 1) * part)
                    piece = value[:, p * part : (p + 1) * part]
                    for k in range(zs):
                        source = piece[k * height : (k + 1) * height]
                        held[slot, p ^ clip, k if tall else k ^ z, :, lanes] = source
            send_out(slot, tiles, repeat, first if tall else first + repeat * height, tall)
            number += 1
    for slot in range(min(number, 2)):
        pltpu.make_async_copy(held.at[slot], held.at[slot], out_sems.at[slot]).wait()


def weight_grad_call(meta, products, clip_size, zs, split, name):
    jobs, arrays, scratch = [], [], []
    first = flops = 0
    tile = min(p[0][0][2] for p in products)
    height = tile // zs
    piece = None
    for lefts, rights, lane_parts, tall in products:
        depth, total = rights[0][0].shape[0], rights[0][2]
        rows = lefts[0][2]
        if tall:
            tiles, piece = rows // tile, total // clip_size
        elif lane_parts > 1:
            tiles, piece = 1, total // clip_size
        else:
            tiles, piece = total // (2 * tile), 2 * tile // clip_size
        count = len(lefts)
        places = tuple(a[1] for a in lefts + rights)
        jobs.append((count, lane_parts, tall, tiles, first, places))
        first += height * tiles
        arrays += [a[0] for a in lefts + rights]
        flops += 2 * count * depth * rows * total
        scratch += [
            pltpu.VMEM((count * depth, rows), BF16),
            pltpu.VMEM((count * depth, total), BF16),
        ]
    if split:
        outs = [shaped((clip_size // 2, zs // 2, first, piece), BF16)] * 4
    else:
        outs = [shaped((clip_size, zs, first, piece), BF16)]
    return pl.pallas_call(
        functools.partial(weight_grad_kernel, tuple(jobs), clip_size, zs, split),
        out_shape=outs,
        in_specs=[SMEM] + [ANY] * len(arrays),
        out_specs=[ANY] * len(outs),
        scratch_shapes=[
            pltpu.VMEM((2, clip_size, zs, height, piece), BF16),
            pltpu.SemaphoreType.DMA((2,)),
            pltpu.SemaphoreType.DMA((len(arrays),)),
        ]
        + scratch,
        compiler_params=params(),
        cost_estimate=cost(flops, flops / 512),
        name=name,
    )(meta, *arrays)


def place_kernel(jobs, pieces, meta, *refs):
    parts, outs = refs[:pieces], refs[pieces:]
    clip = meta[1]
    cols = parts[0].shape[1]
    for e in range(pieces):
        first = 0
        for out, (height, repeats, tall) in zip(outs, jobs):
            for repeat in range(repeats):
                base = 0 if tall else repeat * cols * pieces
                target = pl.ds(pl.multiple_of(base + (clip ^ e) * cols, cols), cols)
                value = parts[e][first : first + height].astype(F32)
                if tall:
                    out[repeat * height : (repeat + 1) * height, target] = value
                else:
                    out[:, target] = value
                first += height


def place_call(meta, parts, jobs, outs):
    return pl.pallas_call(
        functools.partial(place_kernel, jobs, len(parts)),
        out_shape=outs,
        in_specs=[SMEM] + [VMEM] * len(parts),
        out_specs=[VMEM] * len(outs),
        compiler_params=params(),
        cost_estimate=cost(0, sum(o.size * 4 for o in outs)),
        name="place_grads",
    )(meta, *parts)


def place_qkv_kernel(meta, *refs):
    parts, out = refs[:-1], refs[-1]
    parity, clip = meta[0] % 2, meta[1]
    thirds = out.shape[1] // 3
    for e, part in enumerate(parts):
        for role in range(2):
            block = 2 * (clip ^ e) + (parity ^ role)
            for kind in range(3):
                at = pl.ds(pl.multiple_of(kind * thirds + block * LANES, LANES), LANES)
                out[:, at] = part[role, :, kind * LANES : (kind + 1) * LANES].astype(F32)


def place_qkv_call(meta, parts, out):
    return pl.pallas_call(
        place_qkv_kernel,
        out_shape=out,
        in_specs=[SMEM] + [VMEM] * len(parts),
        out_specs=VMEM,
        compiler_params=params(),
        cost_estimate=cost(0, out.size * 6),
        name="place_qkv_grad",
    )(meta, *parts)


def exchange(array, axis, size, distance):
    return lax.ppermute(array, axis, [(k, k ^ distance) for k in range(size)])


def after(value, *others):
    return lax.optimization_barrier((value, *others))


def spread(slots_out, seq_size):
    return [slots_out[0]] + [
        exchange(slots_out[k], "seq", seq_size, 2 * k) for k in range(1, seq_size // 2)
    ]


def add_low(left, right):
    return (left.astype(F32) + right.astype(F32)).astype(BF16)


def step_out(pairs, bits, size):
    return [exchange(send, "clip", size, bit) for (_, send), bit in zip(pairs, bits)]


def step_in(pairs, arrived):
    left = []
    for (keep, _), new in zip(pairs, arrived):
        half = keep.shape[0] // 2
        if half:
            left.append((add_low(keep[:half], new[:half]), add_low(keep[half:], new[half:])))
        else:
            left.append((add_low(keep[0], new[0]), None))
    return left


def clip_orders(clip_size):
    down = [1 << k for k in reversed(range(clip_size.bit_length() - 1))]
    return [1] + down[:-1], down


def z_out(blocks, seq_size):
    return exchange(jnp.stack(blocks[1::2]), "seq", seq_size, seq_size // len(blocks))


def z_in(blocks, arrived):
    return [add_low(keep, new) for keep, new in zip(blocks[0::2], arrived)]


def sum_z(blocks, seq_size):
    while len(blocks) > 1:
        blocks = z_in(blocks, z_out(blocks, seq_size))
    return blocks[0]


def gather_pieces(piece, clip_size):
    return [piece] + [exchange(piece, "clip", clip_size, d) for d in range(1, clip_size)]


def double(array, axis, size):
    bit = 1
    while bit < size:
        array = jnp.concatenate([array, exchange(array, axis, size, bit)])
        bit *= 2
    return array


def silu_act(values_in):
    return values_in * jax.nn.sigmoid(values_in)


def rotary_tables(stamps, patch_count, head):
    lane = jnp.arange(LANES, dtype=jnp.int32)
    quarter = head // 4
    freqs = 10000.0 ** (-(lane % quarter).astype(F32) / quarter)
    sign = jnp.where(lane % head < head // 2, -1.0, 1.0).astype(F32)
    tables = []
    for places in (stamps, jnp.arange(patch_count, dtype=jnp.int32)):
        angles = places.astype(F32)[:, None] * freqs[None, :]
        tables += [jnp.cos(angles), jnp.sin(angles) * sign[None, :]]
    return tables


def on_device(
    tokens,
    cotangent,
    context_count,
    noise_level,
    frame_time,
    level_table,
    mod_weight,
    mod_bias,
    qkv_weight,
    qkv_bias,
    proj_weight,
    proj_bias,
    up_weight,
    up_bias,
    down_weight,
    down_bias,
):
    seq_size, clip_size = lax.axis_size("seq"), lax.axis_size("clip")
    me, mine = lax.axis_index("seq"), lax.axis_index("clip")
    clips, _, rows, width = tokens.shape
    head = width // HEADS
    hidden = up_weight.shape[1]
    zs = seq_size // 2
    me = me.astype(jnp.int32)
    mine = mine.astype(jnp.int32)
    parity = me % 2
    aligned = (width // seq_size) % LANES == 0
    stamps = jnp.stack([noise_level[:, 0], frame_time[:, 0]])
    other_stamps = exchange(stamps, "seq", seq_size, 1)
    other_tokens = exchange(tokens, "seq", seq_size, 1)
    meta = jnp.concatenate([jnp.stack([me, mine]), context_count])
    levels = jnp.concatenate(
        [
            jnp.where(me < context_count, 0, stamps[0]),
            jnp.where((me ^ 1) < context_count, 0, other_stamps[0]),
        ]
    )
    levels_used = levels[:clips]
    mod_bias_row = mod_bias[None]
    mod_one, condition = modulation_call(levels, level_table, mod_weight, mod_bias_row, 0, 2)
    condition = condition[:clips]
    tables = rotary_tables(jnp.concatenate([stamps[1], other_stamps[1]]), rows, head)
    qkv_bias_row = qkv_bias[None]
    if aligned:
        weight_half, bias_half = qkv_weight, qkv_bias_row
    else:
        weight_half = half_columns(qkv_weight, seq_size, parity)
        bias_half = half_columns(qkv_bias_row, seq_size, parity)

    swap = lambda array: exchange(array, "seq", seq_size, 1)
    full = lambda array: (array, 0, array.shape[1])
    at_n2, at_act, at_gtwo, at_hid, _ = mixed_places(width, hidden)
    out = qkv_call(
        meta, tokens, other_tokens, mod_one, tables, weight_half, bias_half, zs, head, aligned
    )
    normed = out[zs * clips :]
    parts = [spread(out[:zs], seq_size)]
    mod_two, _ = modulation_call(
        levels[:clips], level_table, mod_weight, mod_bias_row, 2, 4
    )
    proj_row, up_row, down_row = proj_bias[None], up_bias[None], down_bias[None]
    parts[0], mod_two, proj_row, up_row, down_row = after(
        parts[0], mod_two, proj_row, up_row, down_row
    )
    exact, logs, attended, crossed = [], [], [], []
    for c in range(clips):
        sends = out[(c + 1) * zs : (c + 2) * zs] if c < clips - 1 else None
        if c < clips - 1:
            parts.append(spread(sends, seq_size))
        done = attend_call(meta, c, parts[c], head)
        exact.append(done[zs])
        logs.append(done[zs + 1])
        sends = done[:zs]
        if c < clips - 1:
            sends, parts[c + 1] = after(sends, parts[c + 1])
        if c:
            sends, attended[-1] = after(sends, attended[-1])
            crossed.append(swap(jnp.stack([a[1] for a in attended[-1]])))
        attended.append(spread(sends, seq_size))
    layer, middles, row_grads, up_bgrads, saved, mixed, far_ones, grads = ([] for _ in range(8))
    for c in range(clips):
        if c:
            meta, grads[-1][0] = after(meta, grads[-1][0])
        out = forward_back_call(
            meta, c, tokens, cotangent, mod_two, proj_row, up_row, down_row, attended[c],
            crossed[c], proj_weight, up_weight, down_weight,
        )
        layer.append(out[0])
        middles.append(out[1])
        row_grads.append(out[2])
        up_bgrads.append(out[3])
        gone, mine_mixed = out[6], out[9]
        if c < clips - 1:
            gone, mine_mixed, attended[c + 1] = after(gone, mine_mixed, attended[c + 1])
            crossed.append(swap(jnp.stack([a[1] for a in attended[c + 1]])))
        if c:
            gone, mine_mixed, grads[-1], mixed[-1] = after(gone, mine_mixed, grads[-1], mixed[-1])
        far_ones.append(swap(gone))
        if c < clips - 1:
            far_ones[-1], crossed[-1] = after(far_ones[-1], crossed[-1])
        saved.append((out[4], out[5], gone, out[7], out[8]))
        if c == clips - 1:
            far_ones[-1], mine_mixed = after(far_ones[-1], mine_mixed)
        back = list(proj_back_call(meta, gone, far_ones[c], proj_weight, zs))
        if c < clips - 1:
            back[0], mine_mixed = after(back[0], mine_mixed)
        mixed.append([mine_mixed, swap(mine_mixed)])
        grads.append(spread(back, seq_size))
    row = width // seq_size
    orders = clip_orders(clip_size)
    steps = len(orders[0])
    products = [([], [], 1, False), ([], [], 1, True), ([], [], 1, False)]
    for c in range(clips):
        att_own, att_far, gone, n2_own, act_own = saved[c]
        own, far = mixed[c]
        products[0][0].extend([full(att_own), full(att_far)])
        products[0][1].extend([full(gone), full(far_ones[c])])
        products[1][0].extend([full(act_own), (far, at_act, hidden // 2)])
        products[1][1].extend([(own, at_gtwo, width), (far, at_gtwo, width)])
        products[2][0].extend([full(n2_own), (far, at_n2, width // 2)])
        products[2][1].extend([(own, at_hid, hidden), (far, at_hid, hidden)])
    meta, grads[-1][0] = after(meta, grads[-1][0])
    (shares,) = weight_grad_call(meta, products, clip_size, zs, False, "weight_grads")
    meta, shares = after(meta, shares)
    summed = lax.psum_scatter(
        shares.reshape(-1, shares.shape[-1]), "clip", scatter_dimension=0, tiled=True
    ).reshape(shares.shape[1:])
    returned = []
    for c in range(clips):
        if c:
            meta, returned[-1][0] = after(meta, returned[-1][0])
        out = attend_grad_call(meta, c, parts[c], grads[c], exact[c], logs[c], head)
        if c < clips - 1:
            out, grads[c + 1] = after(out, grads[c + 1])
        else:
            out, returned[-1] = after(out, returned[-1])
        returned.append(spread(out, seq_size))
    turns = list(zip(*orders))
    grad_rights, nears, fars, qkv_bgrads = [], [], [], []
    for c in range(clips):
        if c == 0:
            meta, returned[-1][0] = after(meta, returned[-1][0])
        out = qkv_grad_call(meta, c, tables, returned[c], weight_half, head, aligned)
        grad_rights.extend(out[:2])
        nears.append(out[2])
        fars.append(swap(out[3]))
        qkv_bgrads.append(out[4][:3])
    tokens_grad, late_rows = norm_grad_call(tokens, mod_one, nears, fars, middles)
    blocks = list(summed)
    if len(blocks) > 1:
        landed = z_out(blocks, seq_size)
        late_rows, landed = after(late_rows, landed)
        blocks = z_in(blocks, landed)
    level_rows = jnp.stack([levels_used // 32, levels_used % 32]).astype(F32)
    level_rows = jnp.concatenate([level_rows, jnp.zeros((2, width - clips), F32)], axis=1)
    mod_rows = []
    for c in range(clips):
        mod_rows += [late_rows[c, 0:2], row_grads[c][0:4]]
    bias_rows = [
        sum(qkv_bgrads).reshape(3 * width // 2),
        jnp.zeros((width // 2,), F32),
        sum(up_bgrads).reshape(hidden),
        sum(r[4] for r in row_grads),
        sum(r[5] for r in row_grads),
    ]
    bias_rows = jnp.concatenate(bias_rows).reshape(-1, width)
    late = jnp.concatenate([condition, level_rows] + mod_rows + [bias_rows], axis=0)
    start, stop = clips + 2, clips + 2 + 6 * clips
    late = double(late.astype(BF16)[None], "seq", seq_size)
    blocks = list(summed)
    lefts = [normed[role * clips + c] for c in range(clips) for role in range(2)]
    if aligned:
        shares = weight_grad_call(
            meta,
            [([full(a) for a in lefts], [full(a) for a in grad_rights], 3, False)],
            clip_size,
            zs,
            True,
            "qkv_weight_grad",
        )
        pairs_qkv = [shares[:2], shares[2:]]
        arrived = step_out(pairs_qkv, turns[0], clip_size)
        if len(blocks) > 1:
            landed = z_out(blocks, seq_size)
            arrived, landed = after(arrived, landed)
            blocks = z_in(blocks, landed)
        pairs_qkv = step_in(pairs_qkv, arrived)
        for bits in turns[1:]:
            pairs_qkv = step_in(pairs_qkv, step_out(pairs_qkv, bits, clip_size))
    own_sums = jnp.sum(
        late[:, stop:].astype(F32).reshape(zs, 2, late.shape[1] - stop, width), axis=0
    ).astype(BF16)
    sums_rows = 2 * own_sums.shape[1]
    message = jnp.concatenate(
        [late[:, :stop].reshape(seq_size * stop, width), own_sums.reshape(sums_rows, width)]
    )
    late = double(message[None], "clip", clip_size)
    piece = sum_z(blocks, seq_size)
    if aligned:
        pairs_qkv, late = after(pairs_qkv, late)
        blocks = [*pairs_qkv[0][0], *pairs_qkv[1][0]]
        if len(blocks) > 1:
            landed = z_out(blocks, seq_size)
            landed, late = after(landed, late)
            blocks = z_in(blocks, landed)
    own_sums = jnp.sum(late[:, seq_size * stop :].astype(F32), axis=0).reshape(2, -1)
    late = late[:, : seq_size * stop].reshape(clip_size * seq_size, stop, width)
    devices = clip_size * seq_size
    grad_modulation = late[:, start:].reshape(devices * clips, 6 * width)
    half_bias = own_sums[:, : 3 * width // 2].reshape(2, 3, zs, 1, width // seq_size)
    bias_sums = jnp.sum(own_sums, axis=0)[2 * width :]
    qkv_bias_sums = jnp.where(
        parity == 0,
        jnp.concatenate([half_bias[0], half_bias[1]], axis=2),
        jnp.concatenate([half_bias[1], half_bias[0]], axis=2),
    ).reshape(3 * width)
    all_condition = late[:, :clips].reshape(devices * clips, width).astype(F32)
    codes = late[:, clips:start, :clips].astype(jnp.int32)
    all_levels = (codes[:, 0] * 32 + codes[:, 1]).reshape(devices * clips)
    all_active, silu_pull = jax.vjp(silu_act, all_condition)
    my_active = lax.dynamic_slice_in_dim(all_active, me * row, row, axis=1).astype(BF16)
    mod_wgrad = lax.dot_general(
        my_active, grad_modulation, (((0,), (0,)), ((), ())), preferred_element_type=F32
    )
    (grad_condition,) = silu_pull(
        lax.dot_general(
            grad_modulation, mod_weight, (((1,), (1,)), ((), ())), preferred_element_type=F32
        )
    )
    table_row = level_table.shape[0] // seq_size
    onehot = (
        all_levels[:, None] == (me * table_row + jnp.arange(table_row, dtype=jnp.int32))[None, :]
    ).astype(F32)
    table_grad = lax.dot_general(
        onehot,
        grad_condition,
        (((0,), (0,)), ((), ())),
        precision=HIGHEST_PRECISION,
        preferred_element_type=F32,
    )
    mod_sums = jnp.sum(grad_modulation.astype(F32), axis=0)

    def own_part(vector):
        size = vector.shape[0] // seq_size
        return lax.dynamic_slice_in_dim(vector, me * size, size, axis=0)

    mod_bgrad = own_part(mod_sums)
    qkv_bgrad = own_part(qkv_bias_sums)
    up_bgrad = own_part(bias_sums[:hidden])
    down_bgrad = own_part(bias_sums[hidden : hidden + width])
    proj_bgrad = own_part(bias_sums[hidden + width : hidden + 2 * width])
    if aligned:
        pieces = gather_pieces(piece, clip_size)
        if len(blocks) > 1:
            landed = z_out(blocks, seq_size)
            landed, mod_wgrad, table_grad = after(landed, mod_wgrad, table_grad)
            blocks = z_in(blocks, landed)
        piece = sum_z(blocks, seq_size).reshape(2, row, 3 * LANES)
        own_rows = lax.dynamic_index_in_dim(piece, parity, 0, keepdims=False)
        far_rows = swap(lax.dynamic_index_in_dim(piece, 1 - parity, 0, keepdims=False))
        far_rows, pieces = after(far_rows, pieces)
        pieces_qkv = gather_pieces(jnp.stack([own_rows, far_rows]), clip_size)
    else:
        pieces = gather_pieces(piece, clip_size)
        share = sum(
            lax.dot_general(left, right, (((0,), (0,)), ((), ())), preferred_element_type=F32)
            for left, right in zip(lefts, grad_rights)
        ).astype(BF16)
        share = share.reshape(width, 3, zs, 1, width // seq_size)
        blank = jnp.zeros_like(share)
        share = jnp.where(
            parity == 0,
            jnp.concatenate([share, blank], axis=3),
            jnp.concatenate([blank, share], axis=3),
        ).reshape(width, 3 * width)
        qkv_wgrad = lax.psum(
            lax.psum_scatter(share, "seq", scatter_dimension=0, tiled=True), "clip"
        ).astype(F32)

    proj_wgrad, down_wgrad, up_wgrad = place_call(
        meta,
        pieces,
        (
            (row, 1, False),
            (row, hidden // width, True),
            (row, hidden // width, False),
        ),
        [shaped((row, width), F32), shaped((hidden // seq_size, width), F32), shaped((row, hidden), F32)],
    )
    if aligned:
        pieces_qkv, proj_wgrad = after(pieces_qkv, proj_wgrad)
        qkv_wgrad = place_qkv_call(meta, pieces_qkv, shaped((row, 3 * width), F32))
    layer_out = jnp.stack(layer)[:, None]
    return (
        layer_out,
        tokens_grad,
        table_grad,
        mod_wgrad,
        mod_bgrad,
        qkv_wgrad,
        qkv_bgrad,
        proj_wgrad,
        proj_bgrad,
        up_wgrad,
        up_bgrad,
        down_wgrad,
        down_bgrad,
    )


def solution(mesh):
    placed = (
        P("clip", "seq", None, None),
        P("clip", "seq", None, None),
        P("clip"),
        P("clip", "seq"),
        P("clip", "seq"),
    ) + (P(),) * 11
    return jax.shard_map(
        on_device,
        mesh=mesh,
        in_specs=placed,
        out_specs=(
            P("clip", "seq", None, None),
            P("clip", "seq", None, None),
            P("seq", None),
            P("seq", None),
            P("seq"),
            P("seq", None),
            P("seq"),
            P("seq", None),
            P("seq"),
            P("seq", None),
            P("seq"),
            P("seq", None),
            P("seq"),
        ),
        check_vma=False,
    )
```

```python
import functools

import jax
import jax.numpy as jnp
from jax import lax
from jax.experimental import pallas as pl
from jax.experimental.pallas import tpu as pltpu
from jax.sharding import PartitionSpec as P

HEADS = 16
EPS = 1e-06
HIGHEST_PRECISION = lax.Precision.HIGHEST
F32 = jnp.float32
BF16 = jnp.bfloat16
ANY = pl.BlockSpec(memory_space=pltpu.HBM)
VMEM = pl.BlockSpec(memory_space=pltpu.VMEM)
SMEM = pl.BlockSpec(memory_space=pltpu.SMEM)
LANES = 128
BLOCK = 256
FF_BLOCK = 1024
IN_FLIGHT = 3
JOBS_AHEAD = 2
GROUPS = (8, 4, 2, 1)
GELU_A = 0.7978845608028654
GELU_B = 0.044715
WEIGHT = 1.0
VMEM_BYTES = 62 << 20


def shaped(shape, dtype):
    return jax.ShapeDtypeStruct(shape, dtype)


def params():
    return pltpu.CompilerParams(vmem_limit_bytes=VMEM_BYTES)


def cost(flops, moved, transcendentals=0):
    return pl.CostEstimate(
        flops=int(flops * WEIGHT),
        bytes_accessed=int(moved * WEIGHT),
        transcendentals=int(transcendentals * WEIGHT),
    )


def dot_nn(left, right):
    return lax.dot_general(left, right, (((1,), (0,)), ((), ())), preferred_element_type=F32)


def dot_nt(left, right):
    return lax.dot_general(left, right, (((1,), (1,)), ((), ())), preferred_element_type=F32)


def dot_tn(left, right):
    return lax.dot_general(left, right, (((0,), (0,)), ((), ())), preferred_element_type=F32)


def split_heads(values, pairs, head):
    if pairs == 1:
        return [values]
    lane = lax.broadcasted_iota(jnp.int32, values.shape, 1)
    return [jnp.where(lane // head == h, values, jnp.zeros_like(values)) for h in range(pairs)]


def swap_halves(values, head):
    half = head // 2
    lane = lax.broadcasted_iota(jnp.int32, values.shape, 1)
    ahead = pltpu.roll(values, values.shape[1] - half, 1)
    behind = pltpu.roll(values, half, 1)
    return jnp.where(lax.rem(lane, head) < half, ahead, behind)


def turn(values, cosine, signed_sine, head, back):
    parts = []
    for at in range(0, values.shape[1], LANES):
        piece = values[:, at : at + LANES]
        other = swap_halves(piece, head) * signed_sine
        parts.append(piece * cosine - other if back else piece * cosine + other)
    return jnp.concatenate(parts, axis=1)


def norm_parts(values):
    center = jnp.mean(values, axis=-1, keepdims=True)
    offset = values - center
    spread = jnp.mean(offset * offset, axis=-1, keepdims=True)
    inverse = lax.rsqrt(spread + EPS)
    return offset * inverse, inverse


def norm_pull(grad, hat, inverse, scale_row):
    grad_shift = jnp.sum(grad, axis=0, keepdims=True)
    grad_scale = jnp.sum(grad * hat, axis=0, keepdims=True)
    inner = grad * (1.0 + scale_row)
    mean_one = jnp.mean(inner, axis=-1, keepdims=True)
    mean_two = jnp.mean(inner * hat, axis=-1, keepdims=True)
    return inverse * (inner - mean_one - hat * mean_two), grad_shift, grad_scale


def store_by_parity(own_ref, other_ref, where, parity, block_index, value):
    own = parity == block_index % 2

    @pl.when(own)
    def _():
        own_ref[:, where] = value

    @pl.when(jnp.logical_not(own))
    def _():
        other_ref[:, where] = value


def modulation_kernel(meta, table, weight, bias, out, condition_out, low):
    rows, levels = out.shape[1], table.shape[0]

    @pl.when(pl.program_id(0) == 0)
    def _():
        lane = lax.broadcasted_iota(jnp.int32, (1, levels), 1)
        picked = jnp.concatenate(
            [jnp.where(lane == meta[row], 1.0, 0.0) for row in range(rows)], axis=0
        )
        condition = dot_nn(picked.astype(BF16), table[...])
        condition_out[...] = condition
        low[...] = silu_act(condition).astype(BF16)

    out[0] = dot_nn(low[...], weight[...]) + bias[...].astype(F32)


def modulation_call(levels, table, weight, bias, first, parts):
    rows, width = levels.shape[0], table.shape[1]
    return pl.pallas_call(
        modulation_kernel,
        grid=(parts,),
        out_shape=[shaped((parts, rows, width), F32), shaped((rows, width), F32)],
        in_specs=[
            SMEM,
            pl.BlockSpec(table.shape, lambda t: (0, 0)),
            pl.BlockSpec((width, width), lambda t: (0, first + t)),
            pl.BlockSpec((1, width), lambda t: (0, first + t)),
        ],
        out_specs=[
            pl.BlockSpec((1, rows, width), lambda t: (t, 0, 0)),
            pl.BlockSpec((rows, width), lambda t: (0, 0)),
        ],
        scratch_shapes=[pltpu.VMEM((rows, width), BF16)],
        compiler_params=params(),
        cost_estimate=cost(0, 2 * (parts + 1) * width * width),
        name="modulation",
    )(levels, table, weight, bias)


def turn_table(temporal, spatial, row, head):
    lane = lax.broadcasted_iota(jnp.int32, spatial.shape, 1)
    timed = lax.rem(lane, head // 2) < head // 4
    return jnp.where(timed, temporal[row : row + 1], spatial[...])


def half_columns(weight, groups, parity):
    rows, total = weight.shape
    view = weight.reshape(rows, 3, groups // 2, 2, total // (3 * groups))
    return lax.dynamic_index_in_dim(view, parity, 3, keepdims=False).reshape(rows, total // 2)


def half_specs(height, width, groups, aligned):
    specs = []
    for kind in range(3):
        for block in range(width // (2 * LANES)):
            if aligned:
                specs.append(
                    pl.BlockSpec(
                        (height, LANES), lambda t, m, k=kind, b=block: (0, k * groups + 2 * b + m[0] % 2)
                    )
                )
            else:
                specs.append(
                    pl.BlockSpec(
                        (height, LANES),
                        lambda t, m, k=kind, b=block: (0, k * (width // (2 * LANES)) + b),
                    )
                )
    return specs


def qkv_kernel(zs, head, meta, tokens, other_tokens, mod, *refs):
    tables, refs = refs[:4], refs[4:]
    blocks = tokens.shape[-1] // (2 * LANES)
    weights, biases = refs[: 3 * blocks], refs[3 * blocks : 6 * blocks]
    clips, _, rows, width = tokens.shape
    outs = refs[6 * blocks : 6 * blocks + zs * clips]
    normed_outs, (normed, held) = refs[6 * blocks + zs * clips : -2], refs[-2:]
    cosines = [turn_table(tables[0], tables[2], row, head) for row in range(2 * clips)]
    sines = [turn_table(tables[1], tables[3], row, head) for row in range(2 * clips)]
    lanes = width // (2 * zs)
    z = meta[0] // 2
    for row in range(2 * clips):
        role, clip = row // clips, row % clips
        source = (tokens, other_tokens)[role]
        hat, _ = norm_parts(source[clip, 0].astype(F32))
        low = (hat * (1.0 + mod[1, row : row + 1]) + mod[0, row : row + 1]).astype(BF16)
        normed[row * rows : (row + 1) * rows] = low
        normed_outs[row][...] = low
    for kind in range(3):
        pick = slice(kind * blocks, (kind + 1) * blocks)
        weight = jnp.concatenate([w[...] for w in weights[pick]], axis=1)
        bias = jnp.concatenate([b[...] for b in biases[pick]], axis=1).astype(F32)
        value = dot_nn(normed[...], weight) + bias
        for row in range(2 * clips):
            role, clip = row // clips, row % clips
            part = value[row * rows : (row + 1) * rows]
            if kind < 2:
                part = turn(part, cosines[row], sines[row], head, False)
            part = part.astype(BF16)
            if kind == 0:
                part = part * jnp.asarray(head**-0.5, BF16)
            for group in range(zs):
                held[clip, group ^ z, role, kind] = part[:, group * lanes : (group + 1) * lanes]
    for n, out in enumerate(outs):
        out[...] = held[n // zs, n % zs]


def qkv_call(meta, tokens, other_tokens, mod, tables, weight, bias, zs, head, aligned):
    clips, _, rows, width = tokens.shape
    lanes = width // (2 * zs)
    whole = lambda shape: pl.BlockSpec(shape, lambda t, m: (0,) * len(shape))
    blocks = width // (2 * LANES)
    message = (2, 3, rows, lanes)
    out_shape = [shaped(message, BF16)] * (zs * clips)
    out_shape += [shaped((rows, width), BF16)] * (2 * clips)
    return pl.pallas_call(
        functools.partial(qkv_kernel, zs, head),
        out_shape=out_shape,
        grid_spec=pltpu.PrefetchScalarGridSpec(
            num_scalar_prefetch=1,
            grid=(1,),
            in_specs=[whole(a.shape) for a in (tokens, other_tokens, mod, *tables)]
            + half_specs(width, width, 2 * zs, aligned)
            + half_specs(1, width, 2 * zs, aligned),
            out_specs=[whole(o.shape) for o in out_shape],
            scratch_shapes=[
                pltpu.VMEM((2 * clips * rows, width), BF16),
                pltpu.VMEM((clips, zs, *message), BF16),
            ],
        ),
        compiler_params=params(),
        cost_estimate=cost(
            6 * clips * rows * width * width, 3 * width * width + 32 * rows * width
        ),
        name="norm_qkv",
    )(meta, tokens, other_tokens, mod, *tables, *[weight] * (3 * blocks), *[bias] * (3 * blocks))


def attend_kernel(slots, head, clip, meta, *refs):
    zs = slots // 2
    parts, outs = refs[:zs], refs[zs:slots]
    exact, logs, held, scores, values, sems = refs[slots:]
    copies = [
        pltpu.make_async_copy(parts[k], held.at[pl.ds(2 * k, 2)], sems.at[k])
        for k in range(zs)
    ]
    for copy in copies:
        copy.start()
    for copy in copies:
        copy.wait()
    me, context = meta[0], meta[2 + clip]
    rows, width = held.shape[2], held.shape[3]
    pairs = width // head

    def prepare(frame, _):
        split = split_heads(held[frame ^ me, 2], pairs, head)
        ones = split_heads(jnp.ones((rows, width), BF16), pairs, head)
        for h in range(pairs):
            values[frame, h] = jnp.concatenate([split[h], ones[h]], axis=1)
        return 0

    lax.fori_loop(0, slots, prepare, 0)

    def attend(slot, count):
        queries = split_heads(held[slot, 0], pairs, head)
        total, tops = None, []
        for h in range(pairs):
            peak = None
            for frame in range(count):
                score = dot_nt(queries[h], held[frame ^ me, 1])
                scores[frame, h * rows : (h + 1) * rows] = score
                for at in range(0, rows, LANES):
                    piece = score[:, at : at + LANES]
                    peak = piece if peak is None else jnp.maximum(peak, piece)
            top = jnp.max(peak, axis=1, keepdims=True)
            tops.append(top)
            for frame in range(count):
                power = jnp.exp(scores[frame, h * rows : (h + 1) * rows] - top).astype(BF16)
                term = dot_nn(power, values[frame, h])
                total = term if total is None else total + term
        weight_sum = total[:, width:]
        result = total[:, :width] / weight_sum
        exact[slot] = result
        top = jnp.broadcast_to(tops[0], (rows, width))
        if pairs > 1:
            lane = lax.broadcasted_iota(jnp.int32, (rows, width), 1)
            for h in range(1, pairs):
                top = jnp.where(lane // head >= h, tops[h], top)
        turned = (top + jnp.log(weight_sum)).T
        logs[slot] = jnp.concatenate(
            [turned[h * head : h * head + 1] for h in range(pairs)], axis=1
        )

    def one_frame(frame, _):
        count = jnp.maximum(frame, context - 1) + 1
        for known in range(1, slots + 1):

            @pl.when(count == known)
            def _():
                attend(frame ^ me, known)

        return 0

    lax.fori_loop(0, slots, one_frame, 0)
    for slot in range(slots):
        outs[slot // 2][slot % 2] = exact[slot].astype(BF16)


def attend_call(meta, clip, parts, head):
    zs = len(parts)
    slots = 2 * zs
    rows, width = parts[0].shape[-2:]
    pairs = width // head
    work = slots * slots * rows * rows
    return pl.pallas_call(
        functools.partial(attend_kernel, slots, head, clip),
        out_shape=[shaped((2, rows, width), BF16)] * zs
        + [shaped((slots, rows, width), F32), shaped((slots, 1, pairs * rows), F32)],
        in_specs=[SMEM] + [ANY] * zs,
        out_specs=[VMEM] * (zs + 2),
        scratch_shapes=[
            pltpu.VMEM((slots, 3, rows, width), BF16),
            pltpu.VMEM((slots, pairs * rows, rows), F32),
            pltpu.VMEM((slots, pairs, rows, 2 * width), BF16),
            pltpu.SemaphoreType.DMA((zs,)),
        ],
        compiler_params=params(),
        cost_estimate=cost(work * 16 * width, slots * rows * width * 12, work * pairs),
        name="attend",
    )(meta, *parts)


def attend_grad_kernel(slots, head, clip, meta, *refs):
    zs = slots // 2
    parts, grads = refs[:zs], refs[zs:slots]
    exact, logs = refs[slots], refs[slots + 1]
    outs = refs[slots + 2 : slots + 2 + zs]
    held, grad, query_rows, grad_rows, delta, grad_q, grad_k, grad_v, sems, more = refs[
        slots + 2 + zs :
    ]
    copies = []
    for k in range(zs):
        pair = pl.ds(2 * k, 2)
        copies.append(pltpu.make_async_copy(parts[k], held.at[pair], sems.at[k]))
        copies.append(pltpu.make_async_copy(grads[k], grad.at[pair], more.at[k]))
    for copy in copies:
        copy.start()
    for copy in copies:
        copy.wait()
    me, context = meta[0], meta[2 + clip]
    rows, width = held.shape[2], held.shape[3]
    pairs = width // head

    def prepare(slot, _):
        query_rows[slot] = jnp.concatenate(split_heads(held[slot, 0], pairs, head), axis=0)
        grad_rows[slot] = jnp.concatenate(split_heads(grad[slot], pairs, head), axis=0)
        product = (grad[slot].astype(F32) * exact[slot]).T
        delta[slot] = jnp.concatenate(
            [
                jnp.sum(product[h * head : (h + 1) * head], axis=0, keepdims=True)
                for h in range(pairs)
            ],
            axis=1,
        )
        grad_q[slot] = jnp.zeros((rows, width), F32)
        return 0

    lax.fori_loop(0, slots, prepare, 0)

    def key_frame(frame, _):
        place = frame ^ me
        keys, values = held[place, 1], held[place, 2]
        head_keys = split_heads(keys, pairs, head)
        grad_k[...] = jnp.zeros_like(grad_k)
        grad_v[...] = jnp.zeros_like(grad_v)

        def query_frames(first, count):
            add_k = add_v = None
            for n in range(count):
                slot = (first + n) ^ me
                score = dot_nt(keys, query_rows[slot])
                grad_weight = dot_nt(values, grad_rows[slot])
                weight = jnp.exp(score - logs[slot])
                grad_score = (weight * (grad_weight - delta[slot])).astype(BF16)
                term_v = dot_nn(weight.astype(BF16), grad_rows[slot])
                term_k = dot_nn(grad_score, query_rows[slot])
                add_v = term_v if add_v is None else add_v + term_v
                add_k = term_k if add_k is None else add_k + term_k
                total = grad_q[slot]
                for h in range(pairs):
                    total = total + dot_tn(grad_score[:, h * rows : (h + 1) * rows], head_keys[h])
                grad_q[slot] = total
            grad_v[...] += add_v
            grad_k[...] += add_k

        first = jnp.where(frame < context, 0, frame)
        for size in GROUPS:
            if size > slots:
                continue
            count = (slots - first) // size

            def group_step(n, _, first=first, size=size):
                query_frames(first + n * size, size)
                return 0

            lax.fori_loop(0, count, group_step, 0)
            first = first + count * size
        held[place, 1] = grad_k[...].astype(BF16)
        held[place, 2] = grad_v[...].astype(BF16)
        return 0

    lax.fori_loop(0, slots, key_frame, 0)
    for slot in range(slots):
        out, role = outs[slot // 2], slot % 2
        out[role, 0] = (grad_q[slot] * head**-0.5).astype(BF16)
        out[role, 1] = held[slot, 1]
        out[role, 2] = held[slot, 2]


def attend_grad_call(meta, clip, parts, grads, exact, logs, head):
    zs = len(parts)
    slots = 2 * zs
    rows, width = parts[0].shape[-2:]
    pairs = width // head
    work = slots * slots * rows * rows
    return pl.pallas_call(
        functools.partial(attend_grad_kernel, slots, head, clip),
        out_shape=[shaped((2, 3, rows, width), BF16)] * zs,
        in_specs=[SMEM] + [ANY] * slots + [VMEM, VMEM],
        out_specs=[VMEM] * zs,
        scratch_shapes=[
            pltpu.VMEM((slots, 3, rows, width), BF16),
            pltpu.VMEM((slots, rows, width), BF16),
            pltpu.VMEM((slots, pairs * rows, width), BF16),
            pltpu.VMEM((slots, pairs * rows, width), BF16),
            pltpu.VMEM((slots, 1, pairs * rows), F32),
            pltpu.VMEM((slots, rows, width), F32),
            pltpu.VMEM((rows, width), F32),
            pltpu.VMEM((rows, width), F32),
            pltpu.SemaphoreType.DMA((zs,)),
            pltpu.SemaphoreType.DMA((zs,)),
        ],
        compiler_params=params(),
        cost_estimate=cost(work * 4 * width, slots * rows * width * 2, work * pairs / 10),
        name="attend_grad",
    )(meta, *parts, *grads, exact, logs)


def mixed_places(width, hidden):
    ends = [0]
    for columns in (width // 2, hidden // 2, width, hidden):
        ends.append(ends[-1] + columns)
    return ends


def forward_back_kernel(slots, clip, meta, tokens, cotangent, mod, proj_b, up_b, down_b, *refs):
    zs = slots // 2
    width, hidden_width = tokens.shape[-1], refs[zs + 2].shape[1]
    at_act, at_gtwo, at_hid = mixed_places(width, hidden_width)[1:4]
    parts, swapped, (proj_hbm, up_hbm, down_hbm) = refs[:zs], refs[zs], refs[zs + 1 : zs + 4]
    (
        layer_out, grad_middle_out, row_grads, up_bgrad,
        att_own, att_far, gone_low, n2_own, act_own, mixed,
        held, far, n2_other, gtwo_low, proj, up, down, slope, active, hid, sems,
    ) = refs[zs + 4 :]
    blocks = up.shape[1] // FF_BLOCK
    fetches = [pltpu.make_async_copy(proj_hbm, proj, sems.at[4])]
    for source, target, columns in ((up_hbm, up, True), (down_hbm, down, False)):
        for block in range(blocks):
            at = pl.ds(block * FF_BLOCK, FF_BLOCK)
            at = (slice(None), at) if columns else (at, slice(None))
            fetches.append(
                pltpu.make_async_copy(source.at[at], target.at[at], sems.at[4 + len(fetches)])
            )
    for fetch in fetches[:IN_FLIGHT]:
        fetch.start()

    def fetched(number):
        fetches[number].wait()
        if number + IN_FLIGHT < len(fetches):
            fetches[number + IN_FLIGHT].start()

    me = meta[0]
    parity = me % 2
    rows = tokens.shape[-2]
    lanes = width // slots
    gate_one, shift_two, scale_two, gate_two = (mod[k, clip : clip + 1] for k in range(4))
    for k in range(zs):
        held[(2 * k) ^ me] = parts[k][0]
        held[(2 * k + 1) ^ me] = swapped[k]
        far[k ^ (me // 2)] = parts[k][1]
    attended = jnp.concatenate([held[k] for k in range(slots)], axis=1)
    att_own[...] = jnp.concatenate([held[2 * k + parity] for k in range(zs)], axis=1)
    att_far[...] = jnp.concatenate([far[k] for k in range(zs)], axis=1)
    fetched(0)
    branch_one = dot_nn(attended, proj[...]) + proj_b[...].astype(F32)
    middle = tokens[...].reshape(rows, width).astype(F32) + gate_one * branch_one
    hat_two, inverse_two = norm_parts(middle)
    low_two = (hat_two * (1.0 + scale_two) + shift_two).astype(BF16)
    for block in range(slots):
        store_by_parity(
            n2_own, n2_other, slice(block // 2 * lanes, (block // 2 + 1) * lanes), parity, block,
            low_two[:, block * lanes : (block + 1) * lanes],
        )
    n2_copy = pltpu.make_async_copy(n2_other, mixed.at[:, pl.ds(0, width // 2)], sems.at[2])
    n2_copy.start()
    chunk = hidden_width // slots
    for block in range(blocks):
        at = slice(block * FF_BLOCK, (block + 1) * FF_BLOCK)
        fetched(1 + block)
        hidden = dot_nn(low_two, up[:, at]) + up_b[:, at].astype(F32)
        square = hidden * hidden
        bent = jnp.tanh(GELU_A * (hidden + GELU_B * square * hidden))
        half = 0.5 * (1.0 + bent)
        low = (hidden * half).astype(BF16)
        slope[:, at] = half + (0.5 * GELU_A) * hidden * (1.0 - bent * bent) * (
            1.0 + (3.0 * GELU_B) * square
        )
        active[:, at] = low
        for index in range(block * FF_BLOCK // chunk, (block + 1) * FF_BLOCK // chunk):
            piece = active.at[:, pl.ds(index * chunk, chunk)]
            place = pl.ds(index // 2 * chunk, chunk)

            @pl.when(parity == index % 2)
            def _():
                pltpu.make_async_copy(piece, act_own.at[:, place], sems.at[0]).start()

            @pl.when(parity != index % 2)
            def _():
                pltpu.make_async_copy(
                    piece, mixed.at[:, pl.ds(at_act + index // 2 * chunk, chunk)], sems.at[0]
                ).start()

    branch_two = down_b[...].astype(F32)
    for block in range(blocks):
        at = slice(block * FF_BLOCK, (block + 1) * FF_BLOCK)
        fetched(1 + blocks + block)
        branch_two = branch_two + dot_nn(active[:, at], down[at, :])
    layer_out[...] = (middle + gate_two * branch_two).astype(BF16)
    grad_out = cotangent[...].reshape(rows, width).astype(F32)
    low_grad_two = (grad_out * gate_two).astype(BF16)
    gtwo_low[...] = low_grad_two
    gtwo_copy = pltpu.make_async_copy(gtwo_low, mixed.at[:, pl.ds(at_gtwo, width)], sems.at[3])
    gtwo_copy.start()
    row_grads[3:4] = jnp.sum(grad_out * branch_two, axis=0, keepdims=True)
    row_grads[4:5] = jnp.sum(low_grad_two.astype(F32), axis=0, keepdims=True)
    grad_normed = None
    for block in range(blocks):
        at = slice(block * FF_BLOCK, (block + 1) * FF_BLOCK)
        low = (dot_nt(low_grad_two, down[at, :]) * slope[:, at]).astype(BF16)
        hid[:, at] = low
        pltpu.make_async_copy(
            hid.at[:, at], mixed.at[:, pl.ds(at_hid + block * FF_BLOCK, FF_BLOCK)], sems.at[1]
        ).start()
        up_bgrad[:, at] = jnp.sum(low.astype(F32), axis=0, keepdims=True)
        term = dot_nt(low, up[:, at])
        grad_normed = term if grad_normed is None else grad_normed + term
    grad_middle, grad_shift, grad_scale = norm_pull(grad_normed, hat_two, inverse_two, scale_two)
    grad_middle = grad_middle + grad_out
    grad_middle_out[...] = grad_middle
    low_grad_one = (grad_middle * gate_one).astype(BF16)
    gone_low[...] = low_grad_one
    row_grads[0:1] = jnp.sum(grad_middle * branch_one, axis=0, keepdims=True)
    row_grads[1:2] = grad_shift
    row_grads[2:3] = grad_scale
    row_grads[5:6] = jnp.sum(low_grad_one.astype(F32), axis=0, keepdims=True)
    row_grads[6:8] = jnp.zeros((2, width), F32)
    n2_copy.wait()
    gtwo_copy.wait()
    pltpu.make_async_copy(active, active, sems.at[0]).wait()
    pltpu.make_async_copy(hid, hid, sems.at[1]).wait()


def forward_back_call(
    meta, clip, tokens, cotangent, mod, proj_b, up_b, down_b, parts, swapped, proj, up, down
):
    zs = len(parts)
    slots = 2 * zs
    rows, width = tokens.shape[-2:]
    lanes = width // slots
    hidden = up.shape[1]
    half, half_hidden = width // 2, hidden // 2
    out_shape = [
        shaped((rows, width), BF16),
        shaped((rows, width), F32),
        shaped((8, width), F32),
        shaped((1, hidden), F32),
        shaped((rows, half), BF16),
        shaped((rows, half), BF16),
        shaped((rows, width), BF16),
        shaped((rows, half), BF16),
        shaped((rows, half_hidden), BF16),
        shaped((rows, mixed_places(width, hidden)[4]), BF16),
    ]
    full = lambda shape: pl.BlockSpec(shape, lambda t: (0,) * len(shape))
    pick = pl.BlockSpec((1, 1, rows, width), lambda t: (clip, 0, 0, 0))
    return pl.pallas_call(
        functools.partial(forward_back_kernel, slots, clip),
        grid=(1,),
        out_shape=out_shape,
        in_specs=[SMEM, pick, pick]
        + [full(a.shape) for a in (mod, proj_b, up_b, down_b, *parts, swapped)]
        + [ANY] * 3,
        out_specs=[ANY if k in (8, 9) else full(o.shape) for k, o in enumerate(out_shape)],
        scratch_shapes=[
            pltpu.VMEM((slots, rows, lanes), BF16),
            pltpu.VMEM((zs, rows, lanes), BF16),
            pltpu.VMEM((rows, half), BF16),
            pltpu.VMEM((rows, width), BF16),
            pltpu.VMEM(proj.shape, BF16),
            pltpu.VMEM(up.shape, BF16),
            pltpu.VMEM(down.shape, BF16),
            pltpu.VMEM((rows, hidden), F32),
            pltpu.VMEM((rows, hidden), BF16),
            pltpu.VMEM((rows, hidden), BF16),
            pltpu.SemaphoreType.DMA((5 + 2 * hidden // FF_BLOCK,)),
        ],
        compiler_params=params(),
        cost_estimate=cost(
            4 * rows * width * (width + 2 * hidden),
            4 * width * (width + 2 * hidden),
            rows * hidden,
        ),
        name="feed_forward",
    )(meta, tokens, cotangent, mod, proj_b, up_b, down_b, *parts, swapped, proj, up, down)


def proj_back_kernel(meta, near, far, proj, *outs):
    me = meta[0]
    rows, lanes = near.shape[0], outs[0].shape[2]
    groups = [pl.multiple_of((me ^ (2 * k)) * lanes, lanes) for k in range(len(outs))]
    weight = jnp.concatenate([proj[pl.ds(group, lanes), :] for group in groups], axis=0)
    both = jnp.concatenate([near[...], far[...]], axis=0)
    value = dot_nt(both, weight).astype(BF16)
    for k, out in enumerate(outs):
        for role in range(2):
            out[role] = value[role * rows : (role + 1) * rows, k * lanes : (k + 1) * lanes]


def proj_back_call(meta, near, far, proj, zs):
    rows, width = near.shape
    lanes = width // (2 * zs)
    return pl.pallas_call(
        proj_back_kernel,
        out_shape=[shaped((2, rows, lanes), BF16)] * zs,
        in_specs=[SMEM, VMEM, VMEM, VMEM],
        out_specs=[VMEM] * zs,
        compiler_params=params(),
        cost_estimate=cost(2 * rows * width * width, 2 * width * width + 6 * rows * width),
        name="proj_back",
    )(meta, near, far, proj)


def qkv_grad_kernel(zs, head, clip, meta, *refs):
    tables, refs = refs[:4], refs[4:]
    blocks = refs[zs].shape[0] // (2 * LANES)
    parts, weights = refs[:zs], refs[zs : zs + 3 * blocks]
    near_out, far_out, near_sum, far_sum, bias_out, held = refs[zs + 3 * blocks :]
    rows, width = near_sum.shape
    clips = tables[0].shape[0] // 2
    z = meta[0] // 2
    cosines = [turn_table(tables[0], tables[2], role * clips + clip, head) for role in range(2)]
    sines = [turn_table(tables[1], tables[3], role * clips + clip, head) for role in range(2)]
    for k in range(zs):
        held[k ^ z] = parts[k][...]
    totals = [None, None]
    bias_out[...] = jnp.zeros_like(bias_out)
    half = width // 2
    for kind in range(3):
        weight = jnp.concatenate([w[...] for w in weights[kind * blocks : (kind + 1) * blocks]], axis=1)
        sums = None
        for role, out in enumerate((near_out, far_out)):
            low = jnp.concatenate([held[k, role, kind] for k in range(zs)], axis=1)
            if kind < 2:
                low = turn(low.astype(F32), cosines[role], sines[role], head, True).astype(BF16)
            out[:, kind * half : (kind + 1) * half] = low
            column = jnp.sum(low.astype(F32), axis=0, keepdims=True)
            sums = column if sums is None else sums + column
            term = dot_nt(low, weight)
            totals[role] = term if totals[role] is None else totals[role] + term
        bias_out[kind : kind + 1] = sums
    near_sum[...] = totals[0]
    far_sum[...] = totals[1]


def qkv_grad_call(meta, clip, tables, parts, weight, head, aligned):
    zs = len(parts)
    rows, lanes = parts[0].shape[-2:]
    width = 2 * zs * lanes
    blocks = width // (2 * LANES)
    whole = lambda shape: pl.BlockSpec(shape, lambda t, m: (0,) * len(shape))
    out_shape = [
        shaped((rows, 3 * width // 2), BF16),
        shaped((rows, 3 * width // 2), BF16),
        shaped((rows, width), F32),
        shaped((rows, width), F32),
        shaped((8, width // 2), F32),
    ]
    return pl.pallas_call(
        functools.partial(qkv_grad_kernel, zs, head, clip),
        out_shape=out_shape,
        grid_spec=pltpu.PrefetchScalarGridSpec(
            num_scalar_prefetch=1,
            grid=(1,),
            in_specs=[whole(a.shape) for a in (*tables, *parts)]
            + half_specs(width, width, 2 * zs, aligned),
            out_specs=[whole(o.shape) for o in out_shape],
            scratch_shapes=[pltpu.VMEM((zs, 2, 3, rows, lanes), BF16)],
        ),
        compiler_params=params(),
        cost_estimate=cost(0.6 * rows * width * width, width * width),
        name="qkv_grad",
    )(meta, *tables, *parts, *[weight] * (3 * blocks))


def norm_grad_kernel(tokens, mod, *refs):
    clips = tokens.shape[0]
    nears, fars, middles = refs[:clips], refs[clips : 2 * clips], refs[2 * clips : 3 * clips]
    tokens_grad, row_grads = refs[3 * clips :]
    for c in range(clips):
        hat, inverse = norm_parts(tokens[c, 0].astype(F32))
        grad, shift, scale = norm_pull(
            nears[c][...] + fars[c][...], hat, inverse, mod[1, c : c + 1]
        )
        tokens_grad[c, 0] = grad + middles[c][...]
        row_grads[c, 0:1] = shift
        row_grads[c, 1:2] = scale
        row_grads[c, 2:8] = jnp.zeros((6, tokens.shape[-1]), F32)


def norm_grad_call(tokens, mod, nears, fars, middles):
    clips, _, rows, width = tokens.shape
    return pl.pallas_call(
        norm_grad_kernel,
        out_shape=[shaped(tokens.shape, F32), shaped((clips, 8, width), F32)],
        in_specs=[VMEM] * (2 + 3 * clips),
        out_specs=[VMEM, VMEM],
        compiler_params=params(),
        cost_estimate=cost(clips * rows * width * 3, clips * rows * width * 2),
        name="norm_grad",
    )(tokens, mod, *nears, *fars, *middles)


def weight_grad_kernel(jobs, clip_size, zs, split, meta, *refs):
    arrays_n = sum(2 * job[0] for job in jobs)
    outs_n = 4 if split else 1
    arrays, outs = refs[:arrays_n], refs[arrays_n : arrays_n + outs_n]
    held, out_sems, in_sems = refs[arrays_n + outs_n : arrays_n + outs_n + 3]
    scratch = refs[arrays_n + outs_n + 3 :]
    _, _, _, height, cols = held.shape
    tile = zs * height
    z = meta[0] // 2
    clip = meta[1] if split else 0

    def send_out(slot, tiles, repeat, first, tall):
        for e in range(clip_size):
            for half, first_bit in enumerate((1, clip_size // 2) if split else (0,)):
                keep, send = (outs[2 * half], outs[2 * half + 1]) if split else (outs[0], None)
                rest = [k for k in range(clip_size) if not k & first_bit]
                if e & first_bit:
                    out, place = send, rest.index(e ^ first_bit)
                else:
                    out, place = keep, rest.index(e)
                span = zs // 2 if split else zs
                low, high = half * span, (half + 1) * span
                if not tall:
                    pltpu.make_async_copy(
                        held.at[slot, e, pl.ds(low, span)],
                        out.at[place, :, pl.ds(first, height)],
                        out_sems.at[slot],
                    ).start()
                    continue
                for block in range(zs):
                    row = repeat * zs + block
                    k = row // tiles
                    if low <= k < high:
                        pltpu.make_async_copy(
                            held.at[slot, e, block],
                            out.at[place, k - low, pl.ds(first + row % tiles * height, height)],
                            out_sems.at[slot],
                        ).start()

    copies = []
    at = 0
    for job, (count, _, _, _, _, places) in enumerate(jobs):
        left, right = scratch[2 * job : 2 * job + 2]
        depth = left.shape[0] // count
        for n in range(2 * count):
            target = left if n < count else right
            source = arrays[at + n]
            if source.shape[1] != target.shape[1]:
                source = source.at[:, pl.ds(places[n], target.shape[1])]
            copies.append(
                pltpu.make_async_copy(
                    source,
                    target.at[pl.ds(n % count * depth, depth)],
                    in_sems.at[at + n],
                )
            )
        at += 2 * count
    ends = [0]
    for job in jobs:
        ends.append(ends[-1] + 2 * job[0])
    for copy in copies[: ends[min(JOBS_AHEAD, len(jobs))]]:
        copy.start()

    at = number = 0
    for job, (count, lane_parts, tall, tiles, first, _) in enumerate(jobs):
        left, right = scratch[2 * job : 2 * job + 2]
        block = left.shape[1] // zs
        for n in range(2 * count):
            copies[at + n].wait()
        at += 2 * count
        if job + JOBS_AHEAD < len(jobs):
            for copy in copies[ends[job + JOBS_AHEAD] : ends[job + JOBS_AHEAD + 1]]:
                copy.start()
        wide = right.shape[1] // (tiles * lane_parts if not tall else 1)
        part = wide // clip_size
        for repeat in range(tiles):
            slot = number % 2
            if number >= 2:
                pltpu.make_async_copy(held.at[slot], held.at[slot], out_sems.at[slot]).wait()
            for lane_part in range(lane_parts):
                if tall:
                    per = zs // tiles
                    rows = [
                        left[:, pl.ds(pl.multiple_of(((repeat * per + n) ^ z) * block, block), block)]
                        for n in range(per)
                    ]
                    rows = rows[0] if per == 1 else jnp.concatenate(rows, axis=1)
                    value = dot_tn(rows, right[...]).astype(BF16)
                else:
                    group = repeat + lane_part
                    value = dot_tn(
                        left[...], right[:, group * wide : (group + 1) * wide]
                    ).astype(BF16)
                for p in range(clip_size):
                    lanes = slice(lane_part * part, (lane_part + 1) * part)
                    piece = value[:, p * part : (p + 1) * part]
                    for k in range(zs):
                        source = piece[k * height : (k + 1) * height]
                        held[slot, p ^ clip, k if tall else k ^ z, :, lanes] = source
            send_out(slot, tiles, repeat, first if tall else first + repeat * height, tall)
            number += 1
    for slot in range(min(number, 2)):
        pltpu.make_async_copy(held.at[slot], held.at[slot], out_sems.at[slot]).wait()


def weight_grad_call(meta, products, clip_size, zs, split, name):
    jobs, arrays, scratch = [], [], []
    first = flops = 0
    tile = min(p[0][0][2] for p in products)
    height = tile // zs
    piece = None
    for lefts, rights, lane_parts, tall in products:
        depth, total = rights[0][0].shape[0], rights[0][2]
        rows = lefts[0][2]
        if tall:
            tiles, piece = rows // tile, total // clip_size
        elif lane_parts > 1:
            tiles, piece = 1, total // clip_size
        else:
            tiles, piece = total // (2 * tile), 2 * tile // clip_size
        count = len(lefts)
        places = tuple(a[1] for a in lefts + rights)
        jobs.append((count, lane_parts, tall, tiles, first, places))
        first += height * tiles
        arrays += [a[0] for a in lefts + rights]
        flops += 2 * count * depth * rows * total
        scratch += [
            pltpu.VMEM((count * depth, rows), BF16),
            pltpu.VMEM((count * depth, total), BF16),
        ]
    if split:
        outs = [shaped((clip_size // 2, zs // 2, first, piece), BF16)] * 4
    else:
        outs = [shaped((clip_size, zs, first, piece), BF16)]
    return pl.pallas_call(
        functools.partial(weight_grad_kernel, tuple(jobs), clip_size, zs, split),
        out_shape=outs,
        in_specs=[SMEM] + [ANY] * len(arrays),
        out_specs=[ANY] * len(outs),
        scratch_shapes=[
            pltpu.VMEM((2, clip_size, zs, height, piece), BF16),
            pltpu.SemaphoreType.DMA((2,)),
            pltpu.SemaphoreType.DMA((len(arrays),)),
        ]
        + scratch,
        compiler_params=params(),
        cost_estimate=cost(flops, flops / 512),
        name=name,
    )(meta, *arrays)


def place_kernel(jobs, pieces, meta, *refs):
    parts, outs = refs[:pieces], refs[pieces:]
    clip = meta[1]
    cols = parts[0].shape[1]
    for e in range(pieces):
        first = 0
        for out, (height, repeats, tall) in zip(outs, jobs):
            for repeat in range(repeats):
                base = 0 if tall else repeat * cols * pieces
                target = pl.ds(pl.multiple_of(base + (clip ^ e) * cols, cols), cols)
                value = parts[e][first : first + height].astype(F32)
                if tall:
                    out[repeat * height : (repeat + 1) * height, target] = value
                else:
                    out[:, target] = value
                first += height


def place_call(meta, parts, jobs, outs):
    return pl.pallas_call(
        functools.partial(place_kernel, jobs, len(parts)),
        out_shape=outs,
        in_specs=[SMEM] + [VMEM] * len(parts),
        out_specs=[VMEM] * len(outs),
        compiler_params=params(),
        cost_estimate=cost(0, sum(o.size * 4 for o in outs)),
        name="place_grads",
    )(meta, *parts)


def place_qkv_kernel(meta, *refs):
    parts, out = refs[:-1], refs[-1]
    parity, clip = meta[0] % 2, meta[1]
    thirds = out.shape[1] // 3
    for e, part in enumerate(parts):
        for role in range(2):
            block = 2 * (clip ^ e) + (parity ^ role)
            for kind in range(3):
                at = pl.ds(pl.multiple_of(kind * thirds + block * LANES, LANES), LANES)
                out[:, at] = part[role, :, kind * LANES : (kind + 1) * LANES].astype(F32)


def place_qkv_call(meta, parts, out):
    return pl.pallas_call(
        place_qkv_kernel,
        out_shape=out,
        in_specs=[SMEM] + [VMEM] * len(parts),
        out_specs=VMEM,
        compiler_params=params(),
        cost_estimate=cost(0, out.size * 6),
        name="place_qkv_grad",
    )(meta, *parts)


def exchange(array, axis, size, distance):
    return lax.ppermute(array, axis, [(k, k ^ distance) for k in range(size)])


def after(value, *others):
    return lax.optimization_barrier((value, *others))


def spread(slots_out, seq_size):
    return [slots_out[0]] + [
        exchange(slots_out[k], "seq", seq_size, 2 * k) for k in range(1, seq_size // 2)
    ]


def add_low(left, right):
    return (left.astype(F32) + right.astype(F32)).astype(BF16)


def step_out(pairs, bits, size):
    return [exchange(send, "clip", size, bit) for (_, send), bit in zip(pairs, bits)]


def step_in(pairs, arrived):
    left = []
    for (keep, _), new in zip(pairs, arrived):
        half = keep.shape[0] // 2
        if half:
            left.append((add_low(keep[:half], new[:half]), add_low(keep[half:], new[half:])))
        else:
            left.append((add_low(keep[0], new[0]), None))
    return left


def clip_orders(clip_size):
    down = [1 << k for k in reversed(range(clip_size.bit_length() - 1))]
    return [1] + down[:-1], down


def z_out(blocks, seq_size):
    return exchange(jnp.stack(blocks[1::2]), "seq", seq_size, seq_size // len(blocks))


def z_in(blocks, arrived):
    return [add_low(keep, new) for keep, new in zip(blocks[0::2], arrived)]


def sum_z(blocks, seq_size):
    while len(blocks) > 1:
        blocks = z_in(blocks, z_out(blocks, seq_size))
    return blocks[0]


def gather_pieces(piece, clip_size):
    return [piece] + [exchange(piece, "clip", clip_size, d) for d in range(1, clip_size)]


def double(array, axis, size):
    bit = 1
    while bit < size:
        array = jnp.concatenate([array, exchange(array, axis, size, bit)])
        bit *= 2
    return array


def silu_act(values_in):
    return values_in * jax.nn.sigmoid(values_in)


def rotary_tables(stamps, patch_count, head):
    lane = jnp.arange(LANES, dtype=jnp.int32)
    quarter = head // 4
    freqs = 10000.0 ** (-(lane % quarter).astype(F32) / quarter)
    sign = jnp.where(lane % head < head // 2, -1.0, 1.0).astype(F32)
    tables = []
    for places in (stamps, jnp.arange(patch_count, dtype=jnp.int32)):
        angles = places.astype(F32)[:, None] * freqs[None, :]
        tables += [jnp.cos(angles), jnp.sin(angles) * sign[None, :]]
    return tables


def on_device(
    tokens,
    cotangent,
    context_count,
    noise_level,
    frame_time,
    level_table,
    mod_weight,
    mod_bias,
    qkv_weight,
    qkv_bias,
    proj_weight,
    proj_bias,
    up_weight,
    up_bias,
    down_weight,
    down_bias,
):
    seq_size, clip_size = lax.axis_size("seq"), lax.axis_size("clip")
    me, mine = lax.axis_index("seq"), lax.axis_index("clip")
    clips, _, rows, width = tokens.shape
    head = width // HEADS
    hidden = up_weight.shape[1]
    zs = seq_size // 2
    me = me.astype(jnp.int32)
    mine = mine.astype(jnp.int32)
    parity = me % 2
    aligned = (width // seq_size) % LANES == 0
    stamps = jnp.stack([noise_level[:, 0], frame_time[:, 0]])
    other_stamps = exchange(stamps, "seq", seq_size, 1)
    other_tokens = exchange(tokens, "seq", seq_size, 1)
    meta = jnp.concatenate([jnp.stack([me, mine]), context_count])
    levels = jnp.concatenate(
        [
            jnp.where(me < context_count, 0, stamps[0]),
            jnp.where((me ^ 1) < context_count, 0, other_stamps[0]),
        ]
    )
    levels_used = levels[:clips]
    mod_bias_row = mod_bias[None]
    mod_one, condition = modulation_call(levels, level_table, mod_weight, mod_bias_row, 0, 2)
    condition = condition[:clips]
    tables = rotary_tables(jnp.concatenate([stamps[1], other_stamps[1]]), rows, head)
    qkv_bias_row = qkv_bias[None]
    if aligned:
        weight_half, bias_half = qkv_weight, qkv_bias_row
    else:
        weight_half = half_columns(qkv_weight, seq_size, parity)
        bias_half = half_columns(qkv_bias_row, seq_size, parity)

    swap = lambda array: exchange(array, "seq", seq_size, 1)
    full = lambda array: (array, 0, array.shape[1])
    at_n2, at_act, at_gtwo, at_hid, _ = mixed_places(width, hidden)
    out = qkv_call(
        meta, tokens, other_tokens, mod_one, tables, weight_half, bias_half, zs, head, aligned
    )
    normed = out[zs * clips :]
    parts = [spread(out[:zs], seq_size)]
    mod_two, _ = modulation_call(
        levels[:clips], level_table, mod_weight, mod_bias_row, 2, 4
    )
    proj_row, up_row, down_row = proj_bias[None], up_bias[None], down_bias[None]
    parts[0], mod_two, proj_row, up_row, down_row = after(
        parts[0], mod_two, proj_row, up_row, down_row
    )
    exact, logs, attended, crossed = [], [], [], []
    for c in range(clips):
        sends = out[(c + 1) * zs : (c + 2) * zs] if c < clips - 1 else None
        if c < clips - 1:
            parts.append(spread(sends, seq_size))
        done = attend_call(meta, c, parts[c], head)
        exact.append(done[zs])
        logs.append(done[zs + 1])
        sends = done[:zs]
        if c < clips - 1:
            sends, parts[c + 1] = after(sends, parts[c + 1])
        if c:
            sends, attended[-1] = after(sends, attended[-1])
            crossed.append(swap(jnp.stack([a[1] for a in attended[-1]])))
        attended.append(spread(sends, seq_size))
    layer, middles, row_grads, up_bgrads, saved, mixed, far_ones, grads = ([] for _ in range(8))
    for c in range(clips):
        if c:
            meta, grads[-1][0] = after(meta, grads[-1][0])
        out = forward_back_call(
            meta, c, tokens, cotangent, mod_two, proj_row, up_row, down_row, attended[c],
            crossed[c], proj_weight, up_weight, down_weight,
        )
        layer.append(out[0])
        middles.append(out[1])
        row_grads.append(out[2])
        up_bgrads.append(out[3])
        gone, mine_mixed = out[6], out[9]
        if c < clips - 1:
            gone, mine_mixed, attended[c + 1] = after(gone, mine_mixed, attended[c + 1])
            crossed.append(swap(jnp.stack([a[1] for a in attended[c + 1]])))
        if c:
            gone, mine_mixed, grads[-1], mixed[-1] = after(gone, mine_mixed, grads[-1], mixed[-1])
        far_ones.append(swap(gone))
        if c < clips - 1:
            far_ones[-1], crossed[-1] = after(far_ones[-1], crossed[-1])
        saved.append((out[4], out[5], gone, out[7], out[8]))
        if c == clips - 1:
            far_ones[-1], mine_mixed = after(far_ones[-1], mine_mixed)
        back = list(proj_back_call(meta, gone, far_ones[c], proj_weight, zs))
        if c < clips - 1:
            back[0], mine_mixed = after(back[0], mine_mixed)
        mixed.append([mine_mixed, swap(mine_mixed)])
        grads.append(spread(back, seq_size))
    row = width // seq_size
    orders = clip_orders(clip_size)
    steps = len(orders[0])
    products = [([], [], 1, False), ([], [], 1, True), ([], [], 1, False)]
    for c in range(clips):
        att_own, att_far, gone, n2_own, act_own = saved[c]
        own, far = mixed[c]
        products[0][0].extend([full(att_own), full(att_far)])
        products[0][1].extend([full(gone), full(far_ones[c])])
        products[1][0].extend([full(act_own), (far, at_act, hidden // 2)])
        products[1][1].extend([(own, at_gtwo, width), (far, at_gtwo, width)])
        products[2][0].extend([full(n2_own), (far, at_n2, width // 2)])
        products[2][1].extend([(own, at_hid, hidden), (far, at_hid, hidden)])
    meta, grads[-1][0] = after(meta, grads[-1][0])
    (shares,) = weight_grad_call(meta, products, clip_size, zs, False, "weight_grads")
    meta, shares = after(meta, shares)
    summed = lax.psum_scatter(
        shares.reshape(-1, shares.shape[-1]), "clip", scatter_dimension=0, tiled=True
    ).reshape(shares.shape[1:])
    returned = []
    for c in range(clips):
        if c:
            meta, returned[-1][0] = after(meta, returned[-1][0])
        out = attend_grad_call(meta, c, parts[c], grads[c], exact[c], logs[c], head)
        if c < clips - 1:
            out, grads[c + 1] = after(out, grads[c + 1])
        else:
            out, returned[-1] = after(out, returned[-1])
        returned.append(spread(out, seq_size))
    turns = list(zip(*orders))
    grad_rights, nears, fars, qkv_bgrads = [], [], [], []
    for c in range(clips):
        if c == 0:
            meta, returned[-1][0] = after(meta, returned[-1][0])
        out = qkv_grad_call(meta, c, tables, returned[c], weight_half, head, aligned)
        grad_rights.extend(out[:2])
        nears.append(out[2])
        fars.append(swap(out[3]))
        qkv_bgrads.append(out[4][:3])
    tokens_grad, late_rows = norm_grad_call(tokens, mod_one, nears, fars, middles)
    blocks = list(summed)
    if len(blocks) > 1:
        landed = z_out(blocks, seq_size)
        late_rows, landed = after(late_rows, landed)
        blocks = z_in(blocks, landed)
    level_rows = jnp.stack([levels_used // 32, levels_used % 32]).astype(F32)
    level_rows = jnp.concatenate([level_rows, jnp.zeros((2, width - clips), F32)], axis=1)
    mod_rows = []
    for c in range(clips):
        mod_rows += [late_rows[c, 0:2], row_grads[c][0:4]]
    bias_rows = [
        sum(qkv_bgrads).reshape(3 * width // 2),
        jnp.zeros((width // 2,), F32),
        sum(up_bgrads).reshape(hidden),
        sum(r[4] for r in row_grads),
        sum(r[5] for r in row_grads),
    ]
    bias_rows = jnp.concatenate(bias_rows).reshape(-1, width)
    late = jnp.concatenate([condition, level_rows] + mod_rows + [bias_rows], axis=0)
    start, stop = clips + 2, clips + 2 + 6 * clips
    late = double(late.astype(BF16)[None], "seq", seq_size)
    blocks = list(summed)
    lefts = [normed[role * clips + c] for c in range(clips) for role in range(2)]
    if aligned:
        shares = weight_grad_call(
            meta,
            [([full(a) for a in lefts], [full(a) for a in grad_rights], 3, False)],
            clip_size,
            zs,
            True,
            "qkv_weight_grad",
        )
        pairs_qkv = [shares[:2], shares[2:]]
        arrived = step_out(pairs_qkv, turns[0], clip_size)
        if len(blocks) > 1:
            landed = z_out(blocks, seq_size)
            arrived, landed = after(arrived, landed)
            blocks = z_in(blocks, landed)
        pairs_qkv = step_in(pairs_qkv, arrived)
        for bits in turns[1:]:
            pairs_qkv = step_in(pairs_qkv, step_out(pairs_qkv, bits, clip_size))
    own_sums = jnp.sum(
        late[:, stop:].astype(F32).reshape(zs, 2, late.shape[1] - stop, width), axis=0
    ).astype(BF16)
    sums_rows = 2 * own_sums.shape[1]
    message = jnp.concatenate(
        [late[:, :stop].reshape(seq_size * stop, width), own_sums.reshape(sums_rows, width)]
    )
    late = double(message[None], "clip", clip_size)
    piece = sum_z(blocks, seq_size)
    if aligned:
        pairs_qkv, late = after(pairs_qkv, late)
        blocks = [*pairs_qkv[0][0], *pairs_qkv[1][0]]
        if len(blocks) > 1:
            landed = z_out(blocks, seq_size)
            landed, late = after(landed, late)
            blocks = z_in(blocks, landed)
    own_sums = jnp.sum(late[:, seq_size * stop :].astype(F32), axis=0).reshape(2, -1)
    late = late[:, : seq_size * stop].reshape(clip_size * seq_size, stop, width)
    devices = clip_size * seq_size
    grad_modulation = late[:, start:].reshape(devices * clips, 6 * width)
    half_bias = own_sums[:, : 3 * width // 2].reshape(2, 3, zs, 1, width // seq_size)
    bias_sums = jnp.sum(own_sums, axis=0)[2 * width :]
    qkv_bias_sums = jnp.where(
        parity == 0,
        jnp.concatenate([half_bias[0], half_bias[1]], axis=2),
        jnp.concatenate([half_bias[1], half_bias[0]], axis=2),
    ).reshape(3 * width)
    all_condition = late[:, :clips].reshape(devices * clips, width).astype(F32)
    codes = late[:, clips:start, :clips].astype(jnp.int32)
    all_levels = (codes[:, 0] * 32 + codes[:, 1]).reshape(devices * clips)
    all_active, silu_pull = jax.vjp(silu_act, all_condition)
    my_active = lax.dynamic_slice_in_dim(all_active, me * row, row, axis=1).astype(BF16)
    mod_wgrad = lax.dot_general(
        my_active, grad_modulation, (((0,), (0,)), ((), ())), preferred_element_type=F32
    )
    (grad_condition,) = silu_pull(
        lax.dot_general(
            grad_modulation, mod_weight, (((1,), (1,)), ((), ())), preferred_element_type=F32
        )
    )
    table_row = level_table.shape[0] // seq_size
    onehot = (
        all_levels[:, None] == (me * table_row + jnp.arange(table_row, dtype=jnp.int32))[None, :]
    ).astype(F32)
    table_grad = lax.dot_general(
        onehot,
        grad_condition,
        (((0,), (0,)), ((), ())),
        precision=HIGHEST_PRECISION,
        preferred_element_type=F32,
    )
    mod_sums = jnp.sum(grad_modulation.astype(F32), axis=0)

    def own_part(vector):
        size = vector.shape[0] // seq_size
        return lax.dynamic_slice_in_dim(vector, me * size, size, axis=0)

    mod_bgrad = own_part(mod_sums)
    qkv_bgrad = own_part(qkv_bias_sums)
    up_bgrad = own_part(bias_sums[:hidden])
    down_bgrad = own_part(bias_sums[hidden : hidden + width])
    proj_bgrad = own_part(bias_sums[hidden + width : hidden + 2 * width])
    if aligned:
        pieces = gather_pieces(piece, clip_size)
        if len(blocks) > 1:
            landed = z_out(blocks, seq_size)
            landed, mod_wgrad, table_grad = after(landed, mod_wgrad, table_grad)
            blocks = z_in(blocks, landed)
        piece = sum_z(blocks, seq_size).reshape(2, row, 3 * LANES)
        own_rows = lax.dynamic_index_in_dim(piece, parity, 0, keepdims=False)
        far_rows = swap(lax.dynamic_index_in_dim(piece, 1 - parity, 0, keepdims=False))
        far_rows, pieces = after(far_rows, pieces)
        pieces_qkv = gather_pieces(jnp.stack([own_rows, far_rows]), clip_size)
    else:
        pieces = gather_pieces(piece, clip_size)
        share = sum(
            lax.dot_general(left, right, (((0,), (0,)), ((), ())), preferred_element_type=F32)
            for left, right in zip(lefts, grad_rights)
        ).astype(BF16)
        share = share.reshape(width, 3, zs, 1, width // seq_size)
        blank = jnp.zeros_like(share)
        share = jnp.where(
            parity == 0,
            jnp.concatenate([share, blank], axis=3),
            jnp.concatenate([blank, share], axis=3),
        ).reshape(width, 3 * width)
        qkv_wgrad = lax.psum(
            lax.psum_scatter(share, "seq", scatter_dimension=0, tiled=True), "clip"
        ).astype(F32)

    proj_wgrad, down_wgrad, up_wgrad = place_call(
        meta,
        pieces,
        (
            (row, 1, False),
            (row, hidden // width, True),
            (row, hidden // width, False),
        ),
        [shaped((row, width), F32), shaped((hidden // seq_size, width), F32), shaped((row, hidden), F32)],
    )
    if aligned:
        pieces_qkv, proj_wgrad = after(pieces_qkv, proj_wgrad)
        qkv_wgrad = place_qkv_call(meta, pieces_qkv, shaped((row, 3 * width), F32))
    layer_out = jnp.stack(layer)[:, None]
    return (
        layer_out,
        tokens_grad,
        table_grad,
        mod_wgrad,
        mod_bgrad,
        qkv_wgrad,
        qkv_bgrad,
        proj_wgrad,
        proj_bgrad,
        up_wgrad,
        up_bgrad,
        down_wgrad,
        down_bgrad,
    )


def solution(mesh):
    placed = (
        P("clip", "seq", None, None),
        P("clip", "seq", None, None),
        P("clip"),
        P("clip", "seq"),
        P("clip", "seq"),
    ) + (P(),) * 11
    return jax.shard_map(
        on_device,
        mesh=mesh,
        in_specs=placed,
        out_specs=(
            P("clip", "seq", None, None),
            P("clip", "seq", None, None),
            P("seq", None),
            P("seq", None),
            P("seq"),
            P("seq", None),
            P("seq"),
            P("seq", None),
            P("seq"),
            P("seq", None),
            P("seq"),
            P("seq", None),
            P("seq"),
        ),
        check_vma=False,
    )
```
